32 devices in a mesh: dp: 8 (over y, x, core), mp: 4 (over z).
Axes of the slice: x: 2, y: 2, z: 4, core: 2. Of those that a mesh axis runs over, the one named last changes fastest.
Arguments:
- embedded: bfloat16 [8192, 1040], P('dp', 'mp'), may hold values from -6 to 6, as said below
- feature_ids: int32 [8192, 26], P('dp'), may hold values from 0 to 127
- day_ids: int32 [8192], P('dp'), may hold values from 0 to 23, as said below
- labels: int32 [8192], P('dp'), may hold values 0 or 1
- cross_weight: bfloat16 [3, 1040, 1040], P(None, 'mp'), may hold values from -0.1875 to 0.1875
- cross_bias: bfloat16 [3, 1040], P(None, 'mp'), may hold values from -3 to 3
- tower1: bfloat16 [1040, 1024], P(None, 'mp'), may hold values from -0.1875 to 0.1875
- tower1_bias: bfloat16 [1024], P('mp'), may hold values from -3 to 3
- tower2: bfloat16 [1024, 1024], P('mp'), may hold values from -0.1875 to 0.1875
- tower2_bias: bfloat16 [1024], P('mp'), may hold values from -3 to 3
- head_weight: bfloat16 [1024], P('mp'), may hold values from -0.1875 to 0.1875
Outputs:
- mean_loss: float32 [], replicated
- logits: float32 [8192], P('dp')
- embedded_grad: float32 [8192, 1040], P('dp', 'mp')
- cross_weight_grad: float32 [3, 1040, 1040], P(None, 'mp')
- cross_bias_grad: float32 [3, 1040], P(None, 'mp')
- tower1_grad: float32 [1040, 1024], P(None, 'mp')
- tower1_bias_grad: float32 [1024], P('mp')
- tower2_grad: float32 [1024, 1024], P('mp')
- tower2_bias_grad: float32 [1024], P('mp')
- head_grad: float32 [1024], P('mp')
- day_counts: int32 [24], replicated
- field_counts: int32 [26, 128], replicated
The draws below stay inside these ranges and needn't reach their ends.
Inputs may be any that keep to these rules, and one draw needn't show every extreme that they name: `day_ids`: every day occurs in at least one example. `embedded`: columns 1027 to 1039 are zero.
All inputs are finite; a program needn't handle non-finite values. No bound on the sum of `labels` on one device may be relied on, other than what follows from the above.
Results may differ from the reference program's by a relative error of at most 0.0096.
Values may be sent and summed in bfloat16 or wider, within the bound.
No kernel may reach another device: no remote copies, remote signals or barrier semaphores. Data moves between devices by JAX's collectives and lax.ppermute only.
A program may use at most 64 MiB of HBM per device.

```python
import math
import jax
import jax.numpy as jnp
import numpy as np
from jax import lax

FIELDS = 26
D = 1040
H = 1024
LAYERS = 3
DAYS = 24
BUCKETS = 128
TOK_DEV = 1024
FEATURES = 1027
EXAMPLES = 8192
N_DP = 8


def draw_embedded(key, part):
    key = jax.random.fold_in(key, 11)
    samples = jnp.clip(jax.random.normal(key, (EXAMPLES, D), jnp.float32), -6.0, 6.0)
    keep_mask = (jnp.arange(D) < FEATURES).astype(jnp.float32)
    return (samples * keep_mask[None, :]).astype(jnp.bfloat16)


def draw_day_ids(key, part):
    key = jax.random.fold_in(key, 23)
    key_early, key_late, key_spots = jax.random.split(key, 3)
    early_day = jax.random.randint(key_early, (EXAMPLES,), 0, DAYS)
    late_day = jax.random.randint(key_late, (EXAMPLES,), 0, DAYS)
    day_values = jnp.minimum(early_day, late_day).astype(jnp.int32)
    forced_spots = jax.random.permutation(key_spots, EXAMPLES)[:DAYS]
    return day_values.at[forced_spots].set(jnp.arange(DAYS, dtype=jnp.int32)).astype(jnp.int32)


def set_ends(drawn, own_key, least, largest):
    index_at = [jax.random.randint(jax.random.fold_in(own_key, axis), (), 0, length) for axis, length in enumerate(drawn.shape)]
    longest = drawn.shape.index(max(drawn.shape))
    next_to = index_at[:longest] + [(index_at[longest] + 1) % drawn.shape[longest]] + index_at[longest + 1:]
    return drawn.at[tuple(index_at)].set(least).at[tuple(next_to)].set(largest)


def level_of(stream_key, dims, cuts, least, top_value):
    gain = 1.0
    for axis_at, blocks in cuts:
        steps = jax.random.uniform(jax.random.fold_in(jax.random.fold_in(stream_key, 6), axis_at), (blocks,), jnp.float32, least / len(cuts), top_value / len(cuts))
        gain = gain * jnp.repeat(jnp.exp(steps), dims[axis_at] // blocks).reshape((-1,) + (1,) * (len(dims) - 1 - axis_at))
    return gain


def rank_table(amount, slope):
    weights = [(1 << 20) // math.isqrt(standing ** slope) + 1 for standing in range(1, amount + 1)]
    spread = 1 + sum(weights) // (1 << 30)
    return np.cumsum(np.array([max(1, weight // spread) for weight in weights]))


def ranked_ids(stream_key, shape, amount, skew):
    grid = rank_table(amount, skew)
    ticket = jax.random.randint(jax.random.fold_in(stream_key, 1), shape, 0, int(grid[amount - 1]))
    grade = jnp.searchsorted(jnp.asarray(grid, jnp.int32), ticket, side="right")
    return jax.random.permutation(jax.random.fold_in(stream_key, 2), amount)[grade].astype(jnp.int32)


def gaussian(rng, extent, scale, bound, cuts=(), held_as=jnp.bfloat16):
    factor_of = level_of(rng, extent, cuts, -0.22, 0.18) if cuts else 1.0
    drawn = jax.random.normal(rng, extent, jnp.float32) * scale * factor_of
    return jnp.minimum(jnp.maximum(drawn, -bound), bound).astype(held_as)


def setup_inputs(seed: int = 0) -> dict:
    seeds = jax.random.split(jax.random.key(seed), 12)
    return {
        "embedded": draw_embedded(jax.random.fold_in(seeds[11], 71), 0),
        "feature_ids": set_ends(ranked_ids(seeds[1], (EXAMPLES, FIELDS), BUCKETS, 2), jax.random.fold_in(seeds[1], 3), 0, BUCKETS - 1).astype(jnp.int32),
        "day_ids": draw_day_ids(jax.random.fold_in(seeds[11], 71), 0),
        "labels": set_ends((jax.random.randint(seeds[3], (EXAMPLES,), 0, 4) < 1).astype(jnp.int32), jax.random.fold_in(seeds[3], 1), 0, 1),
        "cross_weight": gaussian(seeds[4], (LAYERS, D, D), D ** -0.5, 0.1875, ((1, 4),)),
        "cross_bias": gaussian(seeds[5], (LAYERS, D), 0.5, 3.0, ((1, 4),)),
        "tower1": gaussian(seeds[6], (D, H), D ** -0.5, 0.1875, ((1, 4),)),
        "tower1_bias": gaussian(seeds[7], (H,), 0.5, 3.0, ((0, 4),)),
        "tower2": gaussian(seeds[8], (H, H), H ** -0.5, 0.1875, ((0, 4),)),
        "tower2_bias": gaussian(seeds[9], (H,), 0.5, 3.0, ((0, 4),)),
        "head_weight": gaussian(seeds[10], (H,), H ** -0.5, 0.1875, ((0, 4),)),
    }


@jax.custom_vjp
def low(v):
    return lax.optimization_barrier(v.astype(jnp.bfloat16)).astype(jnp.float32)

@jax.custom_vjp
def low_back(v):
    return v

def low_keep(v):
    return (low(v), None)

def low_pass(kept, grad):
    return (grad,)

def back_keep(v):
    return (v, None)

def back_low(kept, grad):
    return (low(grad),)
low.defvjp(low_keep, low_pass)
low_back.defvjp(back_keep, back_low)

def gelu_exact(values):
    return jax.nn.gelu(values, approximate=False)

def forward(params, inputs):
    cross_w, cross_b, first_w, first_b, second_w, second_b, head_w = params
    state = inputs
    for layer_index in range(LAYERS):
        z_value = jnp.dot(low(state), cross_w[layer_index].T, precision=lax.Precision.HIGHEST) + cross_b[layer_index]
        z_value = low_back(z_value)
        state = inputs * z_value + state
    pre_one = low_back(jnp.dot(low(state), first_w, precision=lax.Precision.HIGHEST) + first_b)
    act_low = low(gelu_exact(pre_one))
    pre_two = low_back(jnp.dot(act_low, second_w, precision=lax.Precision.HIGHEST) + second_b)
    return jnp.dot(gelu_exact(pre_two), head_w, precision=lax.Precision.HIGHEST)

def reference(embedded, feature_ids, day_ids, labels, cross_weight, cross_bias, tower1, tower1_bias, tower2, tower2_bias, head_weight):
    params = tuple((p.astype(jnp.float32) for p in (cross_weight, cross_bias, tower1, tower1_bias, tower2, tower2_bias, head_weight)))
    day_counts = jax.ops.segment_sum(jnp.ones_like(day_ids), day_ids, num_segments=DAYS).astype(jnp.int32)
    field_counts = jax.vmap(lambda column: jax.ops.segment_sum(jnp.ones_like(column), column, num_segments=BUCKETS))(feature_ids.T).astype(jnp.int32)
    day_weight = 1.0 / (DAYS * day_counts.astype(jnp.float32))
    row_weight = day_weight[day_ids]
    inputs = embedded.astype(jnp.float32).reshape(N_DP, TOK_DEV, D)
    label_float = labels.astype(jnp.float32).reshape(N_DP, TOK_DEV)
    weight_blocks = row_weight.reshape(N_DP, TOK_DEV)

    def step(running, block_data):
        block_inputs, block_labels, block_weight = block_data

        def objective(param_set, xin):
            block_logits = forward(param_set, xin)
            bce_terms = jax.nn.softplus(block_logits) - block_labels * block_logits
            return (EXAMPLES * jnp.sum(block_weight * bce_terms), (block_logits, bce_terms))
        objective_value, pullback, extras = jax.vjp(objective, params, block_inputs, has_aux=True)
        param_grads, input_grads = pullback(jnp.ones_like(objective_value))
        running = jax.tree.map(jnp.add, running, param_grads)
        return (running, (input_grads, extras[0], extras[1]))
    start = jax.tree.map(jnp.zeros_like, params)
    grads, outputs = lax.scan(step, start, (inputs, label_float, weight_blocks))
    input_grads, logits, bce_terms = outputs
    logits = logits.reshape(EXAMPLES)
    loss_sums = jax.ops.segment_sum(bce_terms.reshape(EXAMPLES), day_ids, num_segments=DAYS)
    mean_loss = jnp.sum(loss_sums / day_counts.astype(jnp.float32)) / DAYS
    return (mean_loss, logits, input_grads.reshape(EXAMPLES, D), grads[0], grads[1], grads[2], grads[3], grads[4], grads[5], grads[6], day_counts, field_counts)
```

```python
import functools

import jax
import jax.numpy as jnp
from jax import lax
from jax.experimental import pallas as pl
from jax.experimental.pallas import tpu as pltpu
from jax.sharding import PartitionSpec as P

DAYS = 24
BUCKETS = 128
BF16 = jnp.bfloat16
F32 = jnp.float32
MAIN = 256
SHARE = 32
VMEM = pl.BlockSpec(memory_space=pltpu.VMEM)
SMEM = pl.BlockSpec(memory_space=pltpu.SMEM)
NT = (((1,), (1,)), ((), ()))
TN = (((0,), (0,)), ((), ()))
NN = (((1,), (0,)), ((), ()))


def gelu_parts(values):
    cdf_part = 0.5 * (1.0 + lax.erf(values * 0.7071067811865476))
    slope = cdf_part + values * jnp.exp(-0.5 * values * values) * 0.3989422804014327
    return (values * cdf_part, slope)


def dot(lhs, rhs, dims, precision=None):
    return lax.dot_general(lhs, rhs, dims, preferred_element_type=F32, precision=precision)


def call(kernel, outs, scratch, *args, flops=0, nbytes=0):
    return pl.pallas_call(
        kernel,
        out_shape=outs,
        in_specs=[SMEM] + [VMEM] * (len(args) - 1),
        out_specs=jax.tree.map(lambda _: VMEM, outs),
        scratch_shapes=scratch,
        compiler_params=pltpu.CompilerParams(vmem_limit_bytes=60 * 1024 * 1024),
        cost_estimate=pl.CostEstimate(flops=flops, bytes_accessed=nbytes, transcendentals=0),
    )(*args)


def places(idx):
    core, plane = idx[1], idx[2]
    first, second = core + 1, 2 - core
    mine = [plane, plane ^ first, plane ^ second, plane ^ 3]
    theirs = [plane, plane ^ second, plane ^ first, plane ^ 3]
    return [core * 128 + SHARE * q for q in mine] + [(1 - core) * 128 + SHARE * q for q in theirs]


def block_of(idx, turn, blocks):
    return lax.rem(idx[0] - turn + blocks, blocks)


def rows_at(offset, size, unit=16):
    return pl.ds(pl.multiple_of(offset, unit), size)


def cross_forward(idx, *refs, blocks, layers, width, pad, depth):
    pieces, refs = refs[:blocks], refs[blocks:]
    own, refs = refs[0], refs[1:]
    turned, refs = refs[: blocks - 1], refs[blocks - 1 :]
    slices, refs = refs[:8], refs[8:]
    w_out, z_out, x_out, x0_out, start, state, nat, tail, tails = refs
    left = width - MAIN
    offsets = places(idx)
    tail[...] = jnp.zeros_like(tail)
    start[...] = jnp.zeros_like(start)
    for turn in range(blocks):
        start[block_of(idx, turn, blocks), 0:width, :] = pieces[turn][...].astype(F32)
    state[...] = start[...]
    for block in range(blocks):
        x0_out[pad * block : pad * (block + 1), :] = start[block].astype(BF16)
    for layer in range(layers):
        base = idx[0] * pad
        w_out[layer, rows_at(base, MAIN), :] = own[layer, 0:MAIN, :]
        tail[0:left, :] = own[layer, MAIN:width, :].astype(F32)
        w_out[layer, rows_at(base + MAIN, 16), :] = tail[...].astype(BF16)
    for turn in range(1, blocks):
        base = block_of(idx, turn, blocks) * pad
        tails[...] = turned[turn - 1][layers * SHARE : layers * SHARE + 16, :].astype(F32)
        for layer in range(layers):
            tail[0:left, :] = tails[left * layer : left * (layer + 1), :]
            w_out[layer, rows_at(base + MAIN, 16), :] = tail[...].astype(BF16)
            for offset, piece in zip(offsets, slices):
                w_out[layer, rows_at(base + offset, SHARE), :] = piece[
                    turn - 1, SHARE * layer : SHARE * (layer + 1), :
                ]
    full = nat.shape[0]
    ones = lax.broadcasted_iota(jnp.int32, (full - depth, nat.shape[1]), 0) == 0
    nat[depth:full, :] = ones.astype(F32)
    for layer in range(layers + 1):
        for block in range(blocks):
            nat[width * block : width * (block + 1), :] = state[block, 0:width, :]
        x_out[layer] = nat[...].astype(BF16)
        if layer == layers:
            break

        def step(block, carry, layer=layer):
            rows = rows_at(block * pad, pad)
            z_value = dot(w_out[layer, rows, :], x_out[layer], NN)
            z_out[layer, rows, :] = z_value
            state[block] = start[block] * z_value + state[block]
            return carry

        lax.fori_loop(0, blocks, step, 0)


def tower_both(idx, *refs, blocks, depth, days):
    x3, own1, own2 = refs[:3]
    slices, refs = refs[3:11], refs[11:]
    labels, day_ids, share = refs[:3]
    g1, da2, da1, dx3, logits_out, row1, row2, row_head, row_loss = refs[3:12]
    t1, t2, slope1, act2, headed, total = refs[12:]
    hidden = t1.shape[0]
    size = hidden // blocks
    offsets = places(idx)
    base = idx[0] * size
    t1[rows_at(base, size), :] = own1[...]
    t2[rows_at(base, size), :] = own2[...]
    for turn in range(1, blocks):
        base = block_of(idx, turn, blocks) * size
        for offset, piece in zip(offsets, slices):
            t1[rows_at(base + offset, SHARE), :] = piece[turn - 1, 0:SHARE, :]
            t2[rows_at(base + offset, SHARE), :] = piece[turn - 1, SHARE : 2 * SHARE, 0:hidden]
    low = depth // 128 * 128

    def first(block, carry):
        rows = rows_at(block * size, size)
        act, slope = gelu_parts(dot(t1[rows, :], x3[...], NN))
        g1[rows, :] = act.astype(BF16)
        slope1[rows, :] = slope
        return carry

    lax.fori_loop(0, blocks, first, 0)
    total[...] = jnp.zeros_like(total)

    def second(block, carry):
        rows = rows_at(block * size, size, 128)
        columns = t1[rows, low:].astype(F32)
        head = columns[:, depth - low + 1 : depth - low + 2]
        bias = columns[:, depth - low + 2 : depth - low + 3]
        act, slope = gelu_parts(dot(t2[:, rows], g1[...], TN) + bias)
        act2[rows, :] = act
        headed[rows, :] = head * slope
        total[...] += jnp.sum(act * head, axis=0, keepdims=True)
        return carry

    lax.fori_loop(0, blocks, second, 0)
    logits = total[...]
    logits_out[...] = logits
    lab = labels[...].astype(F32)
    table = (
        lax.broadcasted_iota(jnp.int32, share.shape, 0) == day_ids[...]
    ).astype(F32)
    weight = jnp.sum(table * share[...], axis=0, keepdims=True)
    decay = jnp.exp(-jnp.abs(logits))
    loss = jnp.maximum(logits, 0.0) + jnp.log1p(decay) - lab * logits
    sigmoid = jnp.where(logits >= 0.0, 1.0, decay) / (1.0 + decay)
    dl = weight * (sigmoid - lab)
    exact = lax.Precision.HIGHEST
    spread = lambda row: jnp.broadcast_to(row, (8, row.shape[1]))
    row_loss[...] = dot(spread(loss), table, NT, exact)
    row_head[...] = dot(spread(dl), act2[...], NT, exact)
    da2[...] = (dl * headed[...]).astype(BF16)
    ones = jnp.ones((8, dl.shape[1]), BF16)
    row2[...] = dot(ones, da2[...], NT)

    def third(block, carry):
        rows = rows_at(block * size, size)
        da1[rows, :] = (dot(t2[rows, :], da2[...], NN) * slope1[rows, :]).astype(BF16)
        return carry

    lax.fori_loop(0, blocks, third, 0)
    row1[...] = dot(ones, da1[...], NT)

    def fourth(tile, carry):
        rows = rows_at(tile * 384, 384, 128)
        dx3[rows, :] = dot(t1[:, rows], da1[...], TN)
        return carry

    lax.fori_loop(0, t1.shape[1] // 384, fourth, 0)


def cross_backward(idx, dx3, x0, z_all, w_all, x_all, logits, dz_out, eg_out, rows_out, left_out, flow, padded, total, *, blocks, layers, width, pad, depth):
    flow[...] = dx3[...]
    total[...] = jnp.zeros_like(total)
    padded[...] = jnp.zeros_like(padded)
    ones = jnp.ones((8, x0.shape[1]), BF16)
    left = width - MAIN
    for layer in reversed(range(layers)):
        for block in range(blocks):
            padded[block, 0:width, :] = flow[width * block : width * (block + 1), :]
            rows = slice(pad * block, pad * (block + 1))
            dx = padded[block]
            dz_out[layer, rows, :] = (dx * x0[rows, :].astype(F32)).astype(BF16)
            total[block] += dx * z_all[layer, rows, :]
            left_out[layer, 16 * block : 16 * (block + 1), :] = dot(
                dz_out[layer, pad * block + MAIN : pad * (block + 1), :], x_all[layer], NT
            )
        rows_out[layer, :, :] = dot(ones, dz_out[layer], NT)

        def step(tile, carry, layer=layer):
            rows = rows_at(tile * 384, 384, 128)
            flow[rows, :] += dot(w_all[layer, :, rows], dz_out[layer], TN)
            return carry

        lax.fori_loop(0, flow.shape[0] // 384, step, 0)
    line = logits[...]
    high = line.astype(BF16).astype(F32)
    middle = (line - high).astype(BF16).astype(F32)
    low = line - high - middle
    for block in range(blocks):
        padded[block, 0:width, :] = flow[width * block : width * (block + 1), :]
        total[block] += padded[block]
        total[block, width : width + 1, :] = high
        total[block, width + 1 : width + 2, :] = middle
        total[block, width + 2 : width + 3, :] = low
        eg_out[pad * block : pad * (block + 1), :] = total[block].astype(BF16)


def relative(idx, part):
    turned = part ^ idx[2]
    one, two = turned & 1, (turned >> 1) & 1
    return jnp.where(idx[1] == 0, one * 2 + two, two * 2 + one)


def tower_grads(idx, x_own, x_far, g1_own, g1_far, da2_own, da2_far, da1_own, da1_far, out, *, blocks, depth):
    hidden = g1_own.shape[0]
    size = hidden // blocks

    def step(block, carry):
        rows = rows_at(block * size + idx[1] * 128, 128)
        slot = lax.rem(block - idx[0] + blocks, blocks)
        grad1 = dot(da1_own[rows, :], x_own[...], NT) + dot(da1_far[block], x_far[...], NT)
        grad2 = dot(g1_own[rows, :], da2_own[...], NT) + dot(g1_far[block], da2_far[...], NT)
        for part in range(4):
            at = relative(idx, part)
            lines = slice(SHARE * part, SHARE * (part + 1))
            out[at, slot, 0:SHARE, :] = grad1[lines, :].astype(BF16)
            out[at, slot, SHARE : 2 * SHARE, 0:hidden] = grad2[lines, :].astype(BF16)
            out[at, slot, SHARE : 2 * SHARE, hidden:] = jnp.zeros((SHARE, out.shape[3] - hidden), BF16)
        return carry

    lax.fori_loop(0, blocks, step, 0)


def cross_grads(idx, x_own, x_far, dz_own, dz_far, out, *, blocks, layers, pad):
    for layer in range(layers):

        def step(block, carry, layer=layer):
            rows = rows_at(block * pad + idx[1] * 128, 128)
            slot = lax.rem(block - idx[0] + blocks, blocks)
            grad = dot(dz_own[layer, rows, :], x_own[layer], NT) + dot(dz_far[layer, block], x_far[layer], NT)
            for part in range(4):
                out[relative(idx, part), slot, SHARE * layer : SHARE * (layer + 1), :] = grad[
                    SHARE * part : SHARE * (part + 1), :
                ].astype(BF16)
            return carry

        lax.fori_loop(0, blocks, step, 0)


def finish_tower(idx, *refs):
    slices, (out1, out2, lines) = refs[:8], refs[8:]
    hidden = out2.shape[1]
    for offset, piece in zip(places(idx), slices):
        lines[rows_at(offset, SHARE), :] = piece[0:SHARE, :].astype(F32)
        out2[rows_at(offset, SHARE), :] = piece[SHARE : 2 * SHARE, 0:hidden].astype(F32)
    out1[...] = lines[...].T[0 : out1.shape[0], :]


def finish_cross(idx, *refs):
    slices, (rest, out) = refs[:8], refs[8:]
    left = out.shape[1] - MAIN
    depth = out.shape[2]
    for layer in range(out.shape[0]):
        for offset, piece in zip(places(idx), slices):
            out[layer, rows_at(offset, SHARE), :] = piece[SHARE * layer : SHARE * (layer + 1), 0:depth].astype(F32)
        out[layer, MAIN:, :] = rest[left * layer : left * (layer + 1), 0:depth]


def finish_input(idx, *refs):
    pieces, (out, logits) = refs[:-2], refs[-2:]
    width = out.shape[0]
    size = pieces[0].shape[1]
    for turn, piece in enumerate(pieces):
        lanes = pl.ds(pl.multiple_of(block_of(idx, turn, len(pieces)) * size, 128), size)
        values = piece[...].astype(F32)
        out[:, lanes] = values[0:width, :]
        logits[:, lanes] = values[width : width + 1, :] + values[width + 1 : width + 2, :] + values[width + 2 : width + 3, :]


def per_device(
    embedded,
    feature_ids,
    day_ids,
    labels,
    cross_weight,
    cross_bias,
    tower1,
    tower1_bias,
    tower2,
    tower2_bias,
    head_weight,
):
    blocks = lax.axis_size("mp")
    groups = lax.axis_size("dp")
    tokens, width = embedded.shape
    layers, _, depth = cross_weight.shape
    size, hidden = tower2.shape
    pad = -(-width // 16) * 16
    full = -(-(depth + 3) // 128) * 128
    left = width - MAIN
    part = tokens // blocks
    examples = tokens * groups
    shape = jax.ShapeDtypeStruct

    me = lax.axis_index("mp")
    group = lax.axis_index("dp")
    core, plane = group & 1, (group >> 1) & 3
    idx = jnp.stack([me, core, plane]).astype(jnp.int32)
    own_row = core * 128 + plane * SHARE
    swap = lambda bits: [(i, i ^ bits(i)) for i in range(groups)]
    first = swap(lambda i: 4 if i & 1 else 2)
    second = swap(lambda i: 2 if i & 1 else 4)
    pair = swap(lambda i: 1)
    others = [swap(lambda i, b=b: 1 << b) for b in range(3, groups.bit_length() - 1)]
    turn_by = lambda r: [(i, (i + r) % blocks) for i in range(blocks)]
    hop = lambda value, perm: lax.ppermute(value, "dp", perm)
    turns = lambda values: [
        lax.ppermute(value, "mp", turn_by(r + 1)) for r, value in enumerate(values)
    ]
    ahead = [lax.rem(me + r, blocks) for r in range(blocks)]

    day_hits = day_ids[None, :] == jnp.arange(DAYS, dtype=jnp.int32)[:, None]
    field_hits = feature_ids.T[:, None, :] == jnp.arange(BUCKETS, dtype=jnp.int32)[None, :, None]
    day_line = jnp.pad(jnp.sum(day_hits.astype(jnp.int32), axis=1), (0, BUCKETS - DAYS))
    counts = jnp.concatenate([jnp.sum(field_hits.astype(jnp.int32), axis=2), day_line[None, :]])

    turned_inputs = embedded.T
    chunks = [lax.dynamic_slice(turned_inputs, (0, ahead[r] * part), (width, part)) for r in range(blocks)]
    pieces = [chunks[0]] + turns(chunks[1:])
    fill = lambda *s: jnp.zeros(s, BF16)
    cross_own = jnp.concatenate(
        [cross_weight, cross_bias[:, :, None], fill(layers, width, full - depth - 1)], axis=2
    )
    tower_own = jnp.concatenate(
        [tower1.T, tower1_bias[:, None], head_weight[:, None], tower2_bias[:, None], fill(size, full - depth - 3)],
        axis=1,
    )
    cross_send = jnp.concatenate(
        [
            lax.dynamic_slice(cross_own, (0, own_row, 0), (layers, SHARE, full)).reshape(layers * SHARE, full),
            cross_own[:, MAIN:, :].reshape(layers * left, full),
            fill(16 - layers * left, full),
        ]
    )
    tower_send = jnp.concatenate(
        [
            lax.dynamic_slice(tower_own, (own_row, 0), (SHARE, full)),
            jnp.pad(lax.dynamic_slice(tower2, (own_row, 0), (SHARE, hidden)), ((0, 0), (0, full - hidden))),
        ]
    )

    def hand_round(mine):
        one, two = hop(mine, first), hop(mine, second)
        held = [mine, one, two, hop(one, second)]
        return held + [hop(value, pair) for value in held]

    cross_turned = turns([cross_send] * (blocks - 1))
    cross_slices = hand_round(jnp.stack([value[: layers * SHARE] for value in cross_turned]))
    tower_turned = turns([tower_send] * (blocks - 1))
    tower_slices = hand_round(jnp.stack(tower_turned))

    for perm in [pair, first, second] + others:
        counts = counts + hop(counts, perm)
    field_counts, day_counts = counts[:-1], counts[-1, :DAYS]
    day_totals = day_counts.astype(F32)
    share_day = jnp.pad(examples / (DAYS * day_totals), (0, 32 - DAYS))
    share_day = jnp.broadcast_to(share_day[:, None], (32, part))

    cut = lambda values: lax.dynamic_slice(values, (me * part,), (part,))[None, :]
    flat = blocks * pad
    cross_w, z_all, x_all, x0 = call(
        functools.partial(cross_forward, blocks=blocks, layers=layers, width=width, pad=pad, depth=depth),
        (
            shape((layers, flat, full), BF16),
            shape((layers, flat, part), F32),
            shape((layers + 1, full, part), BF16),
            shape((flat, part), BF16),
        ),
        [
            pltpu.VMEM((blocks, pad, part), F32),
            pltpu.VMEM((blocks, pad, part), F32),
            pltpu.VMEM((full, part), F32),
            pltpu.VMEM((16, full), F32),
            pltpu.VMEM((16, full), F32),
        ],
        idx,
        *pieces,
        cross_own,
        *cross_turned,
        *cross_slices,
        flops=2 * layers * flat * full * part,
        nbytes=20 << 20,
    )
    x_far = hop(x_all, pair)
    g1, da2, da1, dx3, logits, row1, row2, row_head, row_loss = call(
        functools.partial(tower_both, blocks=blocks, depth=depth, days=DAYS),
        (
            shape((hidden, part), BF16),
            shape((hidden, part), BF16),
            shape((hidden, part), BF16),
            shape((full, part), F32),
            shape((1, part), F32),
            shape((8, hidden), F32),
            shape((8, hidden), F32),
            shape((8, hidden), F32),
            shape((8, 32), F32),
        ),
        [
            pltpu.VMEM((hidden, full), BF16),
            pltpu.VMEM((hidden, hidden), BF16),
            pltpu.VMEM((hidden, part), F32),
            pltpu.VMEM((hidden, part), F32),
            pltpu.VMEM((hidden, part), F32),
            pltpu.VMEM((1, part), F32),
        ],
        idx,
        x_all[layers],
        tower_own,
        tower2,
        *tower_slices,
        cut(labels),
        cut(day_ids),
        share_day,
        flops=4 * 2 * hidden * full * part,
        nbytes=10 << 20,
    )
    far_half = lambda values, rows: lax.dynamic_slice_in_dim(
        values.reshape(values.shape[:-2] + (blocks, rows, part)), (1 - core) * 128, 128, axis=values.ndim - 1
    )
    g1_far = hop(far_half(g1, size), pair)
    da2_far = hop(da2, pair)
    da1_far = hop(far_half(da1, size), pair)
    tower_parts = call(
        functools.partial(tower_grads, blocks=blocks, depth=depth),
        shape((4, blocks, 2 * SHARE, full), BF16),
        [],
        idx,
        x_all[layers],
        x_far[layers],
        g1,
        g1_far,
        da2,
        da2_far,
        da1,
        da1_far,
        flops=4 * hidden * full * part,
        nbytes=10 << 20,
    )
    dz, input_grad, row_cross, left_cross = call(
        functools.partial(cross_backward, blocks=blocks, layers=layers, width=width, pad=pad, depth=depth),
        (
            shape((layers, flat, part), BF16),
            shape((flat, part), BF16),
            shape((layers, 8, flat), F32),
            shape((layers, 16 * blocks, full), F32),
        ),
        [
            pltpu.VMEM((full, part), F32),
            pltpu.VMEM((blocks, pad, part), F32),
            pltpu.VMEM((blocks, pad, part), F32),
        ],
        idx,
        dx3,
        x0,
        z_all,
        cross_w,
        x_all,
        logits,
        flops=2 * layers * flat * full * part,
        nbytes=20 << 20,
    )
    dz_far = hop(far_half(dz, pad), pair)
    cross_parts = call(
        functools.partial(cross_grads, blocks=blocks, layers=layers, pad=pad),
        shape((4, blocks, layers * SHARE, full), BF16),
        [],
        idx,
        x_all,
        x_far,
        dz,
        dz_far,
        flops=2 * layers * flat * full * part,
        nbytes=20 << 20,
    )

    def gather_sum(parts):
        held = parts[:2].astype(F32) + hop(parts[2:], first).astype(F32)
        held = held[0] + hop(held[1].astype(BF16), second).astype(F32)
        arrived = turns([held[r].astype(BF16) for r in range(1, blocks)])
        held = held[0] + sum(value.astype(F32) for value in arrived)
        for perm in others:
            held = held + hop(held, perm)
        return hand_round(held.astype(BF16))

    tower_sums = gather_sum(tower_parts)
    cross_sums = gather_sum(cross_parts)

    blocks_of = [lax.dynamic_slice(input_grad, (ahead[r] * pad, 0), (pad, part)) for r in range(blocks)]
    grad_pieces = [blocks_of[0]] + turns(blocks_of[1:])
    input_out, logits_all = call(
        finish_input,
        (shape((width, tokens), F32), shape((1, tokens), F32)),
        [],
        idx,
        *grad_pieces,
        nbytes=2 << 20,
    )

    lines = lambda values: jnp.pad(values, ((0, 0), (0, full - values.shape[1])))
    common = jnp.concatenate(
        [lines(row_cross[:, 0, :]), lines(row1[:1]), lines(row2[:1]), lines(row_head[:1]), lines(row_loss[:1])]
    )
    rest = left_cross.reshape(layers, blocks, 16, full)[:, :, :left, :]
    rest = rest.transpose(1, 0, 2, 3).reshape(blocks, layers * left, full)
    small = jnp.concatenate([rest, jnp.broadcast_to(common[None], (blocks,) + common.shape)], axis=1)
    small_turned = [lax.dynamic_index_in_dim(small, ahead[r], 0, keepdims=False) for r in range(blocks)]
    small_turned = [small_turned[0]] + turns(small_turned[1:])
    in_order = jnp.stack(small_turned[::-1] * 2)
    in_order = lax.dynamic_slice_in_dim(in_order, blocks - 1 - me, blocks, axis=0)
    small = in_order[0]
    for value in range(1, blocks):
        small = small + in_order[value]
    for perm in [pair, first, second] + others:
        small = small + hop(small, perm)

    tower1_grad, tower2_grad = call(
        finish_tower,
        (shape((depth, size), F32), shape((size, hidden), F32)),
        [pltpu.VMEM((size, full), F32)],
        idx,
        *tower_sums,
        nbytes=4 << 20,
    )
    cross_grad = call(
        finish_cross,
        shape((layers, width, depth), F32),
        [],
        idx,
        *cross_sums,
        small,
        nbytes=4 << 20,
    )
    count = layers * left
    cross_bias_grad = lax.dynamic_slice(small, (count, me * pad), (layers, width))
    line = lambda at: lax.dynamic_slice(small, (at, me * size), (1, size))[0]
    loss_sums = small[count + layers + 3, :DAYS]
    total_loss = jnp.sum(loss_sums / day_totals) / DAYS
    return (
        total_loss,
        logits_all[0],
        input_out.T,
        cross_grad,
        cross_bias_grad,
        tower1_grad,
        line(count + layers),
        tower2_grad,
        line(count + layers + 1),
        line(count + layers + 2),
        day_counts,
        field_counts,
    )


def solution(mesh):
    in_specs = (
        P("dp", "mp"),
        P("dp", None),
        P("dp"),
        P("dp"),
        P(None, "mp", None),
        P(None, "mp"),
        P(None, "mp"),
        P("mp"),
        P("mp", None),
        P("mp"),
        P("mp"),
    )
    out_specs = (
        P(),
        P("dp"),
        P("dp", "mp"),
        P(None, "mp", None),
        P(None, "mp"),
        P(None, "mp"),
        P("mp"),
        P("mp", None),
        P("mp"),
        P("mp"),
        P(),
        P(),
    )
    return jax.shard_map(
        per_device, mesh=mesh, in_specs=in_specs, out_specs=out_specs, check_vma=False
    )
```

```python
import functools

import jax
import jax.numpy as jnp
from jax import lax
from jax.experimental import pallas as pl
from jax.experimental.pallas import tpu as pltpu
from jax.sharding import PartitionSpec as P

DAYS = 24
BUCKETS = 128
BF16 = jnp.bfloat16
F32 = jnp.float32
MAIN = 256
SHARE = 32
HALF = MAIN // 2
LANES = 128
REST = 32
COUNT = 32
VMEM = pl.BlockSpec(memory_space=pltpu.VMEM)
SMEM = pl.BlockSpec(memory_space=pltpu.SMEM)
HBM = pl.BlockSpec(memory_space=pl.ANY)
NT = (((1,), (1,)), ((), ()))
TN = (((0,), (0,)), ((), ()))
NN = (((1,), (0,)), ((), ()))


def gelu_parts(values):
    cdf_part = 0.5 * (1.0 + lax.erf(values * 0.7071067811865476))
    slope = cdf_part + values * jnp.exp(-0.5 * values * values) * 0.3989422804014327
    return (values * cdf_part, slope)


def dot(lhs, rhs, dims, precision=None):
    return lax.dot_general(lhs, rhs, dims, preferred_element_type=F32, precision=precision)


def call(kernel, outs, scratch, args, mib, spec=VMEM, copies=0, out_spec=None, aliases={}, flops=0, nbytes=0):
    arrays = [a[0] if isinstance(a, tuple) else a for a in args[1:]]
    specs = [a[1] if isinstance(a, tuple) else spec for a in args[1:]]
    if copies:
        scratch = scratch + [pltpu.SemaphoreType.DMA((copies,))]
    return pl.pallas_call(
        kernel,
        out_shape=outs,
        in_specs=[SMEM] + specs,
        out_specs=out_spec or jax.tree.map(lambda _: spec, outs),
        scratch_shapes=scratch,
        input_output_aliases=aliases,
        compiler_params=pltpu.CompilerParams(vmem_limit_bytes=mib << 20),
        cost_estimate=pl.CostEstimate(flops=flops, bytes_accessed=nbytes, transcendentals=0),
    )(args[0], *arrays)


class Copies:
    def __init__(self, sems):
        self.sems, self.count = sems, 0

    def start(self, source, target):
        copy = pltpu.make_async_copy(source, target, self.sems.at[self.count])
        self.count += 1
        copy.start()
        return copy


def wait(*copies):
    for copy in copies:
        copy.wait()


def after(value, *others):
    return lax.optimization_barrier((value,) + others)[0]


def places(idx):
    core, plane = idx[1], idx[2]
    first, second = core + 1, 2 - core
    mine = [plane, plane ^ first, plane ^ second, plane ^ 3]
    theirs = [plane, plane ^ second, plane ^ first, plane ^ 3]
    return [core * HALF + SHARE * q for q in mine] + [(1 - core) * HALF + SHARE * q for q in theirs]


def relative(idx):
    core, plane = idx[1], idx[2]
    first, second = core + 1, 2 - core
    return [plane, plane ^ second, plane ^ first, plane ^ 3]


def block_of(idx, turn, blocks):
    return lax.rem(idx[0] - turn + blocks, blocks)


def block_ahead(idx, turn, blocks):
    return lax.rem(idx[0] + turn, blocks)


def rows_at(offset, size, unit=16):
    return pl.ds(pl.multiple_of(offset, unit), size)


def split3(line):
    high = line.astype(BF16).astype(F32)
    middle = (line - high).astype(BF16).astype(F32)
    return high, middle, line - high - middle


def lane_of(shape):
    return lax.broadcasted_iota(jnp.int32, shape, 1)


def pack_first(idx, weight, out, sems):
    copies = Copies(sems)
    wait(copies.start(weight.at[0, rows_at(idx[1] * HALF + idx[2] * SHARE, SHARE), :], out))


def pack_cross(idx, weight, bias, out, lines):
    layers, width, depth = weight.shape
    left = width - MAIN
    own_row = idx[1] * HALF + idx[2] * SHARE
    lines[...] = jnp.zeros_like(lines)
    for layer in range(layers):
        if layer:
            out[SHARE * (layer - 1) : SHARE * layer, :] = weight[layer, rows_at(own_row, SHARE), :]
        lines[left * layer : left * (layer + 1), :] = weight[layer, MAIN:width, :].astype(F32)
        at = left * layers + layer
        lines[at : at + 1, 0:width] = bias[layer : layer + 1, :].astype(F32)
    out[(layers - 1) * SHARE :, :] = lines[...].astype(BF16)


def pack_rest(idx, inputs, vectors, weight1, weight2, ids, days, *refs, blocks):
    out, own1, tally, chunks = refs[0], refs[1], refs[2], refs[3:]
    depth, size = weight1.shape
    width = inputs.shape[0]
    hidden = weight2.shape[1]
    part = chunks[0].shape[1]
    own_row = idx[1] * HALF + idx[2] * SHARE
    own1[:, 0:depth] = weight1[...].T
    own1[:, depth:] = jnp.zeros((size, own1.shape[1] - depth), BF16)
    out[0:SHARE, :] = own1[rows_at(own_row, SHARE), 0:depth]
    out[SHARE : 2 * SHARE, 0:hidden] = weight2[rows_at(own_row, SHARE), :]
    out[SHARE : 2 * SHARE, hidden:] = jnp.zeros((SHARE, depth - hidden), BF16)
    for turn in range(blocks):
        lanes = pl.ds(pl.multiple_of(block_ahead(idx, turn, blocks) * part, LANES), part)
        chunks[turn][0:width, :] = inputs[:, lanes]
        chunks[turn][width : width + 3, :] = vectors[...]
    fields, tokens = ids.shape
    bucket = lax.broadcasted_iota(jnp.int32, (BUCKETS, tokens), 0)
    lane = lane_of((BUCKETS, LANES))
    tile = jnp.zeros((BUCKETS, LANES), F32)
    for field in range(fields + 1):
        line = ids[field : field + 1, :] if field < fields else days[...]
        hits = jnp.sum((bucket == line).astype(F32), axis=1, keepdims=True)
        high = jnp.floor(hits * (1.0 / 256.0))
        tile = jnp.where(lane == field, high, tile)
        tile = jnp.where(lane == COUNT + field, hits - 256.0 * high, tile)
    tally[0:BUCKETS, :] = tile.astype(BF16)
    tally[BUCKETS:, :] = jnp.zeros((tally.shape[0] - BUCKETS, LANES), BF16)


def place_cross(idx, weight, own, slices, blocks, layer, pad):
    weight[layer, rows_at(idx[0] * pad, MAIN), :] = own[layer, 0:MAIN, :]
    pieces = slices[8:] if layer else slices[:8]
    at = SHARE * (layer - 1) if layer else 0
    for turn in range(1, blocks):
        base = block_of(idx, turn, blocks) * pad
        for offset, piece in zip(places(idx), pieces):
            weight[layer, rows_at(base + offset, SHARE), :] = piece[turn - 1, at : at + SHARE, :]


def place_rest(idx, weight, turned, lines, tail, blocks, layers, left, pad):
    tail[...] = jnp.zeros_like(tail)
    for turn, piece in enumerate(turned):
        lines[block_of(idx, turn, blocks)] = piece[(layers - 1) * SHARE :, :].astype(F32)
    for block in range(blocks):
        for layer in range(layers):
            tail[0:left, :] = lines[block, left * layer : left * (layer + 1), :]
            at = pad * block + MAIN
            weight[layer, at : at + 16, :] = tail[...].astype(BF16)


def cross_forward(idx, *refs, blocks, layers, width, pad, depth):
    pieces, refs = refs[:blocks], refs[blocks:]
    own, refs = refs[0], refs[1:]
    turned, refs = refs[:blocks], refs[blocks:]
    slices, refs = refs[:16], refs[16:]
    z_out, x_out, weight, lines, tail, start, state, nat = refs
    left = width - MAIN
    place_rest(idx, weight, turned, lines, tail, blocks, layers, left, pad)
    bias = [lines[block, :, 0:384].T for block in range(blocks)]
    for turn, piece in enumerate(pieces):
        block = block_of(idx, turn, blocks)
        start[block, 0:width, :] = piece[0:width, :].astype(F32)
        start[block, width:, :] = jnp.zeros((pad - width, piece.shape[1]), F32)
    full = nat.shape[0]
    ones = lax.broadcasted_iota(jnp.int32, (full - depth, nat.shape[1]), 0) == 0
    nat[depth:full, :] = ones.astype(F32)
    for block in range(blocks):
        nat[width * block : width * (block + 1), :] = start[block, 0:width, :]
    for layer in range(layers):
        x_out[layer] = nat[...].astype(BF16)
        place_cross(idx, weight, own, slices, blocks, layer, pad)
        at = left * layers + layer
        for block in range(blocks):
            rows = slice(pad * block, pad * (block + 1))
            value = dot(weight[layer, rows, :], x_out[layer, 0:depth, :], NN) + bias[block][0:pad, at : at + 1]
            z_out[layer, rows, :] = value
            before = start[block] if layer == 0 else state[block]
            value = start[block] * value + before
            state[block] = value
            nat[width * block : width * (block + 1), :] = value[0:width, :]
    x_out[layers] = nat[...].astype(BF16)


def tower_both(idx, *refs, blocks, layers, width, depth, fields, examples):
    (labels, day_ids), refs = refs[:2], refs[2:]
    pieces, refs = refs[:blocks], refs[blocks:]
    (own1, own2), refs = refs[:2], refs[2:]
    slices, refs = refs[:8], refs[8:]
    x_all, acts, far, heads, flow, lines_out, day_out, field_out = refs[:8]
    inputs, t1, t2, slope1, act2, headed, vectors = refs[8:]
    hidden = t1.shape[0]
    size = hidden // blocks
    part = x_all.shape[2]
    low = depth // LANES * LANES
    offsets = places(idx)
    base = idx[0] * size
    t1[rows_at(base, size), :] = own1[...]
    t2[rows_at(base, size), :] = own2[...]
    for turn, piece in enumerate(pieces):
        inputs[block_of(idx, turn, blocks)] = piece[width : width + 3, :].astype(F32)
    for turn in range(1, blocks):
        base = block_of(idx, turn, blocks) * size
        for offset, piece in zip(offsets, slices):
            rows = rows_at(base + offset, SHARE)
            t1[rows, :] = piece[turn - 1, 0:SHARE, :]
            t2[rows, :] = piece[turn - 1, SHARE : 2 * SHARE, 0:hidden]
    parts = [slice(size * block, size * (block + 1)) for block in range(blocks)]
    columns = []
    for block in range(blocks):
        vectors[0:3, :] = inputs[block]
        columns.append(vectors[...].T)
    for rows, column in zip(parts, columns):
        act, slope = gelu_parts(dot(t1[rows, 0:depth], x_all[layers, 0:depth, :], NN) + column[:, 0:1])
        acts[0, rows, :] = act.astype(BF16)
        slope1[rows, :] = slope
    logits = jnp.zeros((1, part), F32)
    for rows, column in zip(parts, columns):
        act, slope = gelu_parts(dot(t2[:, rows], acts[0], TN) + column[:, 2:3])
        act2[rows, :] = act
        headed[rows, :] = column[:, 1:2] * slope
        logits += jnp.sum(act * column[:, 1:2], axis=0, keepdims=True)

    tally = jnp.zeros(slices[0].shape[:2] + (LANES,), F32)
    for piece in slices:
        tally += piece[:, :, low:].astype(F32)
    tally = tally.reshape(-1, LANES)[0:BUCKETS, :]
    shift = depth - low
    high = tally[:, shift : shift + fields + 1]
    count = 256.0 * high + tally[:, shift + COUNT : shift + COUNT + fields + 1]
    days = count[0:32, fields : fields + 1]
    padded = jnp.concatenate([count, jnp.zeros((BUCKETS, LANES - fields - 1), F32)], axis=1).T
    field_out[...] = padded[0:fields, :].astype(jnp.int32)
    day_out[...] = padded[fields : fields + 1, :].astype(jnp.int32)

    mine = pl.ds(pl.multiple_of(idx[0] * part, LANES), part)
    lab = labels[:, mine].astype(F32)
    table = (lax.broadcasted_iota(jnp.int32, (32, part), 0) == day_ids[:, mine]).astype(F32)
    share = examples / (DAYS * jnp.maximum(days, 1.0))
    weights = jnp.sum(table * share, axis=0, keepdims=True)
    decay = jnp.exp(-jnp.abs(logits))
    loss = jnp.maximum(logits, 0.0) + jnp.log1p(decay) - lab * logits
    sigmoid = jnp.where(logits >= 0.0, 1.0, decay) / (1.0 + decay)
    dl = weights * (sigmoid - lab)
    losses = dot(jnp.broadcast_to(loss, (8, part)), table, NT, lax.Precision.HIGHEST)[0:1, :]
    lines_out[0:1, :] = logits
    lines_out[1:2, :] = jnp.zeros_like(logits)
    lines_out[1:2, 0 : losses.shape[1]] = losses

    acts[1] = (dl * headed[...]).astype(BF16)
    far[0:hidden, :] = acts[1]
    for rows in parts:
        acts[2, rows, :] = (dot(t2[rows, :], acts[1], NN) * slope1[rows, :]).astype(BF16)
    for block in range(blocks):
        rows = rows_at(block * size + (1 - idx[1]) * HALF, HALF)
        at = hidden + HALF * block
        far[at : at + HALF, :] = acts[0, rows, :]
        at = hidden + HALF * (block + blocks)
        far[at : at + HALF, :] = acts[2, rows, :]
    for rows in parts:
        heads[rows, :] = jnp.broadcast_to(jnp.sum(act2[rows, :] * dl, axis=1, keepdims=True), (size, LANES))
    flow[...] = dot(t1[:, 0:depth], acts[2], TN)


def cross_backward(idx, *refs, blocks, layers, width, pad, depth):
    extra_lines, refs = refs[0], refs[1:]
    pieces, refs = refs[:blocks], refs[blocks:]
    own, refs = refs[0], refs[1:]
    turned, refs = refs[:blocks], refs[blocks:]
    slices, refs = refs[:16], refs[16:]
    (dx3, z_all), refs = refs[:2], refs[2:]
    eg_out, refs = refs[:blocks], refs[blocks:]
    dz_out, rest_out, dz_far_last, dz_far_out = refs[:4]
    weight, inputs, lines, tail, flow, padded, total, rest = refs[4:]
    left = width - MAIN
    place_rest(idx, weight, turned, lines, tail, blocks, layers, left, pad)
    for turn, piece in enumerate(pieces):
        inputs[block_of(idx, turn, blocks)] = piece[0:width, :].astype(F32)
    padded[...] = jnp.zeros_like(padded)
    rest[...] = jnp.zeros_like(rest)
    for layer in reversed(range(layers)):
        source = dx3 if layer == layers - 1 else flow
        for block in range(blocks):
            rows = slice(pad * block, pad * (block + 1))
            dx = source[width * block : width * (block + 1), :]
            padded[block, 0:width, :] = dx
            dx = padded[block, 0:width, :]
            dz = dx * inputs[block]
            term = dx * z_all[layer, pad * block : pad * block + width, :]
            total[block, 0:width, :] = term if layer == layers - 1 else total[block, 0:width, :] + term
            rest[left * block : left * (block + 1), :] = dz[MAIN:width, :]
            padded[block, 0:width, :] = dz
            dz_out[layer, rows, :] = padded[block].astype(BF16)
        rest_out[layer] = rest[...].astype(BF16)
        far = dz_far_last.at[0] if layer == layers - 1 else dz_far_out.at[layer]
        far[HALF * blocks :, :] = rest[...].astype(BF16)
        for block in range(blocks):
            rows = rows_at(pad * block + (1 - idx[1]) * HALF, HALF)
            far[HALF * block : HALF * (block + 1), :] = dz_out[layer, rows, :]
        place_cross(idx, weight, own, slices, blocks, layer, pad)
        flow[...] = source[...] + dot(weight[layer], dz_out[layer], TN)
    extras = split3(extra_lines[0:1, :]) + split3(extra_lines[1:2, :])
    for block in range(blocks):
        total[block, 0:width, :] += flow[width * block : width * (block + 1), :]
        total[block, width:, :] = jnp.zeros((pad - width, flow.shape[1]), F32)
        for at, extra in enumerate(extras):
            total[block, width + at : width + at + 1, :] = extra
    for turn in range(blocks):
        eg_out[turn][...] = total[block_ahead(idx, turn, blocks)].astype(BF16)


def tower_grads(idx, x_all, x_far, acts, far, head, near_out, far_out, send_out, *refs, blocks, depth, layers):
    x_cat, acts_in, far_in, heads, lhs, d_cat, near, away, send, sems = refs
    hidden = acts.shape[1]
    size = hidden // blocks
    part = acts.shape[2]
    low = depth // LANES * LANES
    bias = depth - low
    copies = Copies(sems)
    first = [
        copies.start(acts, acts_in),
        copies.start(far, far_in),
        copies.start(x_all.at[layers], x_cat.at[:, 0:part]),
        copies.start(x_far.at[layers], x_cat.at[:, part : 2 * part]),
        copies.start(head, heads),
    ]
    wait(*first)
    lane = lane_of((SHARE, LANES))
    pick = (lax.broadcasted_iota(jnp.int32, (LANES, 2 * part), 0) == bias + 1).astype(BF16)
    order = [(where, slot) for where in range(4) for slot in range(blocks)]
    shares = relative(idx)
    d_cat[:, 0:part] = acts_in[1]
    d_cat[:, part:] = far_in[0:hidden, :]
    scale = []
    for at, (where, slot) in enumerate(order):
        block = block_ahead(idx, slot, blocks)
        rows = rows_at(block * size + idx[1] * HALF + SHARE * shares[where], SHARE)
        other = rows_at(block * size + (1 - idx[1]) * HALF + SHARE * shares[where], SHARE)
        lines = rows_at(hidden + HALF * block + SHARE * shares[where], SHARE)
        after_it = rows_at(hidden + HALF * (block + blocks) + SHARE * shares[where], SHARE)
        here = slice(SHARE * at, SHARE * (at + 1))
        lhs[0, here, 0:part] = acts_in[2, rows, :]
        lhs[0, here, part:] = far_in[after_it, :]
        lhs[1, here, 0:part] = acts_in[0, rows, :]
        lhs[1, here, part:] = far_in[lines, :]
        lhs[2, here, 0:part] = acts_in[1, rows, :]
        lhs[2, here, part:] = far_in[rows, :]
        scale.append(
            jnp.where(lane == bias + 2, heads[rows, :], 0.0) + jnp.where(lane == bias + 3, heads[other, :], 0.0)
        )
    extra = dot(lhs[2], pick, NT)
    wide = dot(lhs[0], x_cat[...], NT)
    deep = dot(lhs[1], d_cat[...], NT)
    for at, (where, slot) in enumerate(order):
        target = (near, away, send.at[0], send.at[1])[where].at[slot]
        here = slice(SHARE * at, SHARE * (at + 1))
        target[0:SHARE, 0:low] = wide[here, 0:low].astype(BF16)
        target[0:SHARE, low:] = (wide[here, low:] + extra[here, :] + scale[at]).astype(BF16)
        target[SHARE : 2 * SHARE, 0:hidden] = deep[here, :].astype(BF16)
        target[SHARE : 2 * SHARE, hidden:] = jnp.zeros((SHARE, target.shape[1] - hidden), BF16)
    wait(copies.start(send, send_out), copies.start(near, near_out), copies.start(away, far_out))


def cross_grads(idx, x_all, x_far, dz, rest, dz_far, near_out, far_out, send_out, *refs, blocks, base, pad, depth):
    x_cat, dz_in, far_in, rest_in, lhs, few, near, away, send, sems = refs
    part = dz.shape[2]
    low = depth // LANES * LANES
    groups = -(-depth // MAIN)
    count = dz_far.shape[0]
    copies = Copies(sems)
    first = []
    for layer in reversed(range(count)):
        first.append(
            [
                copies.start(dz.at[base + layer], dz_in.at[layer]),
                copies.start(dz_far.at[layer], far_in.at[layer]),
                copies.start(rest.at[base + layer], rest_in.at[layer]),
                copies.start(x_all.at[base + layer], x_cat.at[layer, :, 0:part]),
                copies.start(x_far.at[base + layer], x_cat.at[layer, :, part : 2 * part]),
            ]
        )
    few[...] = jnp.zeros_like(few)
    order = [(where, slot) for where in range(4) for slot in range(blocks)]
    shares = relative(idx)
    for layer, started in zip(reversed(range(count)), first):
        wait(*started)
        extra = jnp.zeros((HALF, LANES), F32)
        for group in range(groups):
            lines = slice(REST + 16 * group, REST + 16 * (group + 1))
            few[group, lines, 0:part] = rest_in[layer]
            few[group, lines, part:] = far_in[layer, HALF * blocks :, :]
            if MAIN * (group + 1) <= depth:
                rows = rows_at(MAIN * group + idx[1] * HALF, HALF)
            else:
                rows = slice(MAIN * group, MAIN * group + HALF)
            extra += dot(x_cat[layer, rows, :], few[group], NT)
        for at, (where, slot) in enumerate(order):
            block = block_ahead(idx, slot, blocks)
            rows = rows_at(pad * block + idx[1] * HALF + SHARE * shares[where], SHARE)
            lines = rows_at(HALF * block + SHARE * shares[where], SHARE)
            here = slice(SHARE * at, SHARE * (at + 1))
            lhs[here, 0:part] = dz_in[layer, rows, :]
            lhs[here, part:] = far_in[layer, lines, :]
        grad = dot(lhs[...], x_cat[layer], NT)
        lines = slice(SHARE * layer, SHARE * (layer + 1))
        wide = [extra[SHARE * q : SHARE * (q + 1), :] for q in range(4)]
        for at, (where, slot) in enumerate(order):
            target = (near, away, send.at[0], send.at[1])[where].at[slot]
            here = slice(SHARE * at, SHARE * (at + 1))
            target[lines, 0:low] = grad[here, 0:low].astype(BF16)
            more = wide[0]
            for q in range(1, 4):
                more = jnp.where(shares[where] == q, wide[q], more)
            target[lines, low:] = (grad[here, low:] + more).astype(BF16)
    wait(copies.start(send, send_out), copies.start(near, near_out), copies.start(away, far_out))


def eight(mine, one, two, far):
    return [mine, one, two.at[0], two.at[1]] + [far.at[at] for at in range(4)]


def finish_input(idx, *refs, blocks, lane):
    pieces, (out, logits, losses, day_held) = refs[:blocks], refs[blocks:]
    width = out.shape[0]
    size = pieces[0].shape[1]
    for turn, piece in enumerate(pieces):
        block = block_of(idx, turn, blocks)
        lanes = pl.ds(pl.multiple_of(block * size, LANES), size)
        values = piece[...].astype(F32)
        line = lambda at: values[width + at : width + at + 1, :]
        out[:, lanes] = values[0:width, :]
        logits[:, lanes] = line(0) + line(1) + line(2)
        day_held[block] = jnp.broadcast_to(line(3) + line(4) + line(5), day_held.shape[1:])
    days = day_held[0]
    for block in range(1, blocks):
        days += day_held[block]
    row = lax.broadcasted_iota(jnp.int32, losses.shape, 0)
    tile = jnp.zeros(losses.shape, F32)
    for at, value in enumerate(split3(days[0:1, 0:LANES])):
        tile = jnp.where(row == SHARE + at, value, tile)
    losses[...] = pltpu.roll(tile, lane, 1)


def finish_tower(idx, *refs, depth):
    slices, (counts, out1, out2, rows_out, mean_out, lines, day_held) = eight(*refs[:4]), refs[4:]
    low = depth // LANES * LANES
    size, hidden = out2.shape
    for offset, piece in zip(places(idx), slices):
        lines[rows_at(offset, SHARE), :] = piece[0:SHARE, :].astype(F32)
        out2[rows_at(offset, SHARE), :] = piece[SHARE : 2 * SHARE, 0:hidden].astype(F32)
        tile = piece[SHARE : SHARE + 16, low:].astype(F32)
        day_held[lax.div(offset, SHARE)] = tile[0:1, :] + tile[1:2, :] + tile[2:3, :]
    turned = lines[...].T
    out1[...] = turned[0:depth, :]
    head = turned[depth + 3 : depth + 4, :]
    rows_out[0:1, :] = turned[depth : depth + 1, :]
    rows_out[1:2, :] = turned[depth + 1 : depth + 2, :]
    rows_out[2:3, 0:HALF] = turned[depth + 2 : depth + 3, 0:HALF] + head[:, HALF:]
    rows_out[2:3, HALF:] = turned[depth + 2 : depth + 3, HALF:] + head[:, 0:HALF]
    days = day_held[0]
    for at in range(1, day_held.shape[0]):
        days += day_held[at]
    at = depth - low
    days = days[:, at : at + DAYS]
    mean = days / jnp.maximum(counts[:, 0:DAYS].astype(F32), 1.0)
    mean_out[...] = jnp.sum(mean, axis=1, keepdims=True) / DAYS


def finish_cross(idx, *refs, blocks, base, more):
    slices, refs = eight(*refs[:4]), refs[4:]
    before, (out, bias_out, held, lines, sems) = refs[:more], refs[more:]
    count, width, depth = held.shape
    left = width - MAIN
    low = depth // LANES * LANES
    copies = Copies(sems)
    last = []
    if more:
        bias_out[count:, :] = before[1][...]
    for layer in range(count):
        rows = slice(SHARE * layer, SHARE * (layer + 1))
        for offset, piece in zip(places(idx), slices):
            held[layer, rows_at(offset, SHARE), :] = piece[rows, 0:depth].astype(F32)
            lines[rows_at(offset, SHARE), :] = piece[rows, low:].astype(F32)
        turned = lines[...].T
        bias_out[layer : layer + 1, 0:MAIN] = turned[depth - low : depth - low + 1, :]
        for group in range(-(-depth // MAIN)):
            rest = jnp.zeros((left, MAIN), F32)
            for block in range(blocks):
                at = REST + 16 * group + left * block
                rest = jnp.where(idx[0] == block, turned[at : at + left, :], rest)
            stop = min(depth, MAIN * (group + 1)) - MAIN * group
            held[layer, MAIN:width, MAIN * group : MAIN * group + stop] = rest[:, 0:stop]
        last.append(copies.start(held.at[layer], out.at[base + layer]))
        corner = jnp.broadcast_to(rest[:, stop : stop + 1], (left, LANES))
        ahead = lax.broadcasted_iota(jnp.int32, (left, LANES), 0) == lane_of((left, LANES))
        line = jnp.sum(jnp.where(ahead, corner, 0.0), axis=0, keepdims=True)
        bias_out[layer : layer + 1, MAIN:width] = line[:, 0:left]
    wait(*last)


def per_device(
    embedded,
    feature_ids,
    day_ids,
    labels,
    cross_weight,
    cross_bias,
    tower1,
    tower1_bias,
    tower2,
    tower2_bias,
    head_weight,
):
    blocks = lax.axis_size("mp")
    groups = lax.axis_size("dp")
    tokens, width = embedded.shape
    layers, _, depth = cross_weight.shape
    size, hidden = tower2.shape
    pad = -(-width // 16) * 16
    full = -(-(depth + 3) // LANES) * LANES
    part = tokens // blocks
    examples = tokens * groups
    flat = blocks * pad
    shape = jax.ShapeDtypeStruct
    vmem = pltpu.VMEM

    me = lax.axis_index("mp")
    group = lax.axis_index("dp")
    core, plane = group & 1, (group >> 1) & 3
    idx = jnp.stack([me, core, plane]).astype(jnp.int32)
    swap = lambda bits: [(i, i ^ bits(i)) for i in range(groups)]
    first = swap(lambda i: 4 if i & 1 else 2)
    second = swap(lambda i: 2 if i & 1 else 4)
    pair = swap(lambda i: 1)
    others = [swap(lambda i, b=b: 1 << b) for b in range(3, groups.bit_length() - 1)]
    turn_by = lambda r: [(i, (i + r) % blocks) for i in range(blocks)]
    hop = lambda value, perm: lax.ppermute(value, "dp", perm)
    turns = lambda values: [
        lax.ppermute(value, "mp", turn_by(r + 1)) for r, value in enumerate(values)
    ]

    first_send = call(
        pack_first,
        shape((SHARE, depth), BF16),
        [],
        [idx, cross_weight],
        mib=4,
        spec=HBM,
        out_spec=VMEM,
        copies=1,
    )
    first_turned = turns([first_send] * (blocks - 1))
    cross_send = call(
        pack_cross,
        shape(((layers - 1) * SHARE + 16, depth), BF16),
        [vmem((16, depth), F32)],
        [after(idx, first_send), cross_weight, cross_bias],
        mib=8,
        nbytes=2 << 20,
    )
    vectors = jnp.stack([tower1_bias, head_weight, tower2_bias])
    tower_send, tower_own, tally, *chunks = call(
        functools.partial(pack_rest, blocks=blocks),
        tuple(
            [shape((2 * SHARE, depth), BF16), shape((size, full), BF16), shape(((blocks - 1) * 2 * SHARE, LANES), BF16)]
            + [shape((width + 3, part), BF16)] * blocks
        ),
        [],
        [after(idx, first_send), embedded.T, vectors, tower1, tower2, feature_ids.T, day_ids[None, :]],
        mib=24,
        nbytes=2 << 20,
    )
    for perm in others:
        tally = tally + hop(tally, perm)

    join = lambda *values: lax.optimization_barrier(values)
    with_pair = lambda held: held + [hop(value, pair) for value in held]
    first_mine = jnp.stack(first_turned)
    first_mine, cross_send = join(first_mine, cross_send)
    first_one, first_two = hop(first_mine, first), hop(first_mine, second)
    cross_turned = turns([cross_send] * (blocks - 1))
    first_one, first_two, tower_send, *cross_turned = join(first_one, first_two, tower_send, *cross_turned)

    first_three = hop(first_one, second)
    cross_mine = jnp.stack([value[: (layers - 1) * SHARE] for value in cross_turned])
    cross_one, cross_two = hop(cross_mine, first), hop(cross_mine, second)
    tower_turned = turns([tower_send] * (blocks - 1))
    first_three, cross_one, cross_two, *tower_turned = join(first_three, cross_one, cross_two, *tower_turned)

    first_slices = with_pair([first_mine, first_one, first_two, first_three])
    cross_three = hop(cross_one, second)
    tower_mine = jnp.concatenate(
        [jnp.stack(tower_turned), tally.reshape(blocks - 1, 2 * SHARE, LANES)[:, :, : full - depth]], axis=2
    )
    tower_one, tower_two = hop(tower_mine, first), hop(tower_mine, second)
    pieces = [chunks[0]] + turns([after(chunk, tower_turned[0]) for chunk in chunks[1:]])
    cross_three, tower_one, tower_two, *pieces = join(cross_three, tower_one, tower_two, *pieces)

    tower_three = hop(tower_one, second)
    cross_slices = first_slices + with_pair([cross_mine, cross_one, cross_two, cross_three])
    tower_slices = with_pair([tower_mine, tower_one, tower_two, tower_three])

    z_all, x_all = call(
        functools.partial(cross_forward, blocks=blocks, layers=layers, width=width, pad=pad, depth=depth),
        (shape((layers, flat, part), F32), shape((layers + 1, full, part), BF16)),
        [
            vmem((layers, flat, depth), BF16),
            vmem((blocks, 16, depth), F32),
            vmem((16, depth), F32),
            vmem((blocks, pad, part), F32),
            vmem((blocks, pad, part), F32),
            vmem((full, part), F32),
        ],
        [idx, *pieces, cross_weight, cross_send, *cross_turned, *cross_slices],
        mib=28,
        flops=2 * layers * flat * full * part,
        nbytes=20 << 20,
    )
    x_far = hop(x_all, pair)
    fields = feature_ids.shape[1]
    acts, far, head_col, dx3, lines, day_line, field_counts = call(
        functools.partial(
            tower_both, blocks=blocks, layers=layers, width=width, depth=depth, fields=fields, examples=examples
        ),
        (
            shape((3, hidden, part), BF16),
            shape((2 * hidden, part), BF16),
            shape((hidden, LANES), F32),
            shape((depth, part), F32),
            shape((2, part), F32),
            shape((1, BUCKETS), jnp.int32),
            shape((fields, BUCKETS), jnp.int32),
        ),
        [
            vmem((blocks, 3, part), F32),
            vmem((hidden, full), BF16),
            vmem((hidden, hidden), BF16),
            vmem((hidden, part), F32),
            vmem((hidden, part), F32),
            vmem((hidden, part), F32),
            vmem((8, part), F32),
        ],
        [
            idx,
            labels[None, :],
            day_ids[None, :],
            *pieces,
            tower_own,
            tower2,
            *tower_slices,
            x_all,
        ],
        mib=28,
        flops=8 * hidden * full * part,
        nbytes=10 << 20,
    )
    far = hop(far, pair)

    def halves(rows):
        keep = (blocks, rows, full)
        return keep, keep, (2,) + keep

    def grads(kernel, rows, scratch, args, copies, flops):
        return call(
            kernel,
            tuple(shape(s, BF16) for s in halves(rows)),
            scratch + [vmem(s, BF16) for s in halves(rows)],
            args,
            mib=20,
            spec=HBM,
            copies=copies,
            flops=flops,
            nbytes=10 << 20,
        )

    tower_parts = grads(
        functools.partial(tower_grads, blocks=blocks, depth=depth, layers=layers),
        2 * SHARE,
        [
            vmem((full, 2 * part), BF16),
            vmem((3, hidden, part), BF16),
            vmem((2 * hidden, part), BF16),
            vmem((hidden, LANES), F32),
            vmem((3, HALF * blocks, 2 * part), BF16),
            vmem((hidden, 2 * part), BF16),
        ],
        [idx, x_all, x_far, acts, far, head_col],
        8,
        4 * hidden * full * part,
    )
    tower_arrived = hop(tower_parts[2], first)
    *input_grads, dz, dz_rest, last_far, dz_far = call(
        functools.partial(cross_backward, blocks=blocks, layers=layers, width=width, pad=pad, depth=depth),
        tuple([shape((pad, part), BF16)] * blocks)
        + (
            shape((layers, flat, part), BF16),
            shape((layers, 16, part), BF16),
            shape((1, HALF * blocks + 16, part), BF16),
            shape((layers - 1, HALF * blocks + 16, part), BF16),
        ),
        [
            vmem((layers, flat, depth), BF16),
            vmem((blocks, width, part), F32),
            vmem((blocks, 16, depth), F32),
            vmem((16, depth), F32),
            vmem((depth, part), F32),
            vmem((blocks, pad, part), F32),
            vmem((blocks, pad, part), F32),
            vmem((16, part), F32),
        ],
        [
            after(idx, tower_parts[2]),
            lines,
            *pieces,
            cross_weight,
            cross_send,
            *cross_turned,
            *cross_slices,
            dx3,
            z_all,
        ],
        mib=34,
        flops=2 * layers * flat * full * part,
        nbytes=20 << 20,
    )
    last_far = hop(last_far, pair)
    dz_far = hop(dz_far, pair)

    def cross_parts_of(base, count, far, start):
        return grads(
            functools.partial(cross_grads, blocks=blocks, base=base, pad=pad, depth=depth),
            count * SHARE,
            [
                vmem((count, full, 2 * part), BF16),
                vmem((count, flat, part), BF16),
                vmem((count, HALF * blocks + 16, part), BF16),
                vmem((count, 16, part), BF16),
                vmem((HALF * blocks, 2 * part), BF16),
                vmem((-(-depth // MAIN), LANES, 2 * part), BF16),
            ],
            [start, x_all, x_far, dz, dz_rest, far],
            5 * count + 3,
            2 * count * flat * full * part,
        )

    last_parts = cross_parts_of(layers - 1, 1, last_far, idx)
    cross_parts = cross_parts_of(0, layers - 1, dz_far, after(idx, last_parts[2]))

    down = lambda value: value.astype(BF16)
    up = lambda value: value.astype(F32)

    def near_sum(parts, arrived, last):
        return up(parts[0]) + up(arrived[0]) + up(last)

    def far_send(parts, arrived):
        return hop(down(up(parts[1]) + up(arrived[1])), second)

    def send_blocks(held):
        return turns([down(held[r]) for r in range(1, blocks)])

    def total_of(held, turned):
        held = held[0] + sum(up(value) for value in turned)
        for perm in others:
            held = held + hop(held, perm)
        return held

    def two_of(mine, one):
        return hop(jnp.stack([mine, one]), second)

    def far_of(mine, one, two):
        return hop(jnp.concatenate([jnp.stack([mine, one]), two]), pair)

    tower_arrived, last_send = join(tower_arrived, last_parts[2])
    tower_second = far_send(tower_parts, tower_arrived)
    last_arrived = hop(last_send, first)
    grad_pieces = [input_grads[0]] + turns([after(value, last_send) for value in input_grads[1:]])
    tower_second, last_arrived, cross_send, *grad_pieces = join(
        tower_second, last_arrived, cross_parts[2], *grad_pieces
    )

    tower_held = near_sum(tower_parts, tower_arrived, tower_second)
    tower_turned = send_blocks(tower_held)
    last_second = far_send(last_parts, last_arrived)
    cross_arrived = hop(cross_send, first)
    input_out, logits_all, losses = call(
        functools.partial(finish_input, blocks=blocks, lane=depth % LANES),
        (shape((width, tokens), F32), shape((1, tokens), F32), shape((2 * SHARE, LANES), F32)),
        [vmem((blocks, 8, part), F32)],
        [idx, *grad_pieces],
        mib=16,
        nbytes=2 << 20,
    )
    last_second, cross_arrived, losses, *tower_turned = join(last_second, cross_arrived, losses, *tower_turned)

    last_held = near_sum(last_parts, last_arrived, last_second)
    last_turned = send_blocks(last_held)
    cross_second = far_send(cross_parts, cross_arrived)
    tower_mine = down(total_of(tower_held, tower_turned) + jnp.pad(losses, ((0, 0), (full - LANES, 0))))
    tower_one = hop(tower_mine, first)
    cross_second, tower_one, *last_turned = join(cross_second, tower_one, *last_turned)

    cross_held = near_sum(cross_parts, cross_arrived, cross_second)
    cross_turned = send_blocks(cross_held)
    tower_two = two_of(tower_mine, tower_one)
    last_mine = down(total_of(last_held, last_turned))
    last_one = hop(last_mine, first)
    tower_two, last_one, *cross_turned = join(tower_two, last_one, *cross_turned)

    cross_mine = down(total_of(cross_held, cross_turned))
    cross_one = hop(cross_mine, first)
    last_two = two_of(last_mine, last_one)
    tower_far = far_of(tower_mine, tower_one, tower_two)
    cross_one, last_two, tower_far = join(cross_one, last_two, tower_far)

    cross_two = two_of(cross_mine, cross_one)
    last_far = far_of(last_mine, last_one, last_two)
    tower_sums = [tower_mine, tower_one, tower_two, tower_far]
    last_sums = [last_mine, last_one, last_two, last_far]
    tower1_grad, tower2_grad, rows, mean = call(
        functools.partial(finish_tower, depth=depth),
        (shape((depth, size), F32), shape((size, hidden), F32), shape((3, size), F32), shape((1, 1), F32)),
        [vmem((size, full), F32), vmem((8, 1, LANES), F32)],
        [idx, *tower_sums, day_line],
        mib=16,
        nbytes=4 << 20,
    )
    def finish(sums, base, count, before):
        alias = {5: 0} if before else {}
        return call(
            functools.partial(finish_cross, blocks=blocks, base=base, more=len(before)),
            (shape((layers, width, depth), F32), shape((count + len(before) // 2, width), F32)),
            [vmem((count, width, depth), F32), vmem((MAIN, LANES), F32)],
            [idx, *sums] + [(value, spec) for value, spec in zip(before, (HBM, VMEM))],
            mib=16,
            out_spec=(HBM, VMEM),
            aliases=alias,
            copies=count,
            nbytes=4 << 20,
        )

    before = finish(last_sums, layers - 1, 1, ())
    cross_far = far_of(cross_mine, cross_one, cross_two)
    cross_grad, cross_bias_grad = finish([cross_mine, cross_one, cross_two, cross_far], 0, layers - 1, before)
    day_counts = day_line[0, :DAYS]
    return (
        mean[0, 0],
        logits_all[0],
        input_out.T,
        cross_grad,
        cross_bias_grad,
        tower1_grad,
        rows[0],
        tower2_grad,
        rows[1],
        rows[2],
        day_counts,
        field_counts,
    )


def solution(mesh):
    in_specs = (
        P("dp", "mp"),
        P("dp", None),
        P("dp"),
        P("dp"),
        P(None, "mp", None),
        P(None, "mp"),
        P(None, "mp"),
        P("mp"),
        P("mp", None),
        P("mp"),
        P("mp"),
    )
    out_specs = (
        P(),
        P("dp"),
        P("dp", "mp"),
        P(None, "mp", None),
        P(None, "mp"),
        P(None, "mp"),
        P("mp"),
        P("mp", None),
        P("mp"),
        P("mp"),
        P(),
        P(),
    )
    return jax.shard_map(
        per_device, mesh=mesh, in_specs=in_specs, out_specs=out_specs, check_vma=False
    )
```

```python
import functools

import jax
import jax.numpy as jnp
from jax import lax
from jax.experimental import pallas as pl
from jax.experimental.pallas import tpu as pltpu
from jax.sharding import PartitionSpec as P

DAYS = 24
BUCKETS = 128
BF16 = jnp.bfloat16
F32 = jnp.float32
MAIN = 256
SHARE = 32
HALF = MAIN // 2
LANES = 128
REST = 32
LOSS = 24
COUNT = 16
VMEM = pl.BlockSpec(memory_space=pltpu.VMEM)
SMEM = pl.BlockSpec(memory_space=pltpu.SMEM)
HBM = pl.BlockSpec(memory_space=pl.ANY)
FAR = pl.BlockSpec(memory_space=pltpu.HBM)
NT = (((1,), (1,)), ((), ()))
TN = (((0,), (0,)), ((), ()))
NN = (((1,), (0,)), ((), ()))


def gelu_parts(values):
    cdf_part = 0.5 * (1.0 + lax.erf(values * 0.7071067811865476))
    slope = cdf_part + values * jnp.exp(-0.5 * values * values) * 0.3989422804014327
    return (values * cdf_part, slope)


def dot(lhs, rhs, dims, precision=None):
    return lax.dot_general(lhs, rhs, dims, preferred_element_type=F32, precision=precision)


def call(kernel, outs, scratch, args, mib, spec=VMEM, copies=0, out_spec=None, aliases={}, flops=0, nbytes=0):
    arrays = [a[0] if isinstance(a, tuple) else a for a in args[1:]]
    specs = [a[1] if isinstance(a, tuple) else spec for a in args[1:]]
    if copies:
        scratch = scratch + [pltpu.SemaphoreType.DMA((copies,))]
    return pl.pallas_call(
        kernel,
        out_shape=outs,
        in_specs=[SMEM] + specs,
        out_specs=out_spec or jax.tree.map(lambda _: spec, outs),
        scratch_shapes=scratch,
        input_output_aliases=aliases,
        compiler_params=pltpu.CompilerParams(vmem_limit_bytes=mib << 20),
        cost_estimate=pl.CostEstimate(flops=flops, bytes_accessed=nbytes, transcendentals=0),
    )(args[0], *arrays)


class Copies:
    def __init__(self, sems):
        self.sems, self.count = sems, 0

    def start(self, source, target):
        copy = pltpu.make_async_copy(source, target, self.sems.at[self.count])
        self.count += 1
        copy.start()
        return copy


def wait(*copies):
    for copy in copies:
        copy.wait()


def after(value, *others):
    return lax.optimization_barrier((value,) + others)[0]


def places(idx):
    core, plane = idx[1], idx[2]
    first, second = core + 1, 2 - core
    mine = [plane, plane ^ first, plane ^ second, plane ^ 3]
    theirs = [plane, plane ^ second, plane ^ first, plane ^ 3]
    return [core * HALF + SHARE * q for q in mine] + [(1 - core) * HALF + SHARE * q for q in theirs]


def relative(idx):
    core, plane = idx[1], idx[2]
    first, second = core + 1, 2 - core
    return [plane, plane ^ second, plane ^ first, plane ^ 3]


def block_of(idx, turn, blocks):
    return lax.rem(idx[0] - turn + blocks, blocks)


def block_ahead(idx, turn, blocks):
    return lax.rem(idx[0] + turn, blocks)


def rows_at(offset, size, unit=16):
    return pl.ds(pl.multiple_of(offset, unit), size)


def split3(line):
    high = line.astype(BF16).astype(F32)
    middle = (line - high).astype(BF16).astype(F32)
    return high, middle, line - high - middle


def lane_of(shape):
    return lax.broadcasted_iota(jnp.int32, shape, 1)


def pack_rest(idx, weight, bias, inputs, vectors, weight1, weight2, ids, days, *refs, blocks):
    out, own1, tally = refs[:3]
    chunks, (lines,) = refs[3 : 3 + blocks], refs[3 + blocks :]
    layers, width, depth = weight.shape
    size = weight2.shape[0]
    left = width - MAIN
    part = chunks[0].shape[1]
    full = own1.shape[1]
    own_row = idx[1] * HALF + idx[2] * SHARE

    lines[...] = jnp.zeros_like(lines)
    for layer in range(layers):
        lines[left * layer : left * (layer + 1), 0:depth] = weight[layer, MAIN:width, :].astype(F32)
        at = left * layers + layer
        lines[at : at + 1, 0:width] = bias[layer : layer + 1, :].astype(F32)
    rest = [lines[:, at : at + part].astype(BF16) for at in range(0, lines.shape[1], part)]

    own1[:, 0:depth] = weight1[...].T
    own1[:, depth:] = jnp.zeros((size, full - depth), BF16)
    out[0:SHARE, :] = own1[rows_at(own_row, SHARE), :]
    out[SHARE:, 0 : weight2.shape[1]] = weight2[rows_at(own_row, SHARE), :]
    out[SHARE:, weight2.shape[1] :] = jnp.zeros((SHARE, full - weight2.shape[1]), BF16)

    first = 16 * len(rest)
    for turn in range(blocks):
        lanes = pl.ds(pl.multiple_of(block_ahead(idx, turn, blocks) * part, LANES), part)
        for at, value in enumerate(rest):
            chunks[turn][16 * at : 16 * (at + 1), :] = value
        chunks[turn][first : first + width, :] = inputs[:, lanes]
        chunks[turn][first + width : first + width + 3, :] = vectors[...]

    fields, tokens = ids.shape
    bucket = lax.broadcasted_iota(jnp.int32, (BUCKETS, tokens), 0)
    lane = lane_of((BUCKETS, LANES))
    tile = jnp.zeros((BUCKETS, LANES), F32)
    for field in range(fields + 1):
        line = ids[field : field + 1, :] if field < fields else days[...]
        hits = jnp.sum((bucket == line).astype(F32), axis=1, keepdims=True)
        high = jnp.floor(hits * (1.0 / 256.0))
        tile = jnp.where(lane == COUNT + field, high, tile)
        tile = jnp.where(lane == COUNT + fields + 1 + field, hits - 256.0 * high, tile)
    half = BUCKETS // 2
    tile = tile[0:half, :] + pltpu.roll(tile[half:, :], 2 * (fields + 1), 1)
    tally[0:half, :] = tile.astype(BF16)
    tally[half:, :] = jnp.zeros((tally.shape[0] - half, LANES), BF16)


def cross_eight(refs):
    near, last, near_far, last_far = refs
    return [near.at[at] for at in range(3)] + [last] + [near_far.at[at] for at in range(3)] + [last_far]


def place_cross(idx, weight, own, slices, blocks, layer, pad):
    weight[layer, rows_at(idx[0] * pad, MAIN), :] = own[layer, 0:MAIN, :]
    at = SHARE * layer
    for turn in range(1, blocks):
        base = block_of(idx, turn, blocks) * pad
        for offset, piece in zip(places(idx), slices):
            weight[layer, rows_at(base + offset, SHARE), :] = piece[turn - 1, at : at + SHARE, 0 : weight.shape[2]]


def place_rest(idx, weight, pieces, lines, tail, layers, left, pad):
    blocks = len(pieces)
    depth = weight.shape[2]
    part = pieces[0].shape[1]
    tail[...] = jnp.zeros_like(tail)
    for turn, piece in enumerate(pieces):
        for group in range(-(-depth // part)):
            stop = min(depth, part * (group + 1))
            lines[block_of(idx, turn, blocks), :, part * group : stop] = piece[
                16 * group : 16 * (group + 1), 0 : stop - part * group
            ].astype(F32)
    for block in range(blocks):
        for layer in range(layers):
            tail[0:left, :] = lines[block, left * layer : left * (layer + 1), :]
            at = pad * block + MAIN
            weight[layer, at : at + 16, :] = tail[...].astype(BF16)


def cross_forward(idx, *refs, blocks, layers, width, pad, depth):
    pieces, refs = refs[:blocks], refs[blocks:]
    own, refs = refs[0], refs[1:]
    slices, refs = cross_eight(refs[:4]), refs[4:]
    z_out, x_out, weight, lines, tail, start, state, nat = refs
    left = width - MAIN
    place_rest(idx, weight, pieces, lines, tail, layers, left, pad)
    at = 16 * -(-depth // pieces[0].shape[1])
    bias = [lines[block, :, 0:384].T for block in range(blocks)]
    for turn, piece in enumerate(pieces):
        block = block_of(idx, turn, blocks)
        start[block, 0:width, :] = piece[at : at + width, :].astype(F32)
        start[block, width:, :] = jnp.zeros((pad - width, piece.shape[1]), F32)
    full = nat.shape[0]
    ones = lax.broadcasted_iota(jnp.int32, (full - depth, nat.shape[1]), 0) == 0
    nat[depth:full, :] = ones.astype(F32)
    for block in range(blocks):
        nat[width * block : width * (block + 1), :] = start[block, 0:width, :]
    for layer in range(layers):
        x_out[layer] = nat[...].astype(BF16)
        place_cross(idx, weight, own, slices, blocks, layer, pad)
        at = left * layers + layer
        for block in range(blocks):
            rows = slice(pad * block, pad * (block + 1))
            value = dot(weight[layer, rows, :], x_out[layer, 0:depth, :], NN) + bias[block][0:pad, at : at + 1]
            z_out[layer, rows, :] = value
            before = start[block] if layer == 0 else state[block]
            value = start[block] * value + before
            state[block] = value
            nat[width * block : width * (block + 1), :] = value[0:width, :]
    x_out[layers] = nat[...].astype(BF16)


def tower_both(idx, *refs, blocks, layers, width, depth, fields, examples):
    (labels, day_ids), refs = refs[:2], refs[2:]
    pieces, refs = refs[:blocks], refs[blocks:]
    (own1, own2), refs = refs[:2], refs[2:]
    slices, refs = refs[:8], refs[8:]
    x_all, acts, far, heads, flow, lines_out, day_out, field_out = refs[:8]
    inputs, tower, slope1, act2, headed, vectors = refs[8:]
    hidden = tower.shape[0]
    full = x_all.shape[1]
    size = hidden // blocks
    part = x_all.shape[2]
    low = depth // LANES * LANES
    at = 16 * -(-depth // part) + width
    for turn, piece in enumerate(pieces):
        inputs[block_of(idx, turn, blocks)] = piece[at : at + 3, :].astype(F32)
    base = idx[0] * size
    tower[rows_at(base, size), 0:full] = own1[...]
    tower[rows_at(base, size), full:] = own2[...]
    for turn in range(1, blocks):
        base = block_of(idx, turn, blocks) * size
        for offset, piece in zip(places(idx), slices):
            rows = rows_at(base + offset, SHARE)
            start = piece.shape[1] - 2 * SHARE
            tower[rows, 0:full] = piece[turn - 1, start : start + SHARE, :]
            tower[rows, full:] = piece[turn - 1, start + SHARE :, 0:hidden]
    parts = [slice(size * block, size * (block + 1)) for block in range(blocks)]
    columns = []
    for block in range(blocks):
        vectors[0:3, :] = inputs[block]
        columns.append(vectors[...].T)
    for rows, column in zip(parts, columns):
        act, slope = gelu_parts(dot(tower[rows, 0:depth], x_all[layers, 0:depth, :], NN) + column[:, 0:1])
        acts[0, rows, :] = act.astype(BF16)
        slope1[rows, :] = slope
    logits = jnp.zeros((1, part), F32)
    for rows, column in zip(parts, columns):
        act, slope = gelu_parts(dot(tower[:, full + rows.start : full + rows.stop], acts[0], TN) + column[:, 2:3])
        act2[rows, :] = act
        headed[rows, :] = column[:, 1:2] * slope
        logits += jnp.sum(act * column[:, 1:2], axis=0, keepdims=True)

    half = BUCKETS // 2
    tally = jnp.zeros((half, LANES), F32)
    for piece in slices:
        start = piece.shape[1] - 2 * SHARE
        tally += piece[0 : half // SHARE, start : start + SHARE, low:].astype(F32).reshape(half, LANES)
    count = jnp.concatenate([tally, pltpu.roll(tally, LANES - 2 * (fields + 1), 1)], axis=0)
    high = count[:, COUNT : COUNT + fields + 1]
    count = 256.0 * high + count[:, COUNT + fields + 1 : COUNT + 2 * (fields + 1)]
    days = count[0:32, fields : fields + 1]
    padded = jnp.concatenate([count, jnp.zeros((BUCKETS, LANES - fields - 1), F32)], axis=1).T
    field_out[...] = padded[0:fields, :].astype(jnp.int32)
    day_out[...] = padded[fields : fields + 1, :].astype(jnp.int32)

    mine = pl.ds(pl.multiple_of(idx[0] * part, LANES), part)
    lab = labels[:, mine].astype(F32)
    table = (lax.broadcasted_iota(jnp.int32, (32, part), 0) == day_ids[:, mine]).astype(F32)
    share = examples / (DAYS * jnp.maximum(days, 1.0))
    weights = jnp.sum(table * share, axis=0, keepdims=True)
    decay = jnp.exp(-jnp.abs(logits))
    loss = jnp.maximum(logits, 0.0) + jnp.log1p(decay) - lab * logits
    sigmoid = jnp.where(logits >= 0.0, 1.0, decay) / (1.0 + decay)
    dl = weights * (sigmoid - lab)
    losses = dot(jnp.broadcast_to(loss, (8, part)), table, NT, lax.Precision.HIGHEST)[0:1, :]
    lines_out[0:1, :] = logits
    lines_out[1:2, :] = jnp.zeros_like(logits)
    lines_out[1:2, 0 : losses.shape[1]] = losses

    acts[1] = (dl * headed[...]).astype(BF16)
    far[0:hidden, :] = acts[1]
    for rows in parts:
        acts[2, rows, :] = (dot(tower[rows, full:], acts[1], NN) * slope1[rows, :]).astype(BF16)
    for block in range(blocks):
        rows = rows_at(block * size + (1 - idx[1]) * HALF, HALF)
        at = hidden + HALF * block
        far[at : at + HALF, :] = acts[0, rows, :]
        at = hidden + HALF * (block + blocks)
        far[at : at + HALF, :] = acts[2, rows, :]
    for rows in parts:
        heads[rows, :] = jnp.broadcast_to(jnp.sum(act2[rows, :] * dl, axis=1, keepdims=True), (size, LANES))
    flow[...] = dot(tower[:, 0:depth], acts[2], TN)


def cross_backward(idx, *refs, blocks, layers, width, pad, depth):
    extra_lines, refs = refs[0], refs[1:]
    pieces, refs = refs[:blocks], refs[blocks:]
    own, refs = refs[0], refs[1:]
    slices, refs = cross_eight(refs[:4]), refs[4:]
    (dx3, z_all), refs = refs[:2], refs[2:]
    eg_out, refs = refs[:blocks], refs[blocks:]
    dz_out, rest_out, dz_far_last, dz_far_out = refs[:4]
    weight, inputs, lines, tail, flow, padded, total, rest = refs[4:]
    left = width - MAIN
    place_rest(idx, weight, pieces, lines, tail, layers, left, pad)
    at = 16 * -(-depth // pieces[0].shape[1])
    for turn, piece in enumerate(pieces):
        inputs[block_of(idx, turn, blocks)] = piece[at : at + width, :].astype(F32)
    padded[...] = jnp.zeros_like(padded)
    rest[...] = jnp.zeros_like(rest)
    for layer in reversed(range(layers)):
        source = dx3 if layer == layers - 1 else flow
        for block in range(blocks):
            rows = slice(pad * block, pad * (block + 1))
            dx = source[width * block : width * (block + 1), :]
            padded[block, 0:width, :] = dx
            dx = padded[block, 0:width, :]
            dz = dx * inputs[block]
            term = dx * z_all[layer, pad * block : pad * block + width, :]
            total[block, 0:width, :] = term if layer == layers - 1 else total[block, 0:width, :] + term
            rest[left * block : left * (block + 1), :] = dz[MAIN:width, :]
            padded[block, 0:width, :] = dz
            dz_out[layer, rows, :] = padded[block].astype(BF16)
        rest_out[layer] = rest[...].astype(BF16)
        far = dz_far_last.at[0] if layer == layers - 1 else dz_far_out.at[layer]
        far[HALF * blocks :, :] = rest[...].astype(BF16)
        for block in range(blocks):
            rows = rows_at(pad * block + (1 - idx[1]) * HALF, HALF)
            far[HALF * block : HALF * (block + 1), :] = dz_out[layer, rows, :]
        place_cross(idx, weight, own, slices, blocks, layer, pad)
        flow[...] = source[...] + dot(weight[layer], dz_out[layer], TN)
    extras = split3(extra_lines[0:1, :]) + split3(extra_lines[1:2, :])
    for block in range(blocks):
        total[block, 0:width, :] += flow[width * block : width * (block + 1), :]
        total[block, width:, :] = jnp.zeros((pad - width, flow.shape[1]), F32)
        for at, extra in enumerate(extras):
            total[block, width + at : width + at + 1, :] = extra
    for turn in range(blocks):
        eg_out[turn][...] = total[block_ahead(idx, turn, blocks)].astype(BF16)


def tower_grads(idx, x_all, x_far, acts, far, head, near_out, far_out, send_out, *refs, blocks, depth, layers):
    x_cat, acts_in, far_in, heads, lhs, d_cat, near, away, send, sems = refs
    hidden = acts.shape[1]
    size = hidden // blocks
    part = acts.shape[2]
    low = depth // LANES * LANES
    bias = depth - low
    copies = Copies(sems)
    first = [
        copies.start(acts, acts_in),
        copies.start(far, far_in),
        copies.start(x_all.at[layers], x_cat.at[:, 0:part]),
        copies.start(x_far.at[layers], x_cat.at[:, part : 2 * part]),
        copies.start(head, heads),
    ]
    wait(*first)
    lane = lane_of((SHARE, LANES))
    pick = (lax.broadcasted_iota(jnp.int32, (LANES, 2 * part), 0) == bias + 1).astype(BF16)
    order = [(where, slot) for where in range(4) for slot in range(blocks)]
    shares = relative(idx)
    d_cat[:, 0:part] = acts_in[1]
    d_cat[:, part:] = far_in[0:hidden, :]
    scale = []
    for at, (where, slot) in enumerate(order):
        block = block_ahead(idx, slot, blocks)
        rows = rows_at(block * size + idx[1] * HALF + SHARE * shares[where], SHARE)
        other = rows_at(block * size + (1 - idx[1]) * HALF + SHARE * shares[where], SHARE)
        lines = rows_at(hidden + HALF * block + SHARE * shares[where], SHARE)
        after_it = rows_at(hidden + HALF * (block + blocks) + SHARE * shares[where], SHARE)
        here = slice(SHARE * at, SHARE * (at + 1))
        lhs[0, here, 0:part] = acts_in[2, rows, :]
        lhs[0, here, part:] = far_in[after_it, :]
        lhs[1, here, 0:part] = acts_in[0, rows, :]
        lhs[1, here, part:] = far_in[lines, :]
        lhs[2, here, 0:part] = acts_in[1, rows, :]
        lhs[2, here, part:] = far_in[rows, :]
        scale.append(
            jnp.where(lane == bias + 2, heads[rows, :], 0.0) + jnp.where(lane == bias + 3, heads[other, :], 0.0)
        )
    extra = dot(lhs[2], pick, NT)
    wide = dot(lhs[0], x_cat[...], NT)
    deep = dot(lhs[1], d_cat[...], NT)
    for at, (where, slot) in enumerate(order):
        target = (near, away, send.at[0], send.at[1])[where].at[slot]
        here = slice(SHARE * at, SHARE * (at + 1))
        target[:, 0:low] = wide[here, 0:low].astype(BF16)
        target[:, low : low + LANES] = (wide[here, low:] + extra[here, :] + scale[at]).astype(BF16)
        target[:, low + LANES :] = deep[here, :].astype(BF16)
    wait(copies.start(send, send_out), copies.start(near, near_out), copies.start(away, far_out))


def cross_grads(idx, x_all, x_far, dz, rest, dz_far, near_out, far_out, send_out, *refs, blocks, base, pad, depth):
    x_cat, dz_in, far_in, rest_in, lhs, few, near, away, send, sems = refs
    part = dz.shape[2]
    low = depth // LANES * LANES
    groups = -(-depth // MAIN)
    count = dz_far.shape[0]
    copies = Copies(sems)
    first = []
    for layer in reversed(range(count)):
        first.append(
            [
                copies.start(dz.at[base + layer], dz_in.at[layer]),
                copies.start(dz_far.at[layer], far_in.at[layer]),
                copies.start(rest.at[base + layer], rest_in.at[layer]),
                copies.start(x_all.at[base + layer], x_cat.at[layer, :, 0:part]),
                copies.start(x_far.at[base + layer], x_cat.at[layer, :, part : 2 * part]),
            ]
        )
    few[...] = jnp.zeros_like(few)
    order = [(where, slot) for where in range(4) for slot in range(blocks)]
    shares = relative(idx)
    for layer, started in zip(reversed(range(count)), first):
        wait(*started)
        extra = jnp.zeros((HALF, LANES), F32)
        for group in range(groups):
            lines = slice(REST + 16 * group, REST + 16 * (group + 1))
            few[group, lines, 0:part] = rest_in[layer]
            few[group, lines, part:] = far_in[layer, HALF * blocks :, :]
            if MAIN * (group + 1) <= depth:
                rows = rows_at(MAIN * group + idx[1] * HALF, HALF)
            else:
                rows = slice(MAIN * group, MAIN * group + HALF)
            extra += dot(x_cat[layer, rows, :], few[group], NT)
        for at, (where, slot) in enumerate(order):
            block = block_ahead(idx, slot, blocks)
            rows = rows_at(pad * block + idx[1] * HALF + SHARE * shares[where], SHARE)
            lines = rows_at(HALF * block + SHARE * shares[where], SHARE)
            here = slice(SHARE * at, SHARE * (at + 1))
            lhs[here, 0:part] = dz_in[layer, rows, :]
            lhs[here, part:] = far_in[layer, lines, :]
        grad = dot(lhs[...], x_cat[layer], NT)
        lines = slice(SHARE * layer, SHARE * (layer + 1))
        wide = [extra[SHARE * q : SHARE * (q + 1), :] for q in range(4)]
        for at, (where, slot) in enumerate(order):
            target = (near, away, send.at[0], send.at[1])[where].at[slot]
            here = slice(SHARE * at, SHARE * (at + 1))
            target[lines, 0:low] = grad[here, 0:low].astype(BF16)
            more = wide[0]
            for q in range(1, 4):
                more = jnp.where(shares[where] == q, wide[q], more)
            target[lines, low:] = (grad[here, low:] + more).astype(BF16)
    wait(copies.start(send, send_out), copies.start(near, near_out), copies.start(away, far_out))


def eight(mine, one, two, far):
    return [mine, one, two.at[0], two.at[1]] + [far.at[at] for at in range(4)]


def finish_input(idx, *refs, blocks):
    pieces, (out, logits, losses, day_held) = refs[:blocks], refs[blocks:]
    width = out.shape[0]
    size = pieces[0].shape[1]
    for turn, piece in enumerate(pieces):
        block = block_of(idx, turn, blocks)
        lanes = pl.ds(pl.multiple_of(block * size, LANES), size)
        values = piece[...].astype(F32)
        line = lambda at: values[width + at : width + at + 1, :]
        out[:, lanes] = values[0:width, :]
        logits[:, lanes] = line(0) + line(1) + line(2)
        day_held[block] = jnp.broadcast_to(line(3) + line(4) + line(5), day_held.shape[1:])
    days = day_held[0]
    for block in range(1, blocks):
        days += day_held[block]
    row = lax.broadcasted_iota(jnp.int32, losses.shape, 0)
    tile = jnp.zeros(losses.shape, F32)
    for at, value in enumerate(split3(days[0:1, 0:LANES])):
        tile = jnp.where(row == at, value, tile)
    losses[...] = jnp.where(lane_of(tile.shape) < LOSS, 0.0, pltpu.roll(tile, LOSS, 1))


def finish_tower(idx, *refs, depth):
    slices, (counts, out1, out2, rows_out, mean_out, lines, day_held) = eight(*refs[:4]), refs[4:]
    low = depth // LANES * LANES
    size = out2.shape[0]
    for offset, piece in zip(places(idx), slices):
        lines[rows_at(offset, SHARE), :] = piece[:, 0 : low + LANES].astype(F32)
        out2[rows_at(offset, SHARE), :] = piece[:, low + LANES :].astype(F32)
        tile = piece[0:16, low : low + LANES].astype(F32)
        day_held[lax.div(offset, SHARE)] = tile[0:1, :] + tile[1:2, :] + tile[2:3, :]
    turned = lines[...].T
    out1[...] = turned[0:depth, :]
    head = turned[depth + 3 : depth + 4, :]
    rows_out[0:1, :] = turned[depth : depth + 1, :]
    rows_out[1:2, :] = turned[depth + 1 : depth + 2, :]
    rows_out[2:3, 0:HALF] = turned[depth + 2 : depth + 3, 0:HALF] + head[:, HALF:]
    rows_out[2:3, HALF:] = turned[depth + 2 : depth + 3, HALF:] + head[:, 0:HALF]
    days = day_held[0]
    for at in range(1, day_held.shape[0]):
        days += day_held[at]
    days = days[:, LOSS : LOSS + DAYS]
    mean = days / jnp.maximum(counts[:, 0:DAYS].astype(F32), 1.0)
    mean_out[...] = jnp.sum(mean, axis=1, keepdims=True) / DAYS


def finish_cross(idx, *refs, blocks, base, more):
    slices, refs = eight(*refs[:4]), refs[4:]
    before, (out, bias_out, held, lines, sems) = refs[:more], refs[more:]
    count, width, depth = held.shape
    left = width - MAIN
    low = depth // LANES * LANES
    copies = Copies(sems)
    last = []
    if more:
        bias_out[count:, :] = before[1][...]
    for layer in range(count):
        rows = slice(SHARE * layer, SHARE * (layer + 1))
        for offset, piece in zip(places(idx), slices):
            held[layer, rows_at(offset, SHARE), :] = piece[rows, 0:depth].astype(F32)
            lines[rows_at(offset, SHARE), :] = piece[rows, low:].astype(F32)
        turned = lines[...].T
        bias_out[layer : layer + 1, 0:MAIN] = turned[depth - low : depth - low + 1, :]
        for group in range(-(-depth // MAIN)):
            rest = jnp.zeros((left, MAIN), F32)
            for block in range(blocks):
                at = REST + 16 * group + left * block
                rest = jnp.where(idx[0] == block, turned[at : at + left, :], rest)
            stop = min(depth, MAIN * (group + 1)) - MAIN * group
            held[layer, MAIN:width, MAIN * group : MAIN * group + stop] = rest[:, 0:stop]
        last.append(copies.start(held.at[layer], out.at[base + layer]))
        corner = jnp.broadcast_to(rest[:, stop : stop + 1], (left, LANES))
        ahead = lax.broadcasted_iota(jnp.int32, (left, LANES), 0) == lane_of((left, LANES))
        line = jnp.sum(jnp.where(ahead, corner, 0.0), axis=0, keepdims=True)
        bias_out[layer : layer + 1, MAIN:width] = line[:, 0:left]
    wait(*last)


def per_device(
    embedded,
    feature_ids,
    day_ids,
    labels,
    cross_weight,
    cross_bias,
    tower1,
    tower1_bias,
    tower2,
    tower2_bias,
    head_weight,
):
    blocks = lax.axis_size("mp")
    groups = lax.axis_size("dp")
    tokens, width = embedded.shape
    layers, _, depth = cross_weight.shape
    size, hidden = tower2.shape
    pad = -(-width // 16) * 16
    full = -(-(depth + 3) // LANES) * LANES
    part = tokens // blocks
    examples = tokens * groups
    flat = blocks * pad
    shape = jax.ShapeDtypeStruct
    vmem = pltpu.VMEM

    me = lax.axis_index("mp")
    group = lax.axis_index("dp")
    core, plane = group & 1, (group >> 1) & 3
    idx = jnp.stack([me, core, plane, group & 7]).astype(jnp.int32)
    swap = lambda bits: [(i, i ^ bits(i)) for i in range(groups)]
    first = swap(lambda i: 4 if i & 1 else 2)
    second = swap(lambda i: 2 if i & 1 else 4)
    pair = swap(lambda i: 1)
    others = [swap(lambda i, b=b: 1 << b) for b in range(3, groups.bit_length() - 1)]
    turn_by = lambda r: [(i, (i + r) % blocks) for i in range(blocks)]
    hop = lambda value, perm: lax.ppermute(value, "dp", perm)
    turns = lambda values: [
        lax.ppermute(value, "mp", turn_by(r + 1)) for r, value in enumerate(values)
    ]

    own_row = core * HALF + plane * SHARE
    cross_send = lax.dynamic_slice(cross_weight, (0, own_row, 0), (layers, SHARE, depth))
    cross_send = cross_send.reshape(layers * SHARE, depth)
    cross_turned = turns([cross_send] * (blocks - 1))
    vectors = jnp.stack([tower1_bias, head_weight, tower2_bias])
    wide = full + hidden
    groups_of = -(-depth // part)
    tower_send, tower_own, tally, *chunks = call(
        functools.partial(pack_rest, blocks=blocks),
        tuple(
            [
                shape((2 * SHARE, full), BF16),
                shape((size, full), BF16),
                shape(((blocks - 1) * SHARE, LANES), BF16),
            ]
            + [shape((16 * groups_of + width + 3, part), BF16)] * blocks
        ),
        [vmem((16, groups_of * part), F32)],
        [
            after(idx, cross_send),
            cross_weight,
            cross_bias,
            embedded.T,
            vectors,
            tower1,
            tower2,
            feature_ids.T,
            day_ids[None, :],
        ],
        mib=24,
        nbytes=2 << 20,
    )
    for perm in others:
        tally = tally + hop(tally, perm)
    tally = jnp.pad(tally.reshape(blocks - 1, SHARE, LANES), ((0, 0), (0, SHARE), (full - LANES, 0)))

    join = lambda *values: lax.optimization_barrier(values)
    cross_mine = jnp.stack(cross_turned)
    cross_mine, tower_send, *chunks = join(cross_mine, tower_send, *chunks)
    cross_one, cross_two = hop(cross_mine, first), hop(cross_mine, second)
    tower_turned = turns([tower_send] * (blocks - 1))
    cross_one, cross_two, *tower_turned = join(cross_one, cross_two, *tower_turned)

    pieces = [chunks[0]] + turns([after(chunk, tower_turned[0]) for chunk in chunks[1:]])
    tower_mine = jnp.stack(tower_turned) + tally
    both = jnp.concatenate([jnp.pad(cross_one, ((0, 0), (0, 0), (0, full - depth))), tower_mine], axis=1)
    tower_one, both = hop(tower_mine, first), hop(both, second)
    cross_near = jnp.stack([cross_mine, cross_one, cross_two])
    both, tower_one, cross_near, *pieces = join(both, tower_one, cross_near, *pieces)

    tower_three = hop(tower_one, second)
    both_far, tower_far, tower_next = hop(both, pair), hop(tower_mine, pair), hop(tower_one, pair)
    cross_far = hop(cross_near, pair)
    both_far, tower_far, tower_next, cross_far = join(both_far, tower_far, tower_next, cross_far)
    cross_slices = [cross_near, both, cross_far, both_far]

    z_all, x_all = call(
        functools.partial(cross_forward, blocks=blocks, layers=layers, width=width, pad=pad, depth=depth),
        (shape((layers, flat, part), F32), shape((layers + 1, full, part), BF16)),
        [
            vmem((layers, flat, depth), BF16),
            vmem((blocks, 16, depth), F32),
            vmem((16, depth), F32),
            vmem((blocks, pad, part), F32),
            vmem((blocks, pad, part), F32),
            vmem((full, part), F32),
        ],
        [idx, *pieces, cross_weight, *cross_slices],
        mib=28,
        flops=2 * layers * flat * full * part,
        nbytes=20 << 20,
    )
    tower_last = hop(after(tower_three, z_all), pair)
    tower_slices = [tower_mine, tower_one, both, tower_three, tower_far, tower_next, both_far, tower_last]
    x_far = hop(after(x_all, tower_last), pair)
    fields = feature_ids.shape[1]
    acts, far, head_col, dx3, lines, day_line, field_counts = call(
        functools.partial(
            tower_both, blocks=blocks, layers=layers, width=width, depth=depth, fields=fields, examples=examples
        ),
        (
            shape((3, hidden, part), BF16),
            shape((2 * hidden, part), BF16),
            shape((hidden, LANES), F32),
            shape((depth, part), F32),
            shape((2, part), F32),
            shape((1, BUCKETS), jnp.int32),
            shape((fields, BUCKETS), jnp.int32),
        ),
        [
            vmem((blocks, 3, part), F32),
            vmem((hidden, wide), BF16),
            vmem((hidden, part), F32),
            vmem((hidden, part), F32),
            vmem((hidden, part), F32),
            vmem((8, part), F32),
        ],
        [
            idx,
            labels[None, :],
            day_ids[None, :],
            *pieces,
            tower_own,
            tower2,
            *tower_slices,
            x_all,
        ],
        mib=28,
        flops=8 * hidden * full * part,
        nbytes=10 << 20,
    )
    far = hop(far, pair)

    def grads(kernel, keep, scratch, args, copies, flops):
        outs = keep, keep, (2,) + keep
        return call(
            kernel,
            tuple(shape(s, BF16) for s in outs),
            scratch + [vmem(s, BF16) for s in outs],
            args,
            mib=20,
            spec=HBM,
            copies=copies,
            flops=flops,
            nbytes=10 << 20,
        )

    tower_parts = grads(
        functools.partial(tower_grads, blocks=blocks, depth=depth, layers=layers),
        (blocks, SHARE, wide),
        [
            vmem((full, 2 * part), BF16),
            vmem((3, hidden, part), BF16),
            vmem((2 * hidden, part), BF16),
            vmem((hidden, LANES), F32),
            vmem((3, HALF * blocks, 2 * part), BF16),
            vmem((hidden, 2 * part), BF16),
        ],
        [idx, x_all, x_far, acts, far, head_col],
        8,
        4 * hidden * full * part,
    )
    tower_arrived = hop(tower_parts[2], first)
    *input_grads, dz, dz_rest, last_far, dz_far = call(
        functools.partial(cross_backward, blocks=blocks, layers=layers, width=width, pad=pad, depth=depth),
        tuple([shape((pad, part), BF16)] * blocks)
        + (
            shape((layers, flat, part), BF16),
            shape((layers, 16, part), BF16),
            shape((1, HALF * blocks + 16, part), BF16),
            shape((layers - 1, HALF * blocks + 16, part), BF16),
        ),
        [
            vmem((layers, flat, depth), BF16),
            vmem((blocks, width, part), F32),
            vmem((blocks, 16, depth), F32),
            vmem((16, depth), F32),
            vmem((depth, part), F32),
            vmem((blocks, pad, part), F32),
            vmem((blocks, pad, part), F32),
            vmem((16, part), F32),
        ],
        [
            after(idx, tower_parts[2]),
            lines,
            *pieces,
            cross_weight,
            *cross_slices,
            dx3,
            z_all,
        ],
        mib=34,
        flops=2 * layers * flat * full * part,
        nbytes=20 << 20,
    )
    last_far = hop(last_far, pair)
    dz_far = hop(dz_far, pair)

    def cross_parts_of(base, count, far, start):
        return grads(
            functools.partial(cross_grads, blocks=blocks, base=base, pad=pad, depth=depth),
            (blocks, count * SHARE, full),
            [
                vmem((count, full, 2 * part), BF16),
                vmem((count, flat, part), BF16),
                vmem((count, HALF * blocks + 16, part), BF16),
                vmem((count, 16, part), BF16),
                vmem((HALF * blocks, 2 * part), BF16),
                vmem((-(-depth // MAIN), LANES, 2 * part), BF16),
            ],
            [start, x_all, x_far, dz, dz_rest, far],
            5 * count + 3,
            2 * count * flat * full * part,
        )

    last_parts = cross_parts_of(layers - 1, 1, last_far, idx)
    cross_parts = cross_parts_of(0, layers - 1, dz_far, after(idx, last_parts[2]))

    down = lambda value: value.astype(BF16)
    up = lambda value: value.astype(F32)

    def near_sum(parts, arrived, last):
        return up(parts[0]) + up(arrived[0]) + up(last)

    def far_send(parts, arrived):
        return hop(down(up(parts[1]) + up(arrived[1])), second)

    def send_blocks(held):
        return turns([down(held[r]) for r in range(1, blocks)])

    def total_of(held, turned):
        held = held[0] + sum(up(value) for value in turned)
        for perm in others:
            held = held + hop(held, perm)
        return held

    def two_of(mine, one):
        return hop(jnp.stack([mine, one]), second)

    def far_of(mine, one, two):
        return hop(jnp.concatenate([jnp.stack([mine, one]), two]), pair)

    grad_pieces = [input_grads[0]] + turns(input_grads[1:])
    tower_arrived, last_send, grad_pieces[1] = join(tower_arrived, last_parts[2], grad_pieces[1])
    tower_second = far_send(tower_parts, tower_arrived)
    last_arrived = hop(last_send, first)
    tower_second, last_arrived, cross_send, *grad_pieces = join(
        tower_second, last_arrived, cross_parts[2], *grad_pieces
    )

    tower_held = near_sum(tower_parts, tower_arrived, tower_second)
    tower_turned = send_blocks(tower_held)
    last_second = far_send(last_parts, last_arrived)
    cross_arrived = hop(cross_send, first)
    input_out, logits_all, losses = call(
        functools.partial(finish_input, blocks=blocks),
        (shape((width, tokens), F32), shape((1, tokens), F32), shape((SHARE, LANES), F32)),
        [vmem((blocks, 8, part), F32)],
        [idx, *grad_pieces],
        mib=16,
        nbytes=2 << 20,
    )
    last_second, cross_arrived, losses, *tower_turned = join(last_second, cross_arrived, losses, *tower_turned)

    last_held = near_sum(last_parts, last_arrived, last_second)
    last_turned = send_blocks(last_held)
    cross_second = far_send(cross_parts, cross_arrived)
    tower_mine = down(total_of(tower_held, tower_turned) + jnp.pad(losses, ((0, 0), (full - LANES, hidden))))
    tower_one = hop(tower_mine, first)
    cross_second, tower_one, *last_turned = join(cross_second, tower_one, *last_turned)

    cross_held = near_sum(cross_parts, cross_arrived, cross_second)
    cross_turned = send_blocks(cross_held)
    tower_two = two_of(tower_mine, tower_one)
    last_mine = down(total_of(last_held, last_turned))
    last_one = hop(last_mine, first)
    tower_two, last_one, *cross_turned = join(tower_two, last_one, *cross_turned)

    cross_mine = down(total_of(cross_held, cross_turned))
    cross_one = hop(cross_mine, first)
    last_two = two_of(last_mine, last_one)
    tower_far = far_of(tower_mine, tower_one, tower_two)
    cross_one, last_two, tower_far = join(cross_one, last_two, tower_far)

    cross_two = two_of(cross_mine, cross_one)
    last_far = far_of(last_mine, last_one, last_two)
    tower_sums = [tower_mine, tower_one, tower_two, tower_far]
    last_sums = [last_mine, last_one, last_two, last_far]
    tower1_grad, tower2_grad, rows, mean = call(
        functools.partial(finish_tower, depth=depth),
        (shape((depth, size), F32), shape((size, hidden), F32), shape((3, size), F32), shape((1, 1), F32)),
        [vmem((size, full), F32), vmem((8, 1, LANES), F32)],
        [idx, *tower_sums, day_line],
        mib=16,
        nbytes=4 << 20,
    )
    def finish(sums, base, count, before):
        alias = {5: 0} if before else {}
        return call(
            functools.partial(finish_cross, blocks=blocks, base=base, more=len(before)),
            (shape((layers, width, depth), F32), shape((count + len(before) // 2, width), F32)),
            [vmem((count, width, depth), F32), vmem((MAIN, LANES), F32)],
            [idx, *sums] + [(value, spec) for value, spec in zip(before, (HBM, VMEM))],
            mib=16,
            out_spec=(HBM, VMEM),
            aliases=alias,
            copies=count,
            nbytes=4 << 20,
        )

    before = finish(last_sums, layers - 1, 1, ())
    cross_two, tower1_grad, before = join(cross_two, tower1_grad, before)
    cross_far = far_of(cross_mine, cross_one, cross_two)
    cross_grad, cross_bias_grad = finish([cross_mine, cross_one, cross_two, cross_far], 0, layers - 1, before)
    day_counts = day_line[0, :DAYS]
    return (
        mean[0, 0],
        logits_all[0],
        input_out.T,
        cross_grad,
        cross_bias_grad,
        tower1_grad,
        rows[0],
        tower2_grad,
        rows[1],
        rows[2],
        day_counts,
        field_counts,
    )


def solution(mesh):
    in_specs = (
        P("dp", "mp"),
        P("dp", None),
        P("dp"),
        P("dp"),
        P(None, "mp", None),
        P(None, "mp"),
        P(None, "mp"),
        P("mp"),
        P("mp", None),
        P("mp"),
        P("mp"),
    )
    out_specs = (
        P(),
        P("dp"),
        P("dp", "mp"),
        P(None, "mp", None),
        P(None, "mp"),
        P(None, "mp"),
        P("mp"),
        P("mp", None),
        P("mp"),
        P("mp"),
        P(),
        P(),
    )
    return jax.shard_map(
        per_device, mesh=mesh, in_specs=in_specs, out_specs=out_specs, check_vma=False
    )
```

```python
import functools

import jax
import jax.numpy as jnp
from jax import lax
from jax.experimental import pallas as pl
from jax.experimental.pallas import tpu as pltpu
from jax.sharding import PartitionSpec as P

DAYS = 24
BUCKETS = 128
BF16 = jnp.bfloat16
F32 = jnp.float32
MAIN = 256
SHARE = 32
HALF = MAIN // 2
LANES = 128
APART = 64
LOSS = 24
COUNT = 16
VMEM = pl.BlockSpec(memory_space=pltpu.VMEM)
SMEM = pl.BlockSpec(memory_space=pltpu.SMEM)
HBM = pl.BlockSpec(memory_space=pl.ANY)
FAR = pl.BlockSpec(memory_space=pltpu.HBM)
NT = (((1,), (1,)), ((), ()))
TN = (((0,), (0,)), ((), ()))
NN = (((1,), (0,)), ((), ()))


def gelu_parts(values):
    cdf_part = 0.5 * (1.0 + lax.erf(values * 0.7071067811865476))
    slope = cdf_part + values * jnp.exp(-0.5 * values * values) * 0.3989422804014327
    return (values * cdf_part, slope)


def dot(lhs, rhs, dims, precision=None):
    return lax.dot_general(lhs, rhs, dims, preferred_element_type=F32, precision=precision)


def call(kernel, outs, scratch, args, mib, spec=VMEM, copies=0, out_spec=None, aliases={}, flops=0, nbytes=0):
    arrays = [a[0] if isinstance(a, tuple) else a for a in args[1:]]
    specs = [a[1] if isinstance(a, tuple) else spec for a in args[1:]]
    if copies:
        scratch = scratch + [pltpu.SemaphoreType.DMA((copies,))]
    return pl.pallas_call(
        kernel,
        out_shape=outs,
        in_specs=[SMEM] + specs,
        out_specs=out_spec or jax.tree.map(lambda _: spec, outs),
        scratch_shapes=scratch,
        input_output_aliases=aliases,
        compiler_params=pltpu.CompilerParams(vmem_limit_bytes=mib << 20),
        cost_estimate=pl.CostEstimate(flops=flops, bytes_accessed=nbytes, transcendentals=0),
    )(args[0], *arrays)


class Copies:
    def __init__(self, sems):
        self.sems, self.count = sems, 0

    def start(self, source, target):
        copy = pltpu.make_async_copy(source, target, self.sems.at[self.count])
        self.count += 1
        copy.start()
        return copy


def wait(*copies):
    for copy in copies:
        copy.wait()


def after(value, *others):
    return lax.optimization_barrier((value,) + others)[0]


def places(idx):
    core, plane = idx[1], idx[2]
    first, second = core + 1, 2 - core
    mine = [plane, plane ^ first, plane ^ second, plane ^ 3]
    theirs = [plane, plane ^ second, plane ^ first, plane ^ 3]
    return [core * HALF + SHARE * q for q in mine] + [(1 - core) * HALF + SHARE * q for q in theirs]


def relative(idx):
    core, plane = idx[1], idx[2]
    first, second = core + 1, 2 - core
    return [plane, plane ^ second, plane ^ first, plane ^ 3]


def block_of(idx, turn, blocks):
    return lax.rem(idx[0] - turn + blocks, blocks)


def block_ahead(idx, turn, blocks):
    return lax.rem(idx[0] + turn, blocks)


def rows_at(offset, size, unit=16):
    return pl.ds(pl.multiple_of(offset, unit), size)


def split3(line):
    high = line.astype(BF16).astype(F32)
    middle = (line - high).astype(BF16).astype(F32)
    return high, middle, line - high - middle


def lane_of(shape):
    return lax.broadcasted_iota(jnp.int32, shape, 1)


def pack_rest(idx, weight, bias, inputs, vectors, weight1, weight2, ids, days, *refs, blocks):
    out, own1, tally = refs[:3]
    chunks, (lines,) = refs[3 : 3 + blocks], refs[3 + blocks :]
    layers, width, depth = weight.shape
    size = weight2.shape[0]
    left = width - MAIN
    part = chunks[0].shape[1]
    full = own1.shape[1]
    own_row = idx[1] * HALF + idx[2] * SHARE

    lines[...] = jnp.zeros_like(lines)
    for layer in range(layers):
        lines[left * layer : left * (layer + 1), 0:depth] = weight[layer, MAIN:width, :].astype(F32)
        at = left * layers + layer
        lines[at : at + 1, 0:width] = bias[layer : layer + 1, :].astype(F32)
    rest = [lines[:, at : at + part].astype(BF16) for at in range(0, lines.shape[1], part)]

    own1[:, 0:depth] = weight1[...].T
    own1[:, depth:] = jnp.zeros((size, full - depth), BF16)
    out[:, 0:full] = own1[rows_at(own_row, SHARE), :]
    out[:, full:] = weight2[rows_at(own_row, SHARE), :]

    first = 16 * len(rest)
    for turn in range(blocks):
        lanes = pl.ds(pl.multiple_of(block_ahead(idx, turn, blocks) * part, LANES), part)
        for at, value in enumerate(rest):
            chunks[turn][16 * at : 16 * (at + 1), :] = value
        chunks[turn][first : first + width, :] = inputs[:, lanes]
        chunks[turn][first + width : first + width + 3, :] = vectors[...]

    fields, tokens = ids.shape
    bucket = lax.broadcasted_iota(jnp.int32, (BUCKETS, tokens), 0)
    lane = lane_of((BUCKETS, LANES))
    tile = jnp.zeros((BUCKETS, LANES), F32)
    for field in range(fields + 1):
        line = ids[field : field + 1, :] if field < fields else days[...]
        hits = jnp.sum((bucket == line).astype(F32), axis=1, keepdims=True)
        high = jnp.floor(hits * (1.0 / 256.0))
        tile = jnp.where(lane == COUNT + field, high, tile)
        tile = jnp.where(lane == COUNT + fields + 1 + field, hits - 256.0 * high, tile)
    half = BUCKETS // 2
    tile = tile[0:half, :] + pltpu.roll(tile[half:, :], 2 * (fields + 1), 1)
    tally[0:half, :] = tile.astype(BF16)
    tally[half:, :] = jnp.zeros((tally.shape[0] - half, LANES), BF16)


def cross_eight(refs):
    near, last, near_far, last_far = refs
    return [near.at[at] for at in range(3)] + [last] + [near_far.at[at] for at in range(3)] + [last_far]


def place_cross(idx, weight, own, slices, blocks, layer, pad):
    layers, depth = weight.shape[0], weight.shape[2]
    low = depth // LANES * LANES
    weight[layer, rows_at(idx[0] * pad, MAIN), :] = own[layer, 0:MAIN, :]
    tail = layers * low + (depth - low) * layer
    for turn in range(1, blocks):
        base = block_of(idx, turn, blocks) * pad
        for offset, piece in zip(places(idx), slices):
            rows = rows_at(base + offset, SHARE)
            weight[layer, rows, 0:low] = piece[turn - 1, :, low * layer : low * (layer + 1)]
            weight[layer, rows, low:] = piece[turn - 1, :, tail : tail + depth - low]


def place_rest(idx, weight, pieces, lines, tail, layers, left, pad):
    blocks = len(pieces)
    depth = weight.shape[2]
    part = pieces[0].shape[1]
    tail[...] = jnp.zeros_like(tail)
    for turn, piece in enumerate(pieces):
        for group in range(-(-depth // part)):
            stop = min(depth, part * (group + 1))
            lines[block_of(idx, turn, blocks), :, part * group : stop] = piece[
                16 * group : 16 * (group + 1), 0 : stop - part * group
            ].astype(F32)
    for block in range(blocks):
        for layer in range(layers):
            tail[0:left, :] = lines[block, left * layer : left * (layer + 1), :]
            at = pad * block + MAIN
            weight[layer, at : at + 16, :] = tail[...].astype(BF16)


def cross_forward(idx, *refs, blocks, layers, width, pad, depth):
    pieces, refs = refs[:blocks], refs[blocks:]
    own, refs = refs[0], refs[1:]
    slices, refs = cross_eight(refs[:4]), refs[4:]
    z_out, x_out, weight, lines, tail, start, state, nat = refs
    left = width - MAIN
    place_rest(idx, weight, pieces, lines, tail, layers, left, pad)
    at = 16 * -(-depth // pieces[0].shape[1])
    bias = [lines[block, :, 0:384].T for block in range(blocks)]
    for turn, piece in enumerate(pieces):
        block = block_of(idx, turn, blocks)
        start[block, 0:width, :] = piece[at : at + width, :].astype(F32)
        start[block, width:, :] = jnp.zeros((pad - width, piece.shape[1]), F32)
    full = nat.shape[0]
    ones = lax.broadcasted_iota(jnp.int32, (full - depth, nat.shape[1]), 0) == 0
    nat[depth:full, :] = ones.astype(F32)
    for block in range(blocks):
        nat[width * block : width * (block + 1), :] = start[block, 0:width, :]
    for layer in range(layers):
        x_out[layer] = nat[...].astype(BF16)
        place_cross(idx, weight, own, slices, blocks, layer, pad)
        at = left * layers + layer
        for block in range(blocks):
            rows = slice(pad * block, pad * (block + 1))
            value = dot(weight[layer, rows, :], x_out[layer, 0:depth, :], NN) + bias[block][0:pad, at : at + 1]
            z_out[layer, rows, :] = value
            before = start[block] if layer == 0 else state[block]
            value = start[block] * value + before
            state[block] = value
            nat[width * block : width * (block + 1), :] = value[0:width, :]
    x_out[layers] = nat[...].astype(BF16)


def tower_both(idx, *refs, blocks, layers, width, depth, fields, examples):
    (labels, day_ids), refs = refs[:2], refs[2:]
    pieces, refs = refs[:blocks], refs[blocks:]
    (own1, own2), refs = refs[:2], refs[2:]
    slices, refs = refs[:8], refs[8:]
    x_all, acts, far, heads, flow, lines_out, day_out, field_out = refs[:8]
    inputs, tower, slope1, act2, headed, vectors = refs[8:]
    hidden = tower.shape[0]
    full = x_all.shape[1]
    size = hidden // blocks
    part = x_all.shape[2]
    low = depth // LANES * LANES
    at = 16 * -(-depth // part) + width
    for turn, piece in enumerate(pieces):
        inputs[block_of(idx, turn, blocks)] = piece[at : at + 3, :].astype(F32)
    base = idx[0] * size
    tower[rows_at(base, size), 0:full] = own1[...]
    tower[rows_at(base, size), full:] = own2[...]
    for turn in range(1, blocks):
        base = block_of(idx, turn, blocks) * size
        for offset, piece in zip(places(idx), slices):
            rows = rows_at(base + offset, SHARE)
            tower[rows, :] = piece[turn - 1, :, piece.shape[2] - tower.shape[1] :]
    parts = [slice(size * block, size * (block + 1)) for block in range(blocks)]
    columns = []
    for block in range(blocks):
        vectors[0:3, :] = inputs[block]
        columns.append(vectors[...].T)
    for rows, column in zip(parts, columns):
        act, slope = gelu_parts(dot(tower[rows, 0:depth], x_all[layers, 0:depth, :], NN) + column[:, 0:1])
        acts[0, rows, :] = act.astype(BF16)
        slope1[rows, :] = slope
    logits = jnp.zeros((1, part), F32)
    for rows, column in zip(parts, columns):
        act, slope = gelu_parts(dot(tower[:, full + rows.start : full + rows.stop], acts[0], TN) + column[:, 2:3])
        act2[rows, :] = act
        headed[rows, :] = column[:, 1:2] * slope
        logits += jnp.sum(act * column[:, 1:2], axis=0, keepdims=True)

    half = BUCKETS // 2
    tally = jnp.zeros((half, LANES), F32)
    for piece in slices:
        at = piece.shape[2] - tower.shape[1] + low
        tally += piece[0 : half // SHARE, :, at : at + LANES].astype(F32).reshape(half, LANES)
    count = jnp.concatenate([tally, pltpu.roll(tally, LANES - 2 * (fields + 1), 1)], axis=0)
    high = count[:, COUNT : COUNT + fields + 1]
    count = 256.0 * high + count[:, COUNT + fields + 1 : COUNT + 2 * (fields + 1)]
    days = count[0:32, fields : fields + 1]
    padded = jnp.concatenate([count, jnp.zeros((BUCKETS, LANES - fields - 1), F32)], axis=1).T
    field_out[...] = padded[0:fields, :].astype(jnp.int32)
    day_out[...] = padded[fields : fields + 1, :].astype(jnp.int32)

    mine = pl.ds(pl.multiple_of(idx[0] * part, LANES), part)
    lab = labels[:, mine].astype(F32)
    table = (lax.broadcasted_iota(jnp.int32, (32, part), 0) == day_ids[:, mine]).astype(F32)
    share = examples / (DAYS * jnp.maximum(days, 1.0))
    weights = jnp.sum(table * share, axis=0, keepdims=True)
    decay = jnp.exp(-jnp.abs(logits))
    loss = jnp.maximum(logits, 0.0) + jnp.log1p(decay) - lab * logits
    sigmoid = jnp.where(logits >= 0.0, 1.0, decay) / (1.0 + decay)
    dl = weights * (sigmoid - lab)
    losses = dot(jnp.broadcast_to(loss, (8, part)), table, NT, lax.Precision.HIGHEST)[0:1, :]
    lines_out[0:1, :] = logits
    lines_out[1:2, :] = jnp.zeros_like(logits)
    lines_out[1:2, 0 : losses.shape[1]] = losses

    acts[1] = (dl * headed[...]).astype(BF16)
    far[0:hidden, :] = acts[1]
    for rows in parts:
        acts[2, rows, :] = (dot(tower[rows, full:], acts[1], NN) * slope1[rows, :]).astype(BF16)
    for block in range(blocks):
        rows = rows_at(block * size + (1 - idx[1]) * HALF, HALF)
        at = hidden + HALF * block
        far[at : at + HALF, :] = acts[0, rows, :]
        at = hidden + HALF * (block + blocks)
        far[at : at + HALF, :] = acts[2, rows, :]
    for rows in parts:
        heads[rows, :] = jnp.broadcast_to(jnp.sum(act2[rows, :] * dl, axis=1, keepdims=True), (size, LANES))
    flow[...] = dot(tower[:, 0:depth], acts[2], TN)


def cross_backward(idx, *refs, blocks, layers, width, pad, depth):
    extra_lines, refs = refs[0], refs[1:]
    pieces, refs = refs[:blocks], refs[blocks:]
    own, refs = refs[0], refs[1:]
    slices, refs = cross_eight(refs[:4]), refs[4:]
    (dx3, z_all), refs = refs[:2], refs[2:]
    eg_out, refs = refs[:blocks], refs[blocks:]
    dz_out, rest_out, dz_far_last, dz_far_out = refs[:4]
    weight, inputs, lines, tail, flow, padded, total, rest = refs[4:]
    left = width - MAIN
    place_rest(idx, weight, pieces, lines, tail, layers, left, pad)
    at = 16 * -(-depth // pieces[0].shape[1])
    for turn, piece in enumerate(pieces):
        inputs[block_of(idx, turn, blocks)] = piece[at : at + width, :].astype(F32)
    padded[...] = jnp.zeros_like(padded)
    rest[...] = jnp.zeros_like(rest)
    for layer in reversed(range(layers)):
        source = dx3 if layer == layers - 1 else flow
        for block in range(blocks):
            rows = slice(pad * block, pad * (block + 1))
            dx = source[width * block : width * (block + 1), :]
            padded[block, 0:width, :] = dx
            dx = padded[block, 0:width, :]
            dz = dx * inputs[block]
            term = dx * z_all[layer, pad * block : pad * block + width, :]
            total[block, 0:width, :] = term if layer == layers - 1 else total[block, 0:width, :] + term
            rest[left * block : left * (block + 1), :] = dz[MAIN:width, :]
            padded[block, 0:width, :] = dz
            dz_out[layer, rows, :] = padded[block].astype(BF16)
        rest_out[layer] = rest[...].astype(BF16)
        far = dz_far_last.at[0] if layer == layers - 1 else dz_far_out.at[layer]
        far[HALF * blocks :, :] = rest[...].astype(BF16)
        for block in range(blocks):
            rows = rows_at(pad * block + (1 - idx[1]) * HALF, HALF)
            far[HALF * block : HALF * (block + 1), :] = dz_out[layer, rows, :]
        place_cross(idx, weight, own, slices, blocks, layer, pad)
        flow[...] = source[...] + dot(weight[layer], dz_out[layer], TN)
    extras = split3(extra_lines[0:1, :]) + split3(extra_lines[1:2, :])
    for block in range(blocks):
        total[block, 0:width, :] += flow[width * block : width * (block + 1), :]
        total[block, width:, :] = jnp.zeros((pad - width, flow.shape[1]), F32)
        for at, extra in enumerate(extras):
            total[block, width + at : width + at + 1, :] = extra
    for turn in range(blocks):
        eg_out[turn][...] = total[block_ahead(idx, turn, blocks)].astype(BF16)


def tower_grads(idx, x_all, x_far, acts, far, head, near_out, far_out, send_out, *refs, blocks, depth, layers):
    x_cat, acts_in, far_in, heads, lhs, d_cat, near, away, send, sems = refs
    hidden = acts.shape[1]
    size = hidden // blocks
    part = acts.shape[2]
    low = depth // LANES * LANES
    bias = depth - low
    copies = Copies(sems)
    first = [
        copies.start(acts, acts_in),
        copies.start(far, far_in),
        copies.start(x_all.at[layers], x_cat.at[:, 0:part]),
        copies.start(x_far.at[layers], x_cat.at[:, part : 2 * part]),
        copies.start(head, heads),
    ]
    wait(*first)
    lane = lane_of((SHARE, LANES))
    pick = (lax.broadcasted_iota(jnp.int32, (LANES, 2 * part), 0) == bias + 1).astype(BF16)
    order = [(where, slot) for where in range(4) for slot in range(blocks)]
    shares = relative(idx)
    d_cat[:, 0:part] = acts_in[1]
    d_cat[:, part:] = far_in[0:hidden, :]
    scale = []
    for at, (where, slot) in enumerate(order):
        block = block_ahead(idx, slot, blocks)
        rows = rows_at(block * size + idx[1] * HALF + SHARE * shares[where], SHARE)
        other = rows_at(block * size + (1 - idx[1]) * HALF + SHARE * shares[where], SHARE)
        lines = rows_at(hidden + HALF * block + SHARE * shares[where], SHARE)
        after_it = rows_at(hidden + HALF * (block + blocks) + SHARE * shares[where], SHARE)
        here = slice(SHARE * at, SHARE * (at + 1))
        lhs[0, here, 0:part] = acts_in[2, rows, :]
        lhs[0, here, part:] = far_in[after_it, :]
        lhs[1, here, 0:part] = acts_in[0, rows, :]
        lhs[1, here, part:] = far_in[lines, :]
        lhs[2, here, 0:part] = acts_in[1, rows, :]
        lhs[2, here, part:] = far_in[rows, :]
        scale.append(
            jnp.where(lane == bias + 2, heads[rows, :], 0.0) + jnp.where(lane == bias + 3, heads[other, :], 0.0)
        )
    extra = dot(lhs[2], pick, NT)
    wide = dot(lhs[0], x_cat[...], NT)
    deep = dot(lhs[1], d_cat[...], NT)
    for at, (where, slot) in enumerate(order):
        target = (near, away, send.at[0], send.at[1])[where].at[slot]
        here = slice(SHARE * at, SHARE * (at + 1))
        target[:, 0:low] = wide[here, 0:low].astype(BF16)
        target[:, low : low + LANES] = (wide[here, low:] + extra[here, :] + scale[at]).astype(BF16)
        target[:, low + LANES :] = deep[here, :].astype(BF16)
    wait(copies.start(send, send_out), copies.start(near, near_out), copies.start(away, far_out))


def cross_grads(idx, x_all, x_far, dz, rest, dz_far, near_out, far_out, send_out, *refs, blocks, base, pad, depth):
    x_cat, dz_in, far_in, rest_in, lhs, few, extra, tiles, near, away, send, sems = refs
    part = dz.shape[2]
    low = depth // LANES * LANES
    groups = -(-depth // MAIN)
    count = dz_far.shape[0]
    left = rest_in.shape[1] // blocks
    copies = Copies(sems)
    first = []
    for layer in reversed(range(count)):
        first.append(
            [
                copies.start(dz.at[base + layer], dz_in.at[layer]),
                copies.start(dz_far.at[layer], far_in.at[layer]),
                copies.start(rest.at[base + layer], rest_in.at[layer]),
                copies.start(x_all.at[base + layer], x_cat.at[layer, :, 0:part]),
                copies.start(x_far.at[base + layer], x_cat.at[layer, :, part : 2 * part]),
            ]
        )
    few[...] = jnp.zeros_like(few)
    order = [(where, slot) for where in range(4) for slot in range(blocks)]
    shares = relative(idx)
    lane = lane_of((HALF, LANES))
    bias = depth - low
    span = left * groups
    for layer, started in zip(reversed(range(count)), first):
        wait(*started)
        value = jnp.zeros((HALF, LANES), F32)
        near_rest = rest_in[layer].astype(F32)
        far_rest = far_in[layer, HALF * blocks :, :].astype(F32)
        for group in range(groups):
            for block in range(blocks):
                lines = slice(span * block + left * group, span * block + left * (group + 1))
                few[group, lines, 0:part] = near_rest[left * block : left * (block + 1), :]
                few[group, lines, part:] = far_rest[left * block : left * (block + 1), :]
            if MAIN * (group + 1) <= depth:
                rows = rows_at(MAIN * group + idx[1] * HALF, HALF)
            else:
                rows = slice(MAIN * group, MAIN * group + HALF)
            value += dot(x_cat[layer, rows, :], few[group].astype(BF16), NT)
        inside = (lane > bias) & (lane <= bias + span)
        for block in range(blocks):
            extra[block] = jnp.where(inside, pltpu.roll(value, (bias + 1 - span * block) % LANES, 1), 0.0)
        for at, (where, slot) in enumerate(order):
            block = block_ahead(idx, slot, blocks)
            rows = rows_at(pad * block + idx[1] * HALF + SHARE * shares[where], SHARE)
            lines = rows_at(HALF * block + SHARE * shares[where], SHARE)
            here = slice(SHARE * at, SHARE * (at + 1))
            lhs[here, 0:part] = dz_in[layer, rows, :]
            lhs[here, part:] = far_in[layer, lines, :]
        grad = dot(lhs[...], x_cat[layer], NT)
        for at, (where, slot) in enumerate(order):
            target = (near, away, send.at[0], send.at[1])[where].at[slot]
            here = slice(SHARE * at, SHARE * (at + 1))
            target[:, low * layer : low * (layer + 1)] = grad[here, 0:low].astype(BF16)
            tile = grad[here, low:] + extra[block_ahead(idx, slot, blocks), rows_at(SHARE * shares[where], SHARE), :]
            if layer < count - 1:
                tile = tiles[here, :] + (pltpu.roll(tile, APART * layer, 1) if layer else tile)
            elif layer:
                tile = pltpu.roll(tile, APART * layer, 1)
            if layer:
                tiles[here, :] = tile
            else:
                target[:, low * count :] = tile.astype(BF16)
    wait(copies.start(send, send_out), copies.start(near, near_out), copies.start(away, far_out))


def eight(mine, one, two, far):
    return [mine, one, two.at[0], two.at[1]] + [far.at[at] for at in range(4)]


def finish_input(idx, *refs, blocks):
    pieces, (out, logits, losses, day_held) = refs[:blocks], refs[blocks:]
    width = out.shape[0]
    size = pieces[0].shape[1]
    for turn, piece in enumerate(pieces):
        block = block_of(idx, turn, blocks)
        lanes = pl.ds(pl.multiple_of(block * size, LANES), size)
        values = piece[...].astype(F32)
        line = lambda at: values[width + at : width + at + 1, :]
        out[:, lanes] = values[0:width, :]
        logits[:, lanes] = line(0) + line(1) + line(2)
        day_held[block] = jnp.broadcast_to(line(3) + line(4) + line(5), day_held.shape[1:])
    days = day_held[0]
    for block in range(1, blocks):
        days += day_held[block]
    row = lax.broadcasted_iota(jnp.int32, losses.shape, 0)
    tile = jnp.zeros(losses.shape, F32)
    for at, value in enumerate(split3(days[0:1, 0:LANES])):
        tile = jnp.where(row == at, value, tile)
    losses[...] = jnp.where(lane_of(tile.shape) < LOSS, 0.0, pltpu.roll(tile, LOSS, 1))


def finish_tower(idx, *refs, depth):
    slices, (counts, out1, out2, rows_out, mean_out, lines, day_held) = eight(*refs[:4]), refs[4:]
    low = depth // LANES * LANES
    size = out2.shape[0]
    for offset, piece in zip(places(idx), slices):
        lines[rows_at(offset, SHARE), :] = piece[:, 0 : low + LANES].astype(F32)
        out2[rows_at(offset, SHARE), :] = piece[:, low + LANES :].astype(F32)
        tile = piece[0:16, low : low + LANES].astype(F32)
        day_held[lax.div(offset, SHARE)] = tile[0:1, :] + tile[1:2, :] + tile[2:3, :]
    turned = lines[...].T
    out1[...] = turned[0:depth, :]
    head = turned[depth + 3 : depth + 4, :]
    rows_out[0:1, :] = turned[depth : depth + 1, :]
    rows_out[1:2, :] = turned[depth + 1 : depth + 2, :]
    rows_out[2:3, 0:HALF] = turned[depth + 2 : depth + 3, 0:HALF] + head[:, HALF:]
    rows_out[2:3, HALF:] = turned[depth + 2 : depth + 3, HALF:] + head[:, 0:HALF]
    days = day_held[0]
    for at in range(1, day_held.shape[0]):
        days += day_held[at]
    days = days[:, LOSS : LOSS + DAYS]
    mean = days / jnp.maximum(counts[:, 0:DAYS].astype(F32), 1.0)
    mean_out[...] = jnp.sum(mean, axis=1, keepdims=True) / DAYS


def finish_cross(idx, *refs, blocks, base, more):
    slices, refs = eight(*refs[:4]), refs[4:]
    before, (out, bias_out, held, lines, sems) = refs[:more], refs[more:]
    count, width, depth = held.shape
    left = width - MAIN
    low = depth // LANES * LANES
    copies = Copies(sems)
    last = []
    if more:
        bias_out[count:, :] = before[1][...]
    for offset, piece in zip(places(idx), slices):
        lines[rows_at(offset, SHARE), :] = piece[:, low * count :].astype(F32)
    turned = lines[...].T
    for layer in range(count):
        for offset, piece in zip(places(idx), slices):
            rows = rows_at(offset, SHARE)
            held[layer, rows, 0:low] = piece[:, low * layer : low * (layer + 1)].astype(F32)
        held[layer, 0:MAIN, low:] = lines[:, APART * layer : APART * layer + depth - low]
        bias = APART * layer + depth - low
        bias_out[layer : layer + 1, 0:MAIN] = turned[bias : bias + 1, :]
        for group in range(-(-depth // MAIN)):
            rest = turned[bias + 1 + left * group : bias + 1 + left * (group + 1), :]
            stop = min(depth, MAIN * (group + 1)) - MAIN * group
            held[layer, MAIN:width, MAIN * group : MAIN * group + stop] = rest[:, 0:stop]
        last.append(copies.start(held.at[layer], out.at[base + layer]))
        corner = jnp.broadcast_to(rest[:, stop : stop + 1], (left, LANES))
        ahead = lax.broadcasted_iota(jnp.int32, (left, LANES), 0) == lane_of((left, LANES))
        line = jnp.sum(jnp.where(ahead, corner, 0.0), axis=0, keepdims=True)
        bias_out[layer : layer + 1, MAIN:width] = line[:, 0:left]
    wait(*last)


def per_device(
    embedded,
    feature_ids,
    day_ids,
    labels,
    cross_weight,
    cross_bias,
    tower1,
    tower1_bias,
    tower2,
    tower2_bias,
    head_weight,
):
    blocks = lax.axis_size("mp")
    groups = lax.axis_size("dp")
    tokens, width = embedded.shape
    layers, _, depth = cross_weight.shape
    size, hidden = tower2.shape
    pad = -(-width // 16) * 16
    full = -(-(depth + 3) // LANES) * LANES
    part = tokens // blocks
    examples = tokens * groups
    flat = blocks * pad
    shape = jax.ShapeDtypeStruct
    vmem = pltpu.VMEM

    me = lax.axis_index("mp")
    group = lax.axis_index("dp")
    core, plane = group & 1, (group >> 1) & 3
    idx = jnp.stack([me, core, plane, group & 7]).astype(jnp.int32)
    swap = lambda bits: [(i, i ^ bits(i)) for i in range(groups)]
    first = swap(lambda i: 4 if i & 1 else 2)
    second = swap(lambda i: 2 if i & 1 else 4)
    pair = swap(lambda i: 1)
    others = [swap(lambda i, b=b: 1 << b) for b in range(3, groups.bit_length() - 1)]
    turn_by = lambda r: [(i, (i + r) % blocks) for i in range(blocks)]
    hop = lambda value, perm: lax.ppermute(value, "dp", perm)
    turns = lambda values: [
        lax.ppermute(value, "mp", turn_by(r + 1)) for r, value in enumerate(values)
    ]

    own_row = core * HALF + plane * SHARE
    cross_send = lax.dynamic_slice(cross_weight, (0, own_row, 0), (layers, SHARE, depth))
    low = depth // LANES * LANES
    fill = jnp.zeros((SHARE, LANES - layers * (depth - low)), BF16)
    cross_send = jnp.concatenate([rows[:, :low] for rows in cross_send] + [rows[:, low:] for rows in cross_send] + [fill], axis=1)
    cross_turned = turns([cross_send] * (blocks - 1))
    vectors = jnp.stack([tower1_bias, head_weight, tower2_bias])
    wide = full + hidden
    groups_of = -(-depth // part)
    tower_send, tower_own, tally, *chunks = call(
        functools.partial(pack_rest, blocks=blocks),
        tuple(
            [
                shape((SHARE, wide), BF16),
                shape((size, full), BF16),
                shape(((blocks - 1) * SHARE, LANES), BF16),
            ]
            + [shape((16 * groups_of + width + 3, part), BF16)] * blocks
        ),
        [vmem((16, groups_of * part), F32)],
        [
            after(idx, cross_send),
            cross_weight,
            cross_bias,
            embedded.T,
            vectors,
            tower1,
            tower2,
            feature_ids.T,
            day_ids[None, :],
        ],
        mib=24,
        nbytes=2 << 20,
    )
    for perm in others:
        tally = tally + hop(tally, perm)
    tally = jnp.pad(tally.reshape(blocks - 1, SHARE, LANES), ((0, 0), (0, 0), (full - LANES, hidden)))

    join = lambda *values: lax.optimization_barrier(values)
    cross_mine = jnp.stack(cross_turned)
    cross_mine, tower_send, *chunks = join(cross_mine, tower_send, *chunks)
    cross_one, cross_two = hop(cross_mine, first), hop(cross_mine, second)
    tower_turned = turns([tower_send] * (blocks - 1))
    cross_one, cross_two, *tower_turned = join(cross_one, cross_two, *tower_turned)

    pieces = [chunks[0]] + turns([after(chunk, tower_turned[0]) for chunk in chunks[1:]])
    tower_mine = jnp.stack(tower_turned) + tally
    both = jnp.concatenate([cross_one, tower_mine], axis=2)
    tower_one, both = hop(tower_mine, first), hop(both, second)
    cross_near = jnp.stack([cross_mine, cross_one, cross_two])
    both, tower_one, cross_near, *pieces = join(both, tower_one, cross_near, *pieces)

    tower_three = hop(tower_one, second)
    both_far, tower_far, tower_next = hop(both, pair), hop(tower_mine, pair), hop(tower_one, pair)
    cross_far = hop(cross_near, pair)
    both_far, tower_far, tower_next, cross_far = join(both_far, tower_far, tower_next, cross_far)
    cross_slices = [cross_near, both, cross_far, both_far]

    z_all, x_all = call(
        functools.partial(cross_forward, blocks=blocks, layers=layers, width=width, pad=pad, depth=depth),
        (shape((layers, flat, part), F32), shape((layers + 1, full, part), BF16)),
        [
            vmem((layers, flat, depth), BF16),
            vmem((blocks, 16, depth), F32),
            vmem((16, depth), F32),
            vmem((blocks, pad, part), F32),
            vmem((blocks, pad, part), F32),
            vmem((full, part), F32),
        ],
        [idx, *pieces, cross_weight, *cross_slices],
        mib=28,
        flops=2 * layers * flat * full * part,
        nbytes=20 << 20,
    )
    tower_last = hop(after(tower_three, z_all), pair)
    tower_slices = [tower_mine, tower_one, both, tower_three, tower_far, tower_next, both_far, tower_last]
    x_far = hop(after(x_all, tower_last), pair)
    fields = feature_ids.shape[1]
    acts, far, head_col, dx3, lines, day_line, field_counts = call(
        functools.partial(
            tower_both, blocks=blocks, layers=layers, width=width, depth=depth, fields=fields, examples=examples
        ),
        (
            shape((3, hidden, part), BF16),
            shape((2 * hidden, part), BF16),
            shape((hidden, LANES), F32),
            shape((depth, part), F32),
            shape((2, part), F32),
            shape((1, BUCKETS), jnp.int32),
            shape((fields, BUCKETS), jnp.int32),
        ),
        [
            vmem((blocks, 3, part), F32),
            vmem((hidden, wide), BF16),
            vmem((hidden, part), F32),
            vmem((hidden, part), F32),
            vmem((hidden, part), F32),
            vmem((8, part), F32),
        ],
        [
            idx,
            labels[None, :],
            day_ids[None, :],
            *pieces,
            tower_own,
            tower2,
            *tower_slices,
            x_all,
        ],
        mib=28,
        flops=8 * hidden * full * part,
        nbytes=10 << 20,
    )
    far = hop(far, pair)

    def grads(kernel, keep, scratch, args, copies, flops):
        outs = keep, keep, (2,) + keep
        return call(
            kernel,
            tuple(shape(s, BF16) for s in outs),
            scratch + [vmem(s, BF16) for s in outs],
            args,
            mib=20,
            spec=HBM,
            copies=copies,
            flops=flops,
            nbytes=10 << 20,
        )

    tower_parts = grads(
        functools.partial(tower_grads, blocks=blocks, depth=depth, layers=layers),
        (blocks, SHARE, wide),
        [
            vmem((full, 2 * part), BF16),
            vmem((3, hidden, part), BF16),
            vmem((2 * hidden, part), BF16),
            vmem((hidden, LANES), F32),
            vmem((3, HALF * blocks, 2 * part), BF16),
            vmem((hidden, 2 * part), BF16),
        ],
        [idx, x_all, x_far, acts, far, head_col],
        8,
        4 * hidden * full * part,
    )
    tower_arrived = hop(tower_parts[2], first)
    *input_grads, dz, dz_rest, last_far, dz_far = call(
        functools.partial(cross_backward, blocks=blocks, layers=layers, width=width, pad=pad, depth=depth),
        tuple([shape((pad, part), BF16)] * blocks)
        + (
            shape((layers, flat, part), BF16),
            shape((layers, 16, part), BF16),
            shape((1, HALF * blocks + 16, part), BF16),
            shape((layers - 1, HALF * blocks + 16, part), BF16),
        ),
        [
            vmem((layers, flat, depth), BF16),
            vmem((blocks, width, part), F32),
            vmem((blocks, 16, depth), F32),
            vmem((16, depth), F32),
            vmem((depth, part), F32),
            vmem((blocks, pad, part), F32),
            vmem((blocks, pad, part), F32),
            vmem((16, part), F32),
        ],
        [
            after(idx, tower_parts[2]),
            lines,
            *pieces,
            cross_weight,
            *cross_slices,
            dx3,
            z_all,
        ],
        mib=34,
        flops=2 * layers * flat * full * part,
        nbytes=20 << 20,
    )
    last_far = hop(last_far, pair)
    dz_far = hop(dz_far, pair)

    def cross_parts_of(base, count, far, start):
        return grads(
            functools.partial(cross_grads, blocks=blocks, base=base, pad=pad, depth=depth),
            (blocks, SHARE, count * low + LANES),
            [
                vmem((count, full, 2 * part), BF16),
                vmem((count, flat, part), BF16),
                vmem((count, HALF * blocks + 16, part), BF16),
                vmem((count, 16, part), BF16),
                vmem((HALF * blocks, 2 * part), BF16),
                vmem((-(-depth // MAIN), LANES, 2 * part), F32),
                vmem((blocks, HALF, LANES), F32),
                vmem((HALF * blocks, LANES), F32),
            ],
            [start, x_all, x_far, dz, dz_rest, far],
            5 * count + 3,
            2 * count * flat * full * part,
        )

    last_parts = cross_parts_of(layers - 1, 1, last_far, idx)
    cross_parts = cross_parts_of(0, layers - 1, dz_far, after(idx, last_parts[2]))

    down = lambda value: value.astype(BF16)
    up = lambda value: value.astype(F32)

    def near_sum(parts, arrived, last):
        return up(parts[0]) + up(arrived[0]) + up(last)

    def far_send(parts, arrived):
        return hop(down(up(parts[1]) + up(arrived[1])), second)

    def send_blocks(held):
        return turns([down(held[r]) for r in range(1, blocks)])

    def total_of(held, turned):
        held = held[0] + sum(up(value) for value in turned)
        for perm in others:
            held = held + hop(held, perm)
        return held

    def two_of(mine, one):
        return hop(jnp.stack([mine, one]), second)

    def far_of(mine, one, two):
        return hop(jnp.concatenate([jnp.stack([mine, one]), two]), pair)

    grad_pieces = [input_grads[0]] + turns(input_grads[1:])
    tower_arrived, last_send, grad_pieces[1] = join(tower_arrived, last_parts[2], grad_pieces[1])
    tower_second = far_send(tower_parts, tower_arrived)
    last_arrived = hop(last_send, first)
    tower_second, last_arrived, cross_send, *grad_pieces = join(
        tower_second, last_arrived, cross_parts[2], *grad_pieces
    )

    tower_held = near_sum(tower_parts, tower_arrived, tower_second)
    tower_turned = send_blocks(tower_held)
    last_second = far_send(last_parts, last_arrived)
    cross_arrived = hop(cross_send, first)
    input_out, logits_all, losses = call(
        functools.partial(finish_input, blocks=blocks),
        (shape((width, tokens), F32), shape((1, tokens), F32), shape((SHARE, LANES), F32)),
        [vmem((blocks, 8, part), F32)],
        [idx, *grad_pieces],
        mib=16,
        nbytes=2 << 20,
    )
    last_second, cross_arrived, losses, *tower_turned = join(last_second, cross_arrived, losses, *tower_turned)

    last_held = near_sum(last_parts, last_arrived, last_second)
    last_turned = send_blocks(last_held)
    cross_second = far_send(cross_parts, cross_arrived)
    tower_mine = down(total_of(tower_held, tower_turned) + jnp.pad(losses, ((0, 0), (full - LANES, hidden))))
    tower_one = hop(tower_mine, first)
    cross_second, tower_one, *last_turned = join(cross_second, tower_one, *last_turned)

    cross_held = near_sum(cross_parts, cross_arrived, cross_second)
    cross_turned = send_blocks(cross_held)
    tower_two = two_of(tower_mine, tower_one)
    last_mine = down(total_of(last_held, last_turned))
    last_one = hop(last_mine, first)
    tower_two, last_one, *cross_turned = join(tower_two, last_one, *cross_turned)

    cross_mine = down(total_of(cross_held, cross_turned))
    cross_one = hop(cross_mine, first)
    last_two = two_of(last_mine, last_one)
    tower_far = far_of(tower_mine, tower_one, tower_two)
    cross_one, last_two, tower_far = join(cross_one, last_two, tower_far)

    cross_two = two_of(cross_mine, cross_one)
    last_far = far_of(last_mine, last_one, last_two)
    tower_sums = [tower_mine, tower_one, tower_two, tower_far]
    last_sums = [last_mine, last_one, last_two, last_far]
    tower1_grad, tower2_grad, rows, mean = call(
        functools.partial(finish_tower, depth=depth),
        (shape((depth, size), F32), shape((size, hidden), F32), shape((3, size), F32), shape((1, 1), F32)),
        [vmem((size, full), F32), vmem((8, 1, LANES), F32)],
        [idx, *tower_sums, day_line],
        mib=16,
        nbytes=4 << 20,
    )
    def finish(sums, base, count, before):
        alias = {5: 0} if before else {}
        return call(
            functools.partial(finish_cross, blocks=blocks, base=base, more=len(before)),
            (shape((layers, width, depth), F32), shape((count + len(before) // 2, width), F32)),
            [vmem((count, width, depth), F32), vmem((MAIN, LANES), F32)],
            [idx, *sums] + [(value, spec) for value, spec in zip(before, (HBM, VMEM))],
            mib=16,
            out_spec=(HBM, VMEM),
            aliases=alias,
            copies=count,
            nbytes=4 << 20,
        )

    before = finish(last_sums, layers - 1, 1, ())
    cross_two, tower1_grad, before = join(cross_two, tower1_grad, before)
    cross_far = far_of(cross_mine, cross_one, cross_two)
    cross_grad, cross_bias_grad = finish([cross_mine, cross_one, cross_two, cross_far], 0, layers - 1, before)
    day_counts = day_line[0, :DAYS]
    return (
        mean[0, 0],
        logits_all[0],
        input_out.T,
        cross_grad,
        cross_bias_grad,
        tower1_grad,
        rows[0],
        tower2_grad,
        rows[1],
        rows[2],
        day_counts,
        field_counts,
    )


def solution(mesh):
    in_specs = (
        P("dp", "mp"),
        P("dp", None),
        P("dp"),
        P("dp"),
        P(None, "mp", None),
        P(None, "mp"),
        P(None, "mp"),
        P("mp"),
        P("mp", None),
        P("mp"),
        P("mp"),
    )
    out_specs = (
        P(),
        P("dp"),
        P("dp", "mp"),
        P(None, "mp", None),
        P(None, "mp"),
        P(None, "mp"),
        P("mp"),
        P("mp", None),
        P("mp"),
        P("mp"),
        P(),
        P(),
    )
    return jax.shard_map(
        per_device, mesh=mesh, in_specs=in_specs, out_specs=out_specs, check_vma=False
    )
```

```python
import functools

import jax
import jax.numpy as jnp
from jax import lax
from jax.experimental import pallas as pl
from jax.experimental.pallas import tpu as pltpu
from jax.sharding import PartitionSpec as P

DAYS = 24
BUCKETS = 128
BF16 = jnp.bfloat16
F32 = jnp.float32
MAIN = 256
SHARE = 32
HALF = MAIN // 2
LANES = 128
APART = 64
LOSS = 24
COUNT = 16
VMEM = pl.BlockSpec(memory_space=pltpu.VMEM)
SMEM = pl.BlockSpec(memory_space=pltpu.SMEM)
HBM = pl.BlockSpec(memory_space=pl.ANY)
FAR = pl.BlockSpec(memory_space=pltpu.HBM)
NT = (((1,), (1,)), ((), ()))
TN = (((0,), (0,)), ((), ()))
NN = (((1,), (0,)), ((), ()))


def gelu_parts(values):
    cdf_part = 0.5 * (1.0 + lax.erf(values * 0.7071067811865476))
    slope = cdf_part + values * jnp.exp(-0.5 * values * values) * 0.3989422804014327
    return (values * cdf_part, slope)


def dot(lhs, rhs, dims, precision=None):
    return lax.dot_general(lhs, rhs, dims, preferred_element_type=F32, precision=precision)


def call(kernel, outs, scratch, args, mib, spec=VMEM, copies=0, out_spec=None, aliases={}, flops=0, nbytes=0):
    arrays = [a[0] if isinstance(a, tuple) else a for a in args[1:]]
    specs = [a[1] if isinstance(a, tuple) else spec for a in args[1:]]
    if copies:
        scratch = scratch + [pltpu.SemaphoreType.DMA((copies,))]
    return pl.pallas_call(
        kernel,
        out_shape=outs,
        in_specs=[SMEM] + specs,
        out_specs=out_spec or jax.tree.map(lambda _: spec, outs),
        scratch_shapes=scratch,
        input_output_aliases=aliases,
        compiler_params=pltpu.CompilerParams(vmem_limit_bytes=mib << 20),
        cost_estimate=pl.CostEstimate(flops=flops, bytes_accessed=nbytes, transcendentals=0),
    )(args[0], *arrays)


class Copies:
    def __init__(self, sems):
        self.sems, self.count = sems, 0

    def start(self, source, target):
        copy = pltpu.make_async_copy(source, target, self.sems.at[self.count])
        self.count += 1
        copy.start()
        return copy


def wait(*copies):
    for copy in copies:
        copy.wait()


def after(value, *others):
    return lax.optimization_barrier((value,) + others)[0]


def places(idx):
    core, plane = idx[1], idx[2]
    first, second = core + 1, 2 - core
    mine = [plane, plane ^ first, plane ^ second, plane ^ 3]
    theirs = [plane, plane ^ second, plane ^ first, plane ^ 3]
    return [core * HALF + SHARE * q for q in mine] + [(1 - core) * HALF + SHARE * q for q in theirs]


def relative(idx):
    core, plane = idx[1], idx[2]
    first, second = core + 1, 2 - core
    return [plane, plane ^ second, plane ^ first, plane ^ 3]


def block_of(idx, turn, blocks):
    return lax.rem(idx[0] - turn + blocks, blocks)


def block_ahead(idx, turn, blocks):
    return lax.rem(idx[0] + turn, blocks)


def rows_at(offset, size, unit=16):
    return pl.ds(pl.multiple_of(offset, unit), size)


def split3(line):
    high = line.astype(BF16).astype(F32)
    middle = (line - high).astype(BF16).astype(F32)
    return high, middle, line - high - middle


def lane_of(shape):
    return lax.broadcasted_iota(jnp.int32, shape, 1)


def pack_rest(idx, weight, bias, inputs, vectors, weight1, weight2, ids, days, *refs, blocks):
    out, own1, tally = refs[:3]
    chunks, (lines,) = refs[3 : 3 + blocks], refs[3 + blocks :]
    layers, width, depth = weight.shape
    size = weight2.shape[0]
    left = width - MAIN
    part = chunks[0].shape[1]
    full = own1.shape[1]
    own_row = idx[1] * HALF + idx[2] * SHARE

    lines[...] = jnp.zeros_like(lines)
    for layer in range(layers):
        lines[left * layer : left * (layer + 1), 0:depth] = weight[layer, MAIN:width, :].astype(F32)
        at = left * layers + layer
        lines[at : at + 1, 0:width] = bias[layer : layer + 1, :].astype(F32)
    rest = [lines[:, at : at + part].astype(BF16) for at in range(0, lines.shape[1], part)]

    own1[:, 0:depth] = weight1[...].T
    own1[:, depth:] = jnp.zeros((size, full - depth), BF16)
    out[:, 0:full] = own1[rows_at(own_row, SHARE), :]
    out[:, full:] = weight2[rows_at(own_row, SHARE), :]

    first = 16 * len(rest)
    for turn in range(blocks):
        lanes = pl.ds(pl.multiple_of(block_ahead(idx, turn, blocks) * part, LANES), part)
        for at, value in enumerate(rest):
            chunks[turn][16 * at : 16 * (at + 1), :] = value
        chunks[turn][first : first + width, :] = inputs[:, lanes]
        chunks[turn][first + width : first + width + 3, :] = vectors[...]

    fields, tokens = ids.shape
    bucket = lax.broadcasted_iota(jnp.int32, (BUCKETS, tokens), 0)
    lane = lane_of((BUCKETS, LANES))
    tile = jnp.zeros((BUCKETS, LANES), F32)
    for field in range(fields + 1):
        line = ids[field : field + 1, :] if field < fields else days[...]
        hits = jnp.sum((bucket == line).astype(F32), axis=1, keepdims=True)
        high = jnp.floor(hits * (1.0 / 256.0))
        tile = jnp.where(lane == COUNT + field, high, tile)
        tile = jnp.where(lane == COUNT + fields + 1 + field, hits - 256.0 * high, tile)
    half = BUCKETS // 2
    tile = tile[0:half, :] + pltpu.roll(tile[half:, :], 2 * (fields + 1), 1)
    tally[0:half, :] = tile.astype(BF16)
    tally[half:, :] = jnp.zeros((tally.shape[0] - half, LANES), BF16)


def cross_eight(refs):
    near, last, near_far, last_far = refs
    return [near.at[at] for at in range(3)] + [last] + [near_far.at[at] for at in range(3)] + [last_far]


def place_cross(idx, weight, own, slices, blocks, layer, pad):
    layers, depth = weight.shape[0], weight.shape[2]
    low = depth // LANES * LANES
    weight[layer, rows_at(idx[0] * pad, MAIN), :] = own[layer, 0:MAIN, :]
    tail = layers * low + (depth - low) * layer
    for turn in range(1, blocks):
        base = block_of(idx, turn, blocks) * pad
        for offset, piece in zip(places(idx), slices):
            rows = rows_at(base + offset, SHARE)
            weight[layer, rows, 0:low] = piece[turn - 1, :, low * layer : low * (layer + 1)]
            weight[layer, rows, low:] = piece[turn - 1, :, tail : tail + depth - low]


def place_rest(idx, weight, pieces, lines, tail, layers, left, pad):
    blocks = len(pieces)
    depth = weight.shape[2]
    part = pieces[0].shape[1]
    tail[...] = jnp.zeros_like(tail)
    for turn, piece in enumerate(pieces):
        for group in range(-(-depth // part)):
            stop = min(depth, part * (group + 1))
            lines[block_of(idx, turn, blocks), :, part * group : stop] = piece[
                16 * group : 16 * (group + 1), 0 : stop - part * group
            ].astype(F32)
    for block in range(blocks):
        for layer in range(layers):
            tail[0:left, :] = lines[block, left * layer : left * (layer + 1), :]
            at = pad * block + MAIN
            weight[layer, at : at + 16, :] = tail[...].astype(BF16)


def cross_forward(idx, *refs, blocks, layers, width, pad, depth):
    pieces, refs = refs[:blocks], refs[blocks:]
    own, refs = refs[0], refs[1:]
    slices, refs = cross_eight(refs[:4]), refs[4:]
    z_out, x_out, weight, lines, tail, start, state, nat = refs
    left = width - MAIN
    place_rest(idx, weight, pieces, lines, tail, layers, left, pad)
    at = 16 * -(-depth // pieces[0].shape[1])
    bias = [lines[block, :, 0:384].T for block in range(blocks)]
    for turn, piece in enumerate(pieces):
        block = block_of(idx, turn, blocks)
        start[block, 0:width, :] = piece[at : at + width, :].astype(F32)
        start[block, width:, :] = jnp.zeros((pad - width, piece.shape[1]), F32)
    full = nat.shape[0]
    ones = lax.broadcasted_iota(jnp.int32, (full - depth, nat.shape[1]), 0) == 0
    nat[depth:full, :] = ones.astype(F32)
    for block in range(blocks):
        nat[width * block : width * (block + 1), :] = start[block, 0:width, :]
    for layer in range(layers):
        x_out[layer] = nat[...].astype(BF16)
        place_cross(idx, weight, own, slices, blocks, layer, pad)
        at = left * layers + layer
        for block in range(blocks):
            rows = slice(pad * block, pad * (block + 1))
            value = dot(weight[layer, rows, :], x_out[layer, 0:depth, :], NN) + bias[block][0:pad, at : at + 1]
            z_out[layer, rows, :] = value
            before = start[block] if layer == 0 else state[block]
            value = start[block] * value + before
            state[block] = value
            nat[width * block : width * (block + 1), :] = value[0:width, :]
    x_out[layers] = nat[...].astype(BF16)


def tower_both(idx, *refs, blocks, layers, width, depth, fields, examples):
    (labels, day_ids), refs = refs[:2], refs[2:]
    pieces, refs = refs[:blocks], refs[blocks:]
    (own1, own2), refs = refs[:2], refs[2:]
    slices, refs = refs[:8], refs[8:]
    x_all, acts, far, heads, flow, lines_out, day_out, field_out = refs[:8]
    inputs, tower, slope1, act2, headed, vectors = refs[8:]
    hidden = tower.shape[0]
    full = x_all.shape[1]
    size = hidden // blocks
    part = x_all.shape[2]
    low = depth // LANES * LANES
    at = 16 * -(-depth // part) + width
    for turn, piece in enumerate(pieces):
        inputs[block_of(idx, turn, blocks)] = piece[at : at + 3, :].astype(F32)
    base = idx[0] * size
    tower[rows_at(base, size), 0:full] = own1[...]
    tower[rows_at(base, size), full:] = own2[...]
    for turn in range(1, blocks):
        base = block_of(idx, turn, blocks) * size
        for offset, piece in zip(places(idx), slices):
            rows = rows_at(base + offset, SHARE)
            tower[rows, :] = piece[turn - 1, :, piece.shape[2] - tower.shape[1] :]
    parts = [slice(size * block, size * (block + 1)) for block in range(blocks)]
    columns = []
    for block in range(blocks):
        vectors[0:3, :] = inputs[block]
        columns.append(vectors[...].T)
    for rows, column in zip(parts, columns):
        act, slope = gelu_parts(dot(tower[rows, 0:depth], x_all[layers, 0:depth, :], NN) + column[:, 0:1])
        acts[0, rows, :] = act.astype(BF16)
        slope1[rows, :] = slope
    logits = jnp.zeros((1, part), F32)
    for rows, column in zip(parts, columns):
        act, slope = gelu_parts(dot(tower[:, full + rows.start : full + rows.stop], acts[0], TN) + column[:, 2:3])
        act2[rows, :] = act
        headed[rows, :] = column[:, 1:2] * slope
        logits += jnp.sum(act * column[:, 1:2], axis=0, keepdims=True)

    half = BUCKETS // 2
    tally = jnp.zeros((half, LANES), F32)
    for piece in slices:
        at = piece.shape[2] - tower.shape[1] + low
        tally += piece[0 : half // SHARE, :, at : at + LANES].astype(F32).reshape(half, LANES)
    count = jnp.concatenate([tally, pltpu.roll(tally, LANES - 2 * (fields + 1), 1)], axis=0)
    high = count[:, COUNT : COUNT + fields + 1]
    count = 256.0 * high + count[:, COUNT + fields + 1 : COUNT + 2 * (fields + 1)]
    days = count[0:32, fields : fields + 1]
    padded = jnp.concatenate([count, jnp.zeros((BUCKETS, LANES - fields - 1), F32)], axis=1).T
    field_out[...] = padded[0:fields, :].astype(jnp.int32)
    day_out[...] = padded[fields : fields + 1, :].astype(jnp.int32)

    mine = pl.ds(pl.multiple_of(idx[0] * part, LANES), part)
    lab = labels[:, mine].astype(F32)
    table = (lax.broadcasted_iota(jnp.int32, (32, part), 0) == day_ids[:, mine]).astype(F32)
    share = examples / (DAYS * jnp.maximum(days, 1.0))
    weights = jnp.sum(table * share, axis=0, keepdims=True)
    decay = jnp.exp(-jnp.abs(logits))
    loss = jnp.maximum(logits, 0.0) + jnp.log1p(decay) - lab * logits
    sigmoid = jnp.where(logits >= 0.0, 1.0, decay) / (1.0 + decay)
    dl = weights * (sigmoid - lab)
    losses = dot(jnp.broadcast_to(loss, (8, part)), table, NT, lax.Precision.HIGHEST)[0:1, :]
    lines_out[0:1, :] = logits
    lines_out[1:2, :] = jnp.zeros_like(logits)
    lines_out[1:2, 0 : losses.shape[1]] = losses

    acts[1] = (dl * headed[...]).astype(BF16)
    far[0:hidden, :] = acts[1]
    for rows in parts:
        acts[2, rows, :] = (dot(tower[rows, full:], acts[1], NN) * slope1[rows, :]).astype(BF16)
    for block in range(blocks):
        rows = rows_at(block * size + (1 - idx[1]) * HALF, HALF)
        at = hidden + HALF * block
        far[at : at + HALF, :] = acts[0, rows, :]
        at = hidden + HALF * (block + blocks)
        far[at : at + HALF, :] = acts[2, rows, :]
    for rows in parts:
        heads[rows, :] = jnp.broadcast_to(jnp.sum(act2[rows, :] * dl, axis=1, keepdims=True), (size, LANES))
    flow[...] = dot(tower[:, 0:depth], acts[2], TN)


def cross_backward(idx, *refs, blocks, layers, width, pad, depth):
    extra_lines, refs = refs[0], refs[1:]
    pieces, refs = refs[:blocks], refs[blocks:]
    own, refs = refs[0], refs[1:]
    slices, refs = cross_eight(refs[:4]), refs[4:]
    (dx3, z_all), refs = refs[:2], refs[2:]
    eg_out, refs = refs[:blocks], refs[blocks:]
    dz_out, rest_out, dz_far_last, dz_far_out = refs[:4]
    weight, inputs, lines, tail, flow, padded, total, rest = refs[4:]
    left = width - MAIN
    place_rest(idx, weight, pieces, lines, tail, layers, left, pad)
    at = 16 * -(-depth // pieces[0].shape[1])
    for turn, piece in enumerate(pieces):
        inputs[block_of(idx, turn, blocks)] = piece[at : at + width, :].astype(F32)
    padded[...] = jnp.zeros_like(padded)
    rest[...] = jnp.zeros_like(rest)
    for layer in reversed(range(layers)):
        source = dx3 if layer == layers - 1 else flow
        for block in range(blocks):
            rows = slice(pad * block, pad * (block + 1))
            dx = source[width * block : width * (block + 1), :]
            padded[block, 0:width, :] = dx
            dx = padded[block, 0:width, :]
            dz = dx * inputs[block]
            term = dx * z_all[layer, pad * block : pad * block + width, :]
            total[block, 0:width, :] = term if layer == layers - 1 else total[block, 0:width, :] + term
            rest[left * block : left * (block + 1), :] = dz[MAIN:width, :]
            padded[block, 0:width, :] = dz
            dz_out[layer, rows, :] = padded[block].astype(BF16)
        rest_out[layer] = rest[...].astype(BF16)
        far = dz_far_last.at[0] if layer == layers - 1 else dz_far_out.at[layer]
        far[HALF * blocks :, :] = rest[...].astype(BF16)
        for block in range(blocks):
            rows = rows_at(pad * block + (1 - idx[1]) * HALF, HALF)
            far[HALF * block : HALF * (block + 1), :] = dz_out[layer, rows, :]
        place_cross(idx, weight, own, slices, blocks, layer, pad)
        flow[...] = source[...] + dot(weight[layer], dz_out[layer], TN)
    extras = split3(extra_lines[0:1, :]) + split3(extra_lines[1:2, :])
    for block in range(blocks):
        total[block, 0:width, :] += flow[width * block : width * (block + 1), :]
        total[block, width:, :] = jnp.zeros((pad - width, flow.shape[1]), F32)
        for at, extra in enumerate(extras):
            total[block, width + at : width + at + 1, :] = extra
    for turn in range(blocks):
        eg_out[turn][...] = total[block_ahead(idx, turn, blocks)].astype(BF16)


def tower_grads(idx, x_all, x_far, acts, far, head, near_out, far_out, send_out, *refs, blocks, depth, layers):
    x_cat, acts_in, far_in, heads, lhs, d_cat, near, away, send, sems = refs
    hidden = acts.shape[1]
    size = hidden // blocks
    part = acts.shape[2]
    low = depth // LANES * LANES
    bias = depth - low
    copies = Copies(sems)
    first = [
        copies.start(acts, acts_in),
        copies.start(far, far_in),
        copies.start(x_all.at[layers], x_cat.at[:, 0:part]),
        copies.start(x_far.at[layers], x_cat.at[:, part : 2 * part]),
        copies.start(head, heads),
    ]
    wait(*first)
    lane = lane_of((SHARE, LANES))
    pick = (lax.broadcasted_iota(jnp.int32, (LANES, 2 * part), 0) == bias + 1).astype(BF16)
    order = [(where, slot) for where in range(4) for slot in range(blocks)]
    shares = relative(idx)
    d_cat[:, 0:part] = acts_in[1]
    d_cat[:, part:] = far_in[0:hidden, :]
    scale = []
    for at, (where, slot) in enumerate(order):
        block = block_ahead(idx, slot, blocks)
        rows = rows_at(block * size + idx[1] * HALF + SHARE * shares[where], SHARE)
        other = rows_at(block * size + (1 - idx[1]) * HALF + SHARE * shares[where], SHARE)
        lines = rows_at(hidden + HALF * block + SHARE * shares[where], SHARE)
        after_it = rows_at(hidden + HALF * (block + blocks) + SHARE * shares[where], SHARE)
        here = slice(SHARE * at, SHARE * (at + 1))
        lhs[0, here, 0:part] = acts_in[2, rows, :]
        lhs[0, here, part:] = far_in[after_it, :]
        lhs[1, here, 0:part] = acts_in[0, rows, :]
        lhs[1, here, part:] = far_in[lines, :]
        lhs[2, here, 0:part] = acts_in[1, rows, :]
        lhs[2, here, part:] = far_in[rows, :]
        scale.append(
            jnp.where(lane == bias + 2, heads[rows, :], 0.0) + jnp.where(lane == bias + 3, heads[other, :], 0.0)
        )
    extra = dot(lhs[2], pick, NT)
    wide = dot(lhs[0], x_cat[...], NT)
    deep = dot(lhs[1], d_cat[...], NT)
    for at, (where, slot) in enumerate(order):
        target = (near, away, send.at[0], send.at[1])[where].at[slot]
        here = slice(SHARE * at, SHARE * (at + 1))
        target[:, 0:low] = wide[here, 0:low].astype(BF16)
        target[:, low : low + LANES] = (wide[here, low:] + extra[here, :] + scale[at]).astype(BF16)
        target[:, low + LANES :] = deep[here, :].astype(BF16)
    wait(copies.start(send, send_out), copies.start(near, near_out), copies.start(away, far_out))


def cross_grads(idx, x_all, x_far, dz, rest, dz_far, near_out, far_out, send_out, *refs, blocks, base, pad, depth):
    x_cat, dz_in, far_in, rest_in, lhs, few, extra, tiles, near, away, send, sems = refs
    part = dz.shape[2]
    low = depth // LANES * LANES
    groups = -(-depth // MAIN)
    count = dz_far.shape[0]
    left = rest_in.shape[1] // blocks
    copies = Copies(sems)
    first = []
    for layer in reversed(range(count)):
        first.append(
            [
                copies.start(dz.at[base + layer], dz_in.at[layer]),
                copies.start(dz_far.at[layer], far_in.at[layer]),
                copies.start(rest.at[base + layer], rest_in.at[layer]),
                copies.start(x_all.at[base + layer], x_cat.at[layer, :, 0:part]),
                copies.start(x_far.at[base + layer], x_cat.at[layer, :, part : 2 * part]),
            ]
        )
    few[...] = jnp.zeros_like(few)
    order = [(where, slot) for where in range(4) for slot in range(blocks)]
    shares = relative(idx)
    lane = lane_of((HALF, LANES))
    bias = depth - low
    span = left * groups
    for layer, started in zip(reversed(range(count)), first):
        wait(*started)
        value = jnp.zeros((HALF, LANES), F32)
        near_rest = rest_in[layer].astype(F32)
        far_rest = far_in[layer, HALF * blocks :, :].astype(F32)
        for group in range(groups):
            for block in range(blocks):
                lines = slice(span * block + left * group, span * block + left * (group + 1))
                few[group, lines, 0:part] = near_rest[left * block : left * (block + 1), :]
                few[group, lines, part:] = far_rest[left * block : left * (block + 1), :]
            if MAIN * (group + 1) <= depth:
                rows = rows_at(MAIN * group + idx[1] * HALF, HALF)
            else:
                rows = slice(MAIN * group, MAIN * group + HALF)
            value += dot(x_cat[layer, rows, :], few[group].astype(BF16), NT)
        inside = (lane > bias) & (lane <= bias + span)
        for block in range(blocks):
            extra[block] = jnp.where(inside, pltpu.roll(value, (bias + 1 - span * block) % LANES, 1), 0.0)
        for at, (where, slot) in enumerate(order):
            block = block_ahead(idx, slot, blocks)
            rows = rows_at(pad * block + idx[1] * HALF + SHARE * shares[where], SHARE)
            lines = rows_at(HALF * block + SHARE * shares[where], SHARE)
            here = slice(SHARE * at, SHARE * (at + 1))
            lhs[here, 0:part] = dz_in[layer, rows, :]
            lhs[here, part:] = far_in[layer, lines, :]
        grad = dot(lhs[...], x_cat[layer], NT)
        for at, (where, slot) in enumerate(order):
            target = (near, away, send.at[0], send.at[1])[where].at[slot]
            here = slice(SHARE * at, SHARE * (at + 1))
            target[:, low * layer : low * (layer + 1)] = grad[here, 0:low].astype(BF16)
            tile = grad[here, low:] + extra[block_ahead(idx, slot, blocks), rows_at(SHARE * shares[where], SHARE), :]
            if layer < count - 1:
                tile = tiles[here, :] + (pltpu.roll(tile, APART * layer, 1) if layer else tile)
            elif layer:
                tile = pltpu.roll(tile, APART * layer, 1)
            if layer:
                tiles[here, :] = tile
            else:
                target[:, low * count :] = tile.astype(BF16)
    wait(copies.start(send, send_out), copies.start(near, near_out), copies.start(away, far_out))


def eight(mine, one, two, far):
    return [mine, one, two.at[0], two.at[1]] + [far.at[at] for at in range(4)]


def finish_input(idx, *refs, blocks):
    pieces, (out, logits, losses, day_held) = refs[:blocks], refs[blocks:]
    width = out.shape[0]
    size = pieces[0].shape[1]
    for turn, piece in enumerate(pieces):
        block = block_of(idx, turn, blocks)
        lanes = pl.ds(pl.multiple_of(block * size, LANES), size)
        values = piece[...].astype(F32)
        line = lambda at: values[width + at : width + at + 1, :]
        out[:, lanes] = values[0:width, :]
        logits[:, lanes] = line(0) + line(1) + line(2)
        day_held[block] = jnp.broadcast_to(line(3) + line(4) + line(5), day_held.shape[1:])
    days = day_held[0]
    for block in range(1, blocks):
        days += day_held[block]
    row = lax.broadcasted_iota(jnp.int32, losses.shape, 0)
    tile = jnp.zeros(losses.shape, F32)
    for at, value in enumerate(split3(days[0:1, 0:LANES])):
        tile = jnp.where(row == at, value, tile)
    losses[...] = jnp.where(lane_of(tile.shape) < LOSS, 0.0, pltpu.roll(tile, LOSS, 1))


def finish_tower(idx, *refs, depth):
    slices, (counts, out1, out2, rows_out, mean_out, lines, day_held) = eight(*refs[:4]), refs[4:]
    low = depth // LANES * LANES
    size = out2.shape[0]
    for offset, piece in zip(places(idx), slices):
        lines[rows_at(offset, SHARE), :] = piece[:, 0 : low + LANES].astype(F32)
        out2[rows_at(offset, SHARE), :] = piece[:, low + LANES :].astype(F32)
        tile = piece[0:16, low : low + LANES].astype(F32)
        day_held[lax.div(offset, SHARE)] = tile[0:1, :] + tile[1:2, :] + tile[2:3, :]
    turned = lines[...].T
    out1[...] = turned[0:depth, :]
    head = turned[depth + 3 : depth + 4, :]
    rows_out[0:1, :] = turned[depth : depth + 1, :]
    rows_out[1:2, :] = turned[depth + 1 : depth + 2, :]
    rows_out[2:3, 0:HALF] = turned[depth + 2 : depth + 3, 0:HALF] + head[:, HALF:]
    rows_out[2:3, HALF:] = turned[depth + 2 : depth + 3, HALF:] + head[:, 0:HALF]
    days = day_held[0]
    for at in range(1, day_held.shape[0]):
        days += day_held[at]
    days = days[:, LOSS : LOSS + DAYS]
    mean = days / jnp.maximum(counts[:, 0:DAYS].astype(F32), 1.0)
    mean_out[...] = jnp.sum(mean, axis=1, keepdims=True) / DAYS


def finish_cross(idx, *refs, blocks, base, more):
    slices, refs = eight(*refs[:4]), refs[4:]
    before, (out, bias_out, held, lines, sems) = refs[:more], refs[more:]
    count, width, depth = held.shape
    left = width - MAIN
    low = depth // LANES * LANES
    copies = Copies(sems)
    last = []
    if more:
        bias_out[count:, :] = before[1][...]
    for offset, piece in zip(places(idx), slices):
        lines[rows_at(offset, SHARE), :] = piece[:, low * count :].astype(F32)
    turned = lines[...].T
    for layer in range(count):
        for offset, piece in zip(places(idx), slices):
            rows = rows_at(offset, SHARE)
            held[layer, rows, 0:low] = piece[:, low * layer : low * (layer + 1)].astype(F32)
        held[layer, 0:MAIN, low:] = lines[:, APART * layer : APART * layer + depth - low]
        bias = APART * layer + depth - low
        bias_out[layer : layer + 1, 0:MAIN] = turned[bias : bias + 1, :]
        for group in range(-(-depth // MAIN)):
            rest = turned[bias + 1 + left * group : bias + 1 + left * (group + 1), :]
            stop = min(depth, MAIN * (group + 1)) - MAIN * group
            held[layer, MAIN:width, MAIN * group : MAIN * group + stop] = rest[:, 0:stop]
        last.append(copies.start(held.at[layer], out.at[base + layer]))
        corner = jnp.broadcast_to(rest[:, stop : stop + 1], (left, LANES))
        ahead = lax.broadcasted_iota(jnp.int32, (left, LANES), 0) == lane_of((left, LANES))
        line = jnp.sum(jnp.where(ahead, corner, 0.0), axis=0, keepdims=True)
        bias_out[layer : layer + 1, MAIN:width] = line[:, 0:left]
    wait(*last)


def per_device(
    embedded,
    feature_ids,
    day_ids,
    labels,
    cross_weight,
    cross_bias,
    tower1,
    tower1_bias,
    tower2,
    tower2_bias,
    head_weight,
):
    blocks = lax.axis_size("mp")
    groups = lax.axis_size("dp")
    tokens, width = embedded.shape
    layers, _, depth = cross_weight.shape
    size, hidden = tower2.shape
    pad = -(-width // 16) * 16
    full = -(-(depth + 3) // LANES) * LANES
    part = tokens // blocks
    examples = tokens * groups
    flat = blocks * pad
    shape = jax.ShapeDtypeStruct
    vmem = pltpu.VMEM

    me = lax.axis_index("mp")
    group = lax.axis_index("dp")
    core, plane = group & 1, (group >> 1) & 3
    idx = jnp.stack([me, core, plane, group & 7]).astype(jnp.int32)
    swap = lambda bits: [(i, i ^ bits(i)) for i in range(groups)]
    first = swap(lambda i: 4 if i & 1 else 2)
    second = swap(lambda i: 2 if i & 1 else 4)
    pair = swap(lambda i: 1)
    others = [swap(lambda i, b=b: 1 << b) for b in range(3, groups.bit_length() - 1)]
    turn_by = lambda r: [(i, (i + r) % blocks) for i in range(blocks)]
    hop = lambda value, perm: lax.ppermute(value, "dp", perm)
    turns = lambda values: [
        lax.ppermute(value, "mp", turn_by(r + 1)) for r, value in enumerate(values)
    ]

    own_row = core * HALF + plane * SHARE
    cross_send = lax.dynamic_slice(cross_weight, (0, own_row, 0), (layers, SHARE, depth))
    low = depth // LANES * LANES
    fill = jnp.zeros((SHARE, LANES - layers * (depth - low)), BF16)
    cross_send = jnp.concatenate([rows[:, :low] for rows in cross_send] + [rows[:, low:] for rows in cross_send] + [fill], axis=1)
    cross_turned = turns([cross_send] * (blocks - 1))
    vectors = jnp.stack([tower1_bias, head_weight, tower2_bias])
    wide = full + hidden
    groups_of = -(-depth // part)
    tower_send, tower_own, tally, *chunks = call(
        functools.partial(pack_rest, blocks=blocks),
        tuple(
            [
                shape((SHARE, wide), BF16),
                shape((size, full), BF16),
                shape(((blocks - 1) * SHARE, LANES), BF16),
            ]
            + [shape((16 * groups_of + width + 3, part), BF16)] * blocks
        ),
        [vmem((16, groups_of * part), F32)],
        [
            after(idx, cross_send),
            cross_weight,
            cross_bias,
            embedded.T,
            vectors,
            tower1,
            tower2,
            feature_ids.T,
            day_ids[None, :],
        ],
        mib=24,
        nbytes=2 << 20,
    )
    for perm in others:
        tally = tally + hop(tally, perm)
    tally = jnp.pad(tally.reshape(blocks - 1, SHARE, LANES), ((0, 0), (0, 0), (full - LANES, hidden)))

    join = lambda *values: lax.optimization_barrier(values)
    cross_mine = jnp.stack(cross_turned)
    cross_mine, tower_send, *chunks = join(cross_mine, tower_send, *chunks)
    cross_one, cross_two = hop(cross_mine, first), hop(cross_mine, second)
    tower_turned = turns([tower_send] * (blocks - 1))
    cross_one, cross_two, *tower_turned = join(cross_one, cross_two, *tower_turned)

    turn = lambda value, r: lax.ppermute(value, "mp", turn_by(r))
    pieces = [chunks[0]] + [turn(after(chunks[r], tower_turned[0]), r) for r in range(1, blocks - 1)]
    tower_mine = jnp.stack(tower_turned) + tally
    both = jnp.concatenate([cross_one, tower_mine], axis=2)
    tower_one, both = hop(tower_mine, first), hop(both, second)
    cross_near = jnp.stack([cross_mine, cross_one, cross_two])
    cross_far = hop(cross_near, pair)
    pieces.append(turn(after(chunks[-1], cross_far), blocks - 1))
    both, tower_one, cross_far, *pieces = join(both, tower_one, cross_far, *pieces)

    tower_three = hop(tower_one, second)
    both_far, tower_far, tower_next = hop(both, pair), hop(tower_mine, pair), hop(tower_one, pair)
    both_far, tower_far, tower_next = join(both_far, tower_far, tower_next)
    cross_slices = [cross_near, both, cross_far, both_far]

    z_all, x_all = call(
        functools.partial(cross_forward, blocks=blocks, layers=layers, width=width, pad=pad, depth=depth),
        (shape((layers, flat, part), F32), shape((layers + 1, full, part), BF16)),
        [
            vmem((layers, flat, depth), BF16),
            vmem((blocks, 16, depth), F32),
            vmem((16, depth), F32),
            vmem((blocks, pad, part), F32),
            vmem((blocks, pad, part), F32),
            vmem((full, part), F32),
        ],
        [idx, *pieces, cross_weight, *cross_slices],
        mib=28,
        flops=2 * layers * flat * full * part,
        nbytes=20 << 20,
    )
    tower_last = hop(after(tower_three, z_all), pair)
    tower_slices = [tower_mine, tower_one, both, tower_three, tower_far, tower_next, both_far, tower_last]
    x_far = hop(after(x_all, tower_last), pair)
    fields = feature_ids.shape[1]
    acts, far, head_col, dx3, lines, day_line, field_counts = call(
        functools.partial(
            tower_both, blocks=blocks, layers=layers, width=width, depth=depth, fields=fields, examples=examples
        ),
        (
            shape((3, hidden, part), BF16),
            shape((2 * hidden, part), BF16),
            shape((hidden, LANES), F32),
            shape((depth, part), F32),
            shape((2, part), F32),
            shape((1, BUCKETS), jnp.int32),
            shape((fields, BUCKETS), jnp.int32),
        ),
        [
            vmem((blocks, 3, part), F32),
            vmem((hidden, wide), BF16),
            vmem((hidden, part), F32),
            vmem((hidden, part), F32),
            vmem((hidden, part), F32),
            vmem((8, part), F32),
        ],
        [
            idx,
            labels[None, :],
            day_ids[None, :],
            *pieces,
            tower_own,
            tower2,
            *tower_slices,
            x_all,
        ],
        mib=28,
        flops=8 * hidden * full * part,
        nbytes=10 << 20,
    )
    far = hop(far, pair)

    def grads(kernel, keep, scratch, args, copies, flops):
        outs = keep, keep, (2,) + keep
        return call(
            kernel,
            tuple(shape(s, BF16) for s in outs),
            scratch + [vmem(s, BF16) for s in outs],
            args,
            mib=20,
            spec=HBM,
            copies=copies,
            flops=flops,
            nbytes=10 << 20,
        )

    tower_parts = grads(
        functools.partial(tower_grads, blocks=blocks, depth=depth, layers=layers),
        (blocks, SHARE, wide),
        [
            vmem((full, 2 * part), BF16),
            vmem((3, hidden, part), BF16),
            vmem((2 * hidden, part), BF16),
            vmem((hidden, LANES), F32),
            vmem((3, HALF * blocks, 2 * part), BF16),
            vmem((hidden, 2 * part), BF16),
        ],
        [idx, x_all, x_far, acts, far, head_col],
        8,
        4 * hidden * full * part,
    )
    tower_arrived = hop(tower_parts[2], first)
    *input_grads, dz, dz_rest, last_far, dz_far = call(
        functools.partial(cross_backward, blocks=blocks, layers=layers, width=width, pad=pad, depth=depth),
        tuple([shape((pad, part), BF16)] * blocks)
        + (
            shape((layers, flat, part), BF16),
            shape((layers, 16, part), BF16),
            shape((1, HALF * blocks + 16, part), BF16),
            shape((layers - 1, HALF * blocks + 16, part), BF16),
        ),
        [
            vmem((layers, flat, depth), BF16),
            vmem((blocks, width, part), F32),
            vmem((blocks, 16, depth), F32),
            vmem((16, depth), F32),
            vmem((depth, part), F32),
            vmem((blocks, pad, part), F32),
            vmem((blocks, pad, part), F32),
            vmem((16, part), F32),
        ],
        [
            after(idx, tower_parts[2]),
            lines,
            *pieces,
            cross_weight,
            *cross_slices,
            dx3,
            z_all,
        ],
        mib=34,
        flops=2 * layers * flat * full * part,
        nbytes=20 << 20,
    )
    last_far = hop(last_far, pair)
    dz_far = hop(dz_far, pair)

    def cross_parts_of(base, count, far, start):
        return grads(
            functools.partial(cross_grads, blocks=blocks, base=base, pad=pad, depth=depth),
            (blocks, SHARE, count * low + LANES),
            [
                vmem((count, full, 2 * part), BF16),
                vmem((count, flat, part), BF16),
                vmem((count, HALF * blocks + 16, part), BF16),
                vmem((count, 16, part), BF16),
                vmem((HALF * blocks, 2 * part), BF16),
                vmem((-(-depth // MAIN), LANES, 2 * part), F32),
                vmem((blocks, HALF, LANES), F32),
                vmem((HALF * blocks, LANES), F32),
            ],
            [start, x_all, x_far, dz, dz_rest, far],
            5 * count + 3,
            2 * count * flat * full * part,
        )

    last_parts = cross_parts_of(layers - 1, 1, last_far, idx)
    cross_parts = cross_parts_of(0, layers - 1, dz_far, after(idx, last_parts[2]))

    down = lambda value: value.astype(BF16)
    up = lambda value: value.astype(F32)

    def near_sum(parts, arrived, last):
        return up(parts[0]) + up(arrived[0]) + up(last)

    def far_send(parts, arrived):
        return hop(down(up(parts[1]) + up(arrived[1])), second)

    def send_blocks(held):
        return turns([down(held[r]) for r in range(1, blocks)])

    def total_of(held, turned):
        held = held[0] + sum(up(value) for value in turned)
        for perm in others:
            held = held + hop(held, perm)
        return held

    def two_of(mine, one):
        return hop(jnp.stack([mine, one]), second)

    def far_of(mine, one, two):
        return hop(jnp.concatenate([jnp.stack([mine, one]), two]), pair)

    grad_pieces = [input_grads[0]] + turns(input_grads[1:])
    tower_arrived, last_send, grad_pieces[1] = join(tower_arrived, last_parts[2], grad_pieces[1])
    tower_second = far_send(tower_parts, tower_arrived)
    last_arrived = hop(last_send, first)
    tower_second, last_arrived, cross_send, *grad_pieces = join(
        tower_second, last_arrived, cross_parts[2], *grad_pieces
    )

    tower_held = near_sum(tower_parts, tower_arrived, tower_second)
    tower_turned = send_blocks(tower_held)
    last_second = far_send(last_parts, last_arrived)
    cross_arrived = hop(cross_send, first)
    input_out, logits_all, losses = call(
        functools.partial(finish_input, blocks=blocks),
        (shape((width, tokens), F32), shape((1, tokens), F32), shape((SHARE, LANES), F32)),
        [vmem((blocks, 8, part), F32)],
        [idx, *grad_pieces],
        mib=16,
        nbytes=2 << 20,
    )
    last_held = near_sum(last_parts, last_arrived, last_second)
    last_turned = send_blocks(last_held)
    cross_arrived, losses, last_turned[0], *tower_turned = join(
        cross_arrived, losses, last_turned[0], *tower_turned
    )

    last_turned[1:] = [after(value, last_turned[0]) for value in last_turned[1:]]
    cross_second = far_send(cross_parts, cross_arrived)
    tower_mine = down(total_of(tower_held, tower_turned) + jnp.pad(losses, ((0, 0), (full - LANES, hidden))))
    tower_one = hop(tower_mine, first)
    cross_second, tower_one, *last_turned = join(cross_second, tower_one, *last_turned)

    cross_held = near_sum(cross_parts, cross_arrived, cross_second)
    cross_turned = send_blocks(cross_held)
    tower_two = two_of(tower_mine, tower_one)
    last_mine = down(total_of(last_held, last_turned))
    last_one = hop(last_mine, first)
    tower_two, last_one, *cross_turned = join(tower_two, last_one, *cross_turned)

    cross_mine = down(total_of(cross_held, cross_turned))
    cross_one = hop(cross_mine, first)
    last_two = two_of(last_mine, last_one)
    tower_far = far_of(tower_mine, tower_one, tower_two)
    cross_one, last_two, tower_far = join(cross_one, last_two, tower_far)

    cross_two = two_of(cross_mine, cross_one)
    last_far = far_of(last_mine, last_one, last_two)
    tower_sums = [tower_mine, tower_one, tower_two, tower_far]
    last_sums = [last_mine, last_one, last_two, last_far]
    tower1_grad, tower2_grad, rows, mean = call(
        functools.partial(finish_tower, depth=depth),
        (shape((depth, size), F32), shape((size, hidden), F32), shape((3, size), F32), shape((1, 1), F32)),
        [vmem((size, full), F32), vmem((8, 1, LANES), F32)],
        [idx, *tower_sums, day_line],
        mib=16,
        nbytes=4 << 20,
    )
    def finish(sums, base, count, before):
        alias = {5: 0} if before else {}
        return call(
            functools.partial(finish_cross, blocks=blocks, base=base, more=len(before)),
            (shape((layers, width, depth), F32), shape((count + len(before) // 2, width), F32)),
            [vmem((count, width, depth), F32), vmem((MAIN, LANES), F32)],
            [idx, *sums] + [(value, spec) for value, spec in zip(before, (HBM, VMEM))],
            mib=16,
            out_spec=(HBM, VMEM),
            aliases=alias,
            copies=count,
            nbytes=4 << 20,
        )

    before = finish(last_sums, layers - 1, 1, ())
    cross_two, tower1_grad, before = join(cross_two, tower1_grad, before)
    cross_far = far_of(cross_mine, cross_one, cross_two)
    cross_grad, cross_bias_grad = finish([cross_mine, cross_one, cross_two, cross_far], 0, layers - 1, before)
    day_counts = day_line[0, :DAYS]
    return (
        mean[0, 0],
        logits_all[0],
        input_out.T,
        cross_grad,
        cross_bias_grad,
        tower1_grad,
        rows[0],
        tower2_grad,
        rows[1],
        rows[2],
        day_counts,
        field_counts,
    )


def solution(mesh):
    in_specs = (
        P("dp", "mp"),
        P("dp", None),
        P("dp"),
        P("dp"),
        P(None, "mp", None),
        P(None, "mp"),
        P(None, "mp"),
        P("mp"),
        P("mp", None),
        P("mp"),
        P("mp"),
    )
    out_specs = (
        P(),
        P("dp"),
        P("dp", "mp"),
        P(None, "mp", None),
        P(None, "mp"),
        P(None, "mp"),
        P("mp"),
        P("mp", None),
        P("mp"),
        P("mp"),
        P(),
        P(),
    )
    return jax.shard_map(
        per_device, mesh=mesh, in_specs=in_specs, out_specs=out_specs, check_vma=False
    )
```

```python
import functools

import jax
import jax.numpy as jnp
from jax import lax
from jax.experimental import pallas as pl
from jax.experimental.pallas import tpu as pltpu
from jax.sharding import PartitionSpec as P

DAYS = 24
BUCKETS = 128
BF16 = jnp.bfloat16
F32 = jnp.float32
MAIN = 256
SHARE = 32
HALF = MAIN // 2
LANES = 128
APART = 64
LOSS = 24
COUNT = 16
VMEM = pl.BlockSpec(memory_space=pltpu.VMEM)
SMEM = pl.BlockSpec(memory_space=pltpu.SMEM)
HBM = pl.BlockSpec(memory_space=pl.ANY)
FAR = pl.BlockSpec(memory_space=pltpu.HBM)
NT = (((1,), (1,)), ((), ()))
TN = (((0,), (0,)), ((), ()))
NN = (((1,), (0,)), ((), ()))


def gelu_parts(values):
    cdf_part = 0.5 * (1.0 + lax.erf(values * 0.7071067811865476))
    slope = cdf_part + values * jnp.exp(-0.5 * values * values) * 0.3989422804014327
    return (values * cdf_part, slope)


def dot(lhs, rhs, dims, precision=None):
    return lax.dot_general(lhs, rhs, dims, preferred_element_type=F32, precision=precision)


def call(kernel, outs, scratch, args, mib, spec=VMEM, copies=0, out_spec=None, aliases={}, flops=0, nbytes=0):
    arrays = [a[0] if isinstance(a, tuple) else a for a in args[1:]]
    specs = [a[1] if isinstance(a, tuple) else spec for a in args[1:]]
    if copies:
        scratch = scratch + [pltpu.SemaphoreType.DMA((copies,))]
    return pl.pallas_call(
        kernel,
        out_shape=outs,
        in_specs=[SMEM] + specs,
        out_specs=out_spec or jax.tree.map(lambda _: spec, outs),
        scratch_shapes=scratch,
        input_output_aliases=aliases,
        compiler_params=pltpu.CompilerParams(vmem_limit_bytes=mib << 20),
        cost_estimate=pl.CostEstimate(flops=flops, bytes_accessed=nbytes, transcendentals=0),
    )(args[0], *arrays)


class Copies:
    def __init__(self, sems):
        self.sems, self.count = sems, 0

    def start(self, source, target):
        copy = pltpu.make_async_copy(source, target, self.sems.at[self.count])
        self.count += 1
        copy.start()
        return copy


def wait(*copies):
    for copy in copies:
        copy.wait()


def after(value, *others):
    return lax.optimization_barrier((value,) + others)[0]


def places(idx):
    core, plane = idx[1], idx[2]
    first, second = core + 1, 2 - core
    mine = [plane, plane ^ first, plane ^ second, plane ^ 3]
    theirs = [plane, plane ^ second, plane ^ first, plane ^ 3]
    return [core * HALF + SHARE * q for q in mine] + [(1 - core) * HALF + SHARE * q for q in theirs]


def relative(idx):
    core, plane = idx[1], idx[2]
    first, second = core + 1, 2 - core
    return [plane, plane ^ second, plane ^ first, plane ^ 3]


def block_of(idx, turn, blocks):
    return lax.rem(idx[0] - turn + blocks, blocks)


def block_ahead(idx, turn, blocks):
    return lax.rem(idx[0] + turn, blocks)


def rows_at(offset, size, unit=16):
    return pl.ds(pl.multiple_of(offset, unit), size)


def split3(line):
    high = line.astype(BF16).astype(F32)
    middle = (line - high).astype(BF16).astype(F32)
    return high, middle, line - high - middle


def lane_of(shape):
    return lax.broadcasted_iota(jnp.int32, shape, 1)


def pack_rest(idx, weight, bias, inputs, vectors, weight1, weight2, ids, days, *refs, blocks):
    out, own1, tally = refs[:3]
    chunks, (lines,) = refs[3 : 3 + blocks], refs[3 + blocks :]
    layers, width, depth = weight.shape
    size = weight2.shape[0]
    left = width - MAIN
    part = chunks[0].shape[1]
    full = own1.shape[1]
    own_row = idx[1] * HALF + idx[2] * SHARE

    lines[...] = jnp.zeros_like(lines)
    for layer in range(layers):
        lines[left * layer : left * (layer + 1), 0:depth] = weight[layer, MAIN:width, :].astype(F32)
        at = left * layers + layer
        lines[at : at + 1, 0:width] = bias[layer : layer + 1, :].astype(F32)
    rest = [lines[:, at : at + part].astype(BF16) for at in range(0, lines.shape[1], part)]

    own1[:, 0:depth] = weight1[...].T
    own1[:, depth:] = jnp.zeros((size, full - depth), BF16)
    out[:, 0:full] = own1[rows_at(own_row, SHARE), :]
    out[:, full:] = weight2[rows_at(own_row, SHARE), :]

    first = 16 * len(rest)
    for turn in range(blocks):
        lanes = pl.ds(pl.multiple_of(block_ahead(idx, turn, blocks) * part, LANES), part)
        for at, value in enumerate(rest):
            chunks[turn][16 * at : 16 * (at + 1), :] = value
        chunks[turn][first : first + width, :] = inputs[:, lanes]
        chunks[turn][first + width : first + width + 3, :] = vectors[...]

    fields, tokens = ids.shape
    bucket = lax.broadcasted_iota(jnp.int32, (BUCKETS, tokens), 0)
    lane = lane_of((BUCKETS, LANES))
    tile = jnp.zeros((BUCKETS, LANES), F32)
    for field in range(fields + 1):
        line = ids[field : field + 1, :] if field < fields else days[...]
        hits = jnp.sum((bucket == line).astype(F32), axis=1, keepdims=True)
        high = jnp.floor(hits * (1.0 / 256.0))
        tile = jnp.where(lane == COUNT + field, high, tile)
        tile = jnp.where(lane == COUNT + fields + 1 + field, hits - 256.0 * high, tile)
    half = BUCKETS // 2
    tile = tile[0:half, :] + pltpu.roll(tile[half:, :], 2 * (fields + 1), 1)
    tally[0:half, :] = tile.astype(BF16)
    tally[half:, :] = jnp.zeros((tally.shape[0] - half, LANES), BF16)


def cross_eight(refs):
    near, last, near_far, last_far = refs
    return [near.at[at] for at in range(3)] + [last] + [near_far.at[at] for at in range(3)] + [last_far]


def place_cross(idx, weight, own, slices, blocks, layer, pad):
    layers, depth = weight.shape[0], weight.shape[2]
    low = depth // LANES * LANES
    weight[layer, rows_at(idx[0] * pad, MAIN), :] = own[layer, 0:MAIN, :]
    tail = layers * low + (depth - low) * layer
    for turn in range(1, blocks):
        base = block_of(idx, turn, blocks) * pad
        for offset, piece in zip(places(idx), slices):
            rows = rows_at(base + offset, SHARE)
            weight[layer, rows, 0:low] = piece[turn - 1, :, low * layer : low * (layer + 1)]
            weight[layer, rows, low:] = piece[turn - 1, :, tail : tail + depth - low]


def place_rest(idx, weight, pieces, lines, tail, layers, left, pad):
    blocks = len(pieces)
    depth = weight.shape[2]
    part = pieces[0].shape[1]
    tail[...] = jnp.zeros_like(tail)
    for turn, piece in enumerate(pieces):
        for group in range(-(-depth // part)):
            stop = min(depth, part * (group + 1))
            lines[block_of(idx, turn, blocks), :, part * group : stop] = piece[
                16 * group : 16 * (group + 1), 0 : stop - part * group
            ].astype(F32)
    for block in range(blocks):
        for layer in range(layers):
            tail[0:left, :] = lines[block, left * layer : left * (layer + 1), :]
            at = pad * block + MAIN
            weight[layer, at : at + 16, :] = tail[...].astype(BF16)


def cross_forward(idx, *refs, blocks, layers, width, pad, depth):
    pieces, refs = refs[:blocks], refs[blocks:]
    own, refs = refs[0], refs[1:]
    slices, refs = cross_eight(refs[:4]), refs[4:]
    z_out, x_out, weight, lines, tail, start, state, nat = refs
    left = width - MAIN
    place_rest(idx, weight, pieces, lines, tail, layers, left, pad)
    at = 16 * -(-depth // pieces[0].shape[1])
    bias = [lines[block, :, 0:384].T for block in range(blocks)]
    for turn, piece in enumerate(pieces):
        block = block_of(idx, turn, blocks)
        start[block, 0:width, :] = piece[at : at + width, :].astype(F32)
        start[block, width:, :] = jnp.zeros((pad - width, piece.shape[1]), F32)
    full = nat.shape[0]
    ones = lax.broadcasted_iota(jnp.int32, (full - depth, nat.shape[1]), 0) == 0
    nat[depth:full, :] = ones.astype(F32)
    for block in range(blocks):
        nat[width * block : width * (block + 1), :] = start[block, 0:width, :]
    for layer in range(layers):
        x_out[layer] = nat[...].astype(BF16)
        place_cross(idx, weight, own, slices, blocks, layer, pad)
        at = left * layers + layer
        for block in range(blocks):
            rows = slice(pad * block, pad * (block + 1))
            value = dot(weight[layer, rows, :], x_out[layer, 0:depth, :], NN) + bias[block][0:pad, at : at + 1]
            z_out[layer, rows, :] = value
            before = start[block] if layer == 0 else state[block]
            value = start[block] * value + before
            state[block] = value
            nat[width * block : width * (block + 1), :] = value[0:width, :]
    x_out[layers] = nat[...].astype(BF16)


def tower_both(idx, *refs, blocks, layers, width, depth, fields, examples):
    (labels, day_ids), refs = refs[:2], refs[2:]
    pieces, refs = refs[:blocks], refs[blocks:]
    (own1, own2), refs = refs[:2], refs[2:]
    slices, refs = refs[:8], refs[8:]
    x_all, acts, far, heads, tower, lines_out, day_out, field_out = refs[:8]
    inputs, slope1, act2, headed, vectors = refs[8:]
    hidden = tower.shape[0]
    full = x_all.shape[1]
    size = hidden // blocks
    part = x_all.shape[2]
    low = depth // LANES * LANES
    at = 16 * -(-depth // part) + width
    for turn, piece in enumerate(pieces):
        inputs[block_of(idx, turn, blocks)] = piece[at : at + 3, :].astype(F32)
    base = idx[0] * size
    tower[rows_at(base, size), 0:full] = own1[...]
    tower[rows_at(base, size), full:] = own2[...]
    for turn in range(1, blocks):
        base = block_of(idx, turn, blocks) * size
        for offset, piece in zip(places(idx), slices):
            rows = rows_at(base + offset, SHARE)
            tower[rows, :] = piece[turn - 1, :, piece.shape[2] - tower.shape[1] :]
    parts = [slice(size * block, size * (block + 1)) for block in range(blocks)]
    columns = []
    for block in range(blocks):
        vectors[0:3, :] = inputs[block]
        columns.append(vectors[...].T)
    for rows, column in zip(parts, columns):
        act, slope = gelu_parts(dot(tower[rows, 0:depth], x_all[layers, 0:depth, :], NN) + column[:, 0:1])
        acts[0, rows, :] = act.astype(BF16)
        slope1[rows, :] = slope
    logits = jnp.zeros((1, part), F32)
    for rows, column in zip(parts, columns):
        act, slope = gelu_parts(dot(tower[:, full + rows.start : full + rows.stop], acts[0], TN) + column[:, 2:3])
        act2[rows, :] = act
        headed[rows, :] = column[:, 1:2] * slope
        logits += jnp.sum(act * column[:, 1:2], axis=0, keepdims=True)

    half = BUCKETS // 2
    tally = jnp.zeros((half, LANES), F32)
    for piece in slices:
        at = piece.shape[2] - tower.shape[1] + low
        tally += piece[0 : half // SHARE, :, at : at + LANES].astype(F32).reshape(half, LANES)
    count = jnp.concatenate([tally, pltpu.roll(tally, LANES - 2 * (fields + 1), 1)], axis=0)
    high = count[:, COUNT : COUNT + fields + 1]
    count = 256.0 * high + count[:, COUNT + fields + 1 : COUNT + 2 * (fields + 1)]
    days = count[0:32, fields : fields + 1]
    padded = jnp.concatenate([count, jnp.zeros((BUCKETS, LANES - fields - 1), F32)], axis=1).T
    field_out[...] = padded[0:fields, :].astype(jnp.int32)
    day_out[...] = padded[fields : fields + 1, :].astype(jnp.int32)

    mine = pl.ds(pl.multiple_of(idx[0] * part, LANES), part)
    lab = labels[:, mine].astype(F32)
    table = (lax.broadcasted_iota(jnp.int32, (32, part), 0) == day_ids[:, mine]).astype(F32)
    share = examples / (DAYS * jnp.maximum(days, 1.0))
    weights = jnp.sum(table * share, axis=0, keepdims=True)
    decay = jnp.exp(-jnp.abs(logits))
    loss = jnp.maximum(logits, 0.0) + jnp.log1p(decay) - lab * logits
    sigmoid = jnp.where(logits >= 0.0, 1.0, decay) / (1.0 + decay)
    dl = weights * (sigmoid - lab)
    losses = dot(jnp.broadcast_to(loss, (8, part)), table, NT, lax.Precision.HIGHEST)[0:1, :]
    lines_out[0:1, :] = logits
    lines_out[1:2, :] = jnp.zeros_like(logits)
    lines_out[1:2, 0 : losses.shape[1]] = losses

    acts[1] = (dl * headed[...]).astype(BF16)
    far[0:hidden, :] = acts[1]
    for rows in parts:
        acts[2, rows, :] = (dot(tower[rows, full:], acts[1], NN) * slope1[rows, :]).astype(BF16)
    for block in range(blocks):
        rows = rows_at(block * size + (1 - idx[1]) * HALF, HALF)
        at = hidden + HALF * block
        far[at : at + HALF, :] = acts[0, rows, :]
        at = hidden + HALF * (block + blocks)
        far[at : at + HALF, :] = acts[2, rows, :]
    for rows in parts:
        heads[rows, :] = jnp.broadcast_to(jnp.sum(act2[rows, :] * dl, axis=1, keepdims=True), (size, LANES))


def cross_backward(idx, *refs, blocks, layers, width, pad, depth):
    extra_lines, refs = refs[0], refs[1:]
    pieces, refs = refs[:blocks], refs[blocks:]
    own, refs = refs[0], refs[1:]
    slices, refs = cross_eight(refs[:4]), refs[4:]
    (tower, acts, z_all), refs = refs[:3], refs[3:]
    eg_out, refs = refs[:blocks], refs[blocks:]
    dz_out, rest_out, dz_far_last, dz_far_out = refs[:4]
    weight, inputs, lines, tail, flow, padded, total, rest = refs[4:]
    left = width - MAIN
    place_rest(idx, weight, pieces, lines, tail, layers, left, pad)
    at = 16 * -(-depth // pieces[0].shape[1])
    for turn, piece in enumerate(pieces):
        inputs[block_of(idx, turn, blocks)] = piece[at : at + width, :].astype(F32)
    flow[...] = dot(tower[:, 0:depth], acts[2], TN)
    padded[...] = jnp.zeros_like(padded)
    rest[...] = jnp.zeros_like(rest)
    for layer in reversed(range(layers)):
        for block in range(blocks):
            rows = slice(pad * block, pad * (block + 1))
            dx = flow[width * block : width * (block + 1), :]
            padded[block, 0:width, :] = dx
            dx = padded[block, 0:width, :]
            dz = dx * inputs[block]
            term = dx * z_all[layer, pad * block : pad * block + width, :]
            total[block, 0:width, :] = term if layer == layers - 1 else total[block, 0:width, :] + term
            rest[left * block : left * (block + 1), :] = dz[MAIN:width, :]
            padded[block, 0:width, :] = dz
            dz_out[layer, rows, :] = padded[block].astype(BF16)
        rest_out[layer] = rest[...].astype(BF16)
        far = dz_far_last.at[0] if layer == layers - 1 else dz_far_out.at[layer]
        far[HALF * blocks :, :] = rest[...].astype(BF16)
        for block in range(blocks):
            rows = rows_at(pad * block + (1 - idx[1]) * HALF, HALF)
            far[HALF * block : HALF * (block + 1), :] = dz_out[layer, rows, :]
        place_cross(idx, weight, own, slices, blocks, layer, pad)
        flow[...] += dot(weight[layer], dz_out[layer], TN)
    extras = split3(extra_lines[0:1, :]) + split3(extra_lines[1:2, :])
    for block in range(blocks):
        total[block, 0:width, :] += flow[width * block : width * (block + 1), :]
        total[block, width:, :] = jnp.zeros((pad - width, flow.shape[1]), F32)
        for at, extra in enumerate(extras):
            total[block, width + at : width + at + 1, :] = extra
    for turn in range(blocks):
        eg_out[turn][...] = total[block_ahead(idx, turn, blocks)].astype(BF16)


def tower_grads(idx, x_all, x_far, acts, far, head, *refs, blocks, depth, layers, wheres):
    outs = refs[: 1 + (0 in wheres)]
    x_cat, acts_in, far_in, heads, lhs, d_cat = refs[len(outs) : len(outs) + 6]
    holds, sems = refs[len(outs) + 6 : -1], refs[-1]
    hidden = acts.shape[1]
    size = hidden // blocks
    part = acts.shape[2]
    low = depth // LANES * LANES
    bias = depth - low
    copies = Copies(sems)
    first = [
        copies.start(acts, acts_in),
        copies.start(far, far_in),
        copies.start(x_all.at[layers], x_cat.at[:, 0:part]),
        copies.start(x_far.at[layers], x_cat.at[:, part : 2 * part]),
        copies.start(head, heads),
    ]
    wait(*first)
    lane = lane_of((SHARE, LANES))
    pick = (lax.broadcasted_iota(jnp.int32, (LANES, 2 * part), 0) == bias + 1).astype(BF16)
    order = [(where, slot) for where in wheres for slot in range(blocks)]
    shares = relative(idx)
    d_cat[:, 0:part] = acts_in[1]
    d_cat[:, part:] = far_in[0:hidden, :]
    scale = []
    for at, (where, slot) in enumerate(order):
        block = block_ahead(idx, slot, blocks)
        rows = rows_at(block * size + idx[1] * HALF + SHARE * shares[where], SHARE)
        other = rows_at(block * size + (1 - idx[1]) * HALF + SHARE * shares[where], SHARE)
        lines = rows_at(hidden + HALF * block + SHARE * shares[where], SHARE)
        after_it = rows_at(hidden + HALF * (block + blocks) + SHARE * shares[where], SHARE)
        here = slice(SHARE * at, SHARE * (at + 1))
        lhs[0, here, 0:part] = acts_in[2, rows, :]
        lhs[0, here, part:] = far_in[after_it, :]
        lhs[1, here, 0:part] = acts_in[0, rows, :]
        lhs[1, here, part:] = far_in[lines, :]
        lhs[2, here, 0:part] = acts_in[1, rows, :]
        lhs[2, here, part:] = far_in[rows, :]
        scale.append(
            jnp.where(lane == bias + 2, heads[rows, :], 0.0) + jnp.where(lane == bias + 3, heads[other, :], 0.0)
        )
    extra = dot(lhs[2], pick, NT)
    wide = dot(lhs[0], x_cat[...], NT)
    deep = dot(lhs[1], d_cat[...], NT)
    for at, (where, slot) in enumerate(order):
        target = (holds[where] if 0 in wheres else holds[0].at[where - 2]).at[slot]
        here = slice(SHARE * at, SHARE * (at + 1))
        target[:, 0:low] = wide[here, 0:low].astype(BF16)
        target[:, low : low + LANES] = (wide[here, low:] + extra[here, :] + scale[at]).astype(BF16)
        target[:, low + LANES :] = deep[here, :].astype(BF16)
    wait(*[copies.start(hold, out) for hold, out in zip(holds, outs)])


def cross_grads(idx, x_all, x_far, dz, rest, dz_far, near_out, far_out, send_out, *refs, blocks, base, pad, depth):
    x_cat, dz_in, far_in, rest_in, lhs, few, extra, tiles, near, away, send, sems = refs
    part = dz.shape[2]
    low = depth // LANES * LANES
    groups = -(-depth // MAIN)
    count = dz_far.shape[0]
    left = rest_in.shape[1] // blocks
    copies = Copies(sems)
    first = []
    for layer in reversed(range(count)):
        first.append(
            [
                copies.start(dz.at[base + layer], dz_in.at[layer]),
                copies.start(dz_far.at[layer], far_in.at[layer]),
                copies.start(rest.at[base + layer], rest_in.at[layer]),
                copies.start(x_all.at[base + layer], x_cat.at[layer, :, 0:part]),
                copies.start(x_far.at[base + layer], x_cat.at[layer, :, part : 2 * part]),
            ]
        )
    few[...] = jnp.zeros_like(few)
    order = [(where, slot) for where in range(4) for slot in range(blocks)]
    shares = relative(idx)
    lane = lane_of((HALF, LANES))
    bias = depth - low
    span = left * groups
    for layer, started in zip(reversed(range(count)), first):
        wait(*started)
        value = jnp.zeros((HALF, LANES), F32)
        near_rest = rest_in[layer].astype(F32)
        far_rest = far_in[layer, HALF * blocks :, :].astype(F32)
        for group in range(groups):
            for block in range(blocks):
                lines = slice(span * block + left * group, span * block + left * (group + 1))
                few[group, lines, 0:part] = near_rest[left * block : left * (block + 1), :]
                few[group, lines, part:] = far_rest[left * block : left * (block + 1), :]
            if MAIN * (group + 1) <= depth:
                rows = rows_at(MAIN * group + idx[1] * HALF, HALF)
            else:
                rows = slice(MAIN * group, MAIN * group + HALF)
            value += dot(x_cat[layer, rows, :], few[group].astype(BF16), NT)
        inside = (lane > bias) & (lane <= bias + span)
        for block in range(blocks):
            extra[block] = jnp.where(inside, pltpu.roll(value, (bias + 1 - span * block) % LANES, 1), 0.0)
        for at, (where, slot) in enumerate(order):
            block = block_ahead(idx, slot, blocks)
            rows = rows_at(pad * block + idx[1] * HALF + SHARE * shares[where], SHARE)
            lines = rows_at(HALF * block + SHARE * shares[where], SHARE)
            here = slice(SHARE * at, SHARE * (at + 1))
            lhs[here, 0:part] = dz_in[layer, rows, :]
            lhs[here, part:] = far_in[layer, lines, :]
        grad = dot(lhs[...], x_cat[layer], NT)
        for at, (where, slot) in enumerate(order):
            target = (near, away, send.at[0], send.at[1])[where].at[slot]
            here = slice(SHARE * at, SHARE * (at + 1))
            target[:, low * layer : low * (layer + 1)] = grad[here, 0:low].astype(BF16)
            tile = grad[here, low:] + extra[block_ahead(idx, slot, blocks), rows_at(SHARE * shares[where], SHARE), :]
            if layer < count - 1:
                tile = tiles[here, :] + (pltpu.roll(tile, APART * layer, 1) if layer else tile)
            elif layer:
                tile = pltpu.roll(tile, APART * layer, 1)
            if layer:
                tiles[here, :] = tile
            else:
                target[:, low * count :] = tile.astype(BF16)
    wait(copies.start(send, send_out), copies.start(near, near_out), copies.start(away, far_out))


def eight(mine, one, two, far):
    return [mine, one, two.at[0], two.at[1]] + [far.at[at] for at in range(4)]


def finish_input(idx, *refs, blocks):
    pieces, (out, logits, losses, day_held) = refs[:blocks], refs[blocks:]
    width = out.shape[0]
    size = pieces[0].shape[1]
    for turn, piece in enumerate(pieces):
        block = block_of(idx, turn, blocks)
        lanes = pl.ds(pl.multiple_of(block * size, LANES), size)
        values = piece[...].astype(F32)
        line = lambda at: values[width + at : width + at + 1, :]
        out[:, lanes] = values[0:width, :]
        logits[:, lanes] = line(0) + line(1) + line(2)
        day_held[block] = jnp.broadcast_to(line(3) + line(4) + line(5), day_held.shape[1:])
    days = day_held[0]
    for block in range(1, blocks):
        days += day_held[block]
    row = lax.broadcasted_iota(jnp.int32, losses.shape, 0)
    tile = jnp.zeros(losses.shape, F32)
    for at, value in enumerate(split3(days[0:1, 0:LANES])):
        tile = jnp.where(row == at, value, tile)
    losses[...] = jnp.where(lane_of(tile.shape) < LOSS, 0.0, pltpu.roll(tile, LOSS, 1))


def finish_tower(idx, *refs, depth):
    slices, (counts, out1, out2, rows_out, mean_out, lines, day_held) = eight(*refs[:4]), refs[4:]
    low = depth // LANES * LANES
    size = out2.shape[0]
    for offset, piece in zip(places(idx), slices):
        lines[rows_at(offset, SHARE), :] = piece[:, 0 : low + LANES].astype(F32)
        out2[rows_at(offset, SHARE), :] = piece[:, low + LANES :].astype(F32)
        tile = piece[0:16, low : low + LANES].astype(F32)
        day_held[lax.div(offset, SHARE)] = tile[0:1, :] + tile[1:2, :] + tile[2:3, :]
    turned = lines[...].T
    out1[...] = turned[0:depth, :]
    head = turned[depth + 3 : depth + 4, :]
    rows_out[0:1, :] = turned[depth : depth + 1, :]
    rows_out[1:2, :] = turned[depth + 1 : depth + 2, :]
    rows_out[2:3, 0:HALF] = turned[depth + 2 : depth + 3, 0:HALF] + head[:, HALF:]
    rows_out[2:3, HALF:] = turned[depth + 2 : depth + 3, HALF:] + head[:, 0:HALF]
    days = day_held[0]
    for at in range(1, day_held.shape[0]):
        days += day_held[at]
    days = days[:, LOSS : LOSS + DAYS]
    mean = days / jnp.maximum(counts[:, 0:DAYS].astype(F32), 1.0)
    mean_out[...] = jnp.sum(mean, axis=1, keepdims=True) / DAYS


def finish_cross(idx, *refs, blocks, base, more):
    slices, refs = eight(*refs[:4]), refs[4:]
    before, (out, bias_out, held, lines, sems) = refs[:more], refs[more:]
    count, width, depth = held.shape
    left = width - MAIN
    low = depth // LANES * LANES
    copies = Copies(sems)
    last = []
    if more:
        bias_out[count:, :] = before[1][...]
    for offset, piece in zip(places(idx), slices):
        lines[rows_at(offset, SHARE), :] = piece[:, low * count :].astype(F32)
    turned = lines[...].T
    for layer in range(count):
        for offset, piece in zip(places(idx), slices):
            rows = rows_at(offset, SHARE)
            held[layer, rows, 0:low] = piece[:, low * layer : low * (layer + 1)].astype(F32)
        held[layer, 0:MAIN, low:] = lines[:, APART * layer : APART * layer + depth - low]
        bias = APART * layer + depth - low
        bias_out[layer : layer + 1, 0:MAIN] = turned[bias : bias + 1, :]
        for group in range(-(-depth // MAIN)):
            rest = turned[bias + 1 + left * group : bias + 1 + left * (group + 1), :]
            stop = min(depth, MAIN * (group + 1)) - MAIN * group
            held[layer, MAIN:width, MAIN * group : MAIN * group + stop] = rest[:, 0:stop]
        last.append(copies.start(held.at[layer], out.at[base + layer]))
        corner = jnp.broadcast_to(rest[:, stop : stop + 1], (left, LANES))
        ahead = lax.broadcasted_iota(jnp.int32, (left, LANES), 0) == lane_of((left, LANES))
        line = jnp.sum(jnp.where(ahead, corner, 0.0), axis=0, keepdims=True)
        bias_out[layer : layer + 1, MAIN:width] = line[:, 0:left]
    wait(*last)


def per_device(
    embedded,
    feature_ids,
    day_ids,
    labels,
    cross_weight,
    cross_bias,
    tower1,
    tower1_bias,
    tower2,
    tower2_bias,
    head_weight,
):
    blocks = lax.axis_size("mp")
    groups = lax.axis_size("dp")
    tokens, width = embedded.shape
    layers, _, depth = cross_weight.shape
    size, hidden = tower2.shape
    pad = -(-width // 16) * 16
    full = -(-(depth + 3) // LANES) * LANES
    part = tokens // blocks
    examples = tokens * groups
    flat = blocks * pad
    shape = jax.ShapeDtypeStruct
    vmem = pltpu.VMEM

    me = lax.axis_index("mp")
    group = lax.axis_index("dp")
    core, plane = group & 1, (group >> 1) & 3
    idx = jnp.stack([me, core, plane, group & 7]).astype(jnp.int32)
    swap = lambda bits: [(i, i ^ bits(i)) for i in range(groups)]
    first = swap(lambda i: 4 if i & 1 else 2)
    second = swap(lambda i: 2 if i & 1 else 4)
    pair = swap(lambda i: 1)
    others = [swap(lambda i, b=b: 1 << b) for b in range(3, groups.bit_length() - 1)]
    turn_by = lambda r: [(i, (i + r) % blocks) for i in range(blocks)]
    hop = lambda value, perm: lax.ppermute(value, "dp", perm)
    turns = lambda values: [
        lax.ppermute(value, "mp", turn_by(r + 1)) for r, value in enumerate(values)
    ]

    own_row = core * HALF + plane * SHARE
    cross_send = lax.dynamic_slice(cross_weight, (0, own_row, 0), (layers, SHARE, depth))
    low = depth // LANES * LANES
    fill = jnp.zeros((SHARE, LANES - layers * (depth - low)), BF16)
    cross_send = jnp.concatenate([rows[:, :low] for rows in cross_send] + [rows[:, low:] for rows in cross_send] + [fill], axis=1)
    cross_turned = turns([cross_send] * (blocks - 1))
    vectors = jnp.stack([tower1_bias, head_weight, tower2_bias])
    wide = full + hidden
    groups_of = -(-depth // part)
    tower_send, tower_own, tally, *chunks = call(
        functools.partial(pack_rest, blocks=blocks),
        tuple(
            [
                shape((SHARE, wide), BF16),
                shape((size, full), BF16),
                shape(((blocks - 1) * SHARE, LANES), BF16),
            ]
            + [shape((16 * groups_of + width + 3, part), BF16)] * blocks
        ),
        [vmem((16, groups_of * part), F32)],
        [
            after(idx, cross_send),
            cross_weight,
            cross_bias,
            embedded.T,
            vectors,
            tower1,
            tower2,
            feature_ids.T,
            day_ids[None, :],
        ],
        mib=24,
        nbytes=2 << 20,
    )
    for perm in others:
        tally = tally + hop(tally, perm)
    tally = jnp.pad(tally.reshape(blocks - 1, SHARE, LANES), ((0, 0), (0, 0), (full - LANES, hidden)))

    join = lambda *values: lax.optimization_barrier(values)
    cross_mine = jnp.stack(cross_turned)
    cross_mine, tower_send, *chunks = join(cross_mine, tower_send, *chunks)
    cross_one, cross_two = hop(cross_mine, first), hop(cross_mine, second)
    tower_turned = turns([tower_send] * (blocks - 1))
    cross_one, cross_two, *tower_turned = join(cross_one, cross_two, *tower_turned)

    turn = lambda value, r: lax.ppermute(value, "mp", turn_by(r))
    pieces = [chunks[0]] + [turn(after(chunks[r], tower_turned[0]), r) for r in range(1, blocks - 1)]
    tower_mine = jnp.stack(tower_turned) + tally
    both = jnp.concatenate([cross_one, tower_mine], axis=2)
    tower_one, both = hop(tower_mine, first), hop(both, second)
    cross_near = jnp.stack([cross_mine, cross_one, cross_two])
    cross_far = hop(cross_near, pair)
    pieces.append(turn(after(chunks[-1], cross_far), blocks - 1))
    both, tower_one, cross_far, *pieces = join(both, tower_one, cross_far, *pieces)

    tower_three = hop(tower_one, second)
    both_far, tower_far, tower_next = hop(both, pair), hop(tower_mine, pair), hop(tower_one, pair)
    both_far, tower_far, tower_next = join(both_far, tower_far, tower_next)
    cross_slices = [cross_near, both, cross_far, both_far]

    z_all, x_all = call(
        functools.partial(cross_forward, blocks=blocks, layers=layers, width=width, pad=pad, depth=depth),
        (shape((layers, flat, part), F32), shape((layers + 1, full, part), BF16)),
        [
            vmem((layers, flat, depth), BF16),
            vmem((blocks, 16, depth), F32),
            vmem((16, depth), F32),
            vmem((blocks, pad, part), F32),
            vmem((blocks, pad, part), F32),
            vmem((full, part), F32),
        ],
        [idx, *pieces, cross_weight, *cross_slices],
        mib=28,
        flops=2 * layers * flat * full * part,
        nbytes=20 << 20,
    )
    tower_last = hop(after(tower_three, z_all), pair)
    tower_slices = [tower_mine, tower_one, both, tower_three, tower_far, tower_next, both_far, tower_last]
    x_far = hop(after(x_all, tower_last), pair)
    fields = feature_ids.shape[1]
    acts, far, head_col, tower_all, lines, day_line, field_counts = call(
        functools.partial(
            tower_both, blocks=blocks, layers=layers, width=width, depth=depth, fields=fields, examples=examples
        ),
        (
            shape((3, hidden, part), BF16),
            shape((2 * hidden, part), BF16),
            shape((hidden, LANES), F32),
            shape((hidden, wide), BF16),
            shape((2, part), F32),
            shape((1, BUCKETS), jnp.int32),
            shape((fields, BUCKETS), jnp.int32),
        ),
        [
            vmem((blocks, 3, part), F32),
            vmem((hidden, part), F32),
            vmem((hidden, part), F32),
            vmem((hidden, part), F32),
            vmem((8, part), F32),
        ],
        [
            idx,
            labels[None, :],
            day_ids[None, :],
            *pieces,
            tower_own,
            tower2,
            *tower_slices,
            x_all,
        ],
        mib=28,
        flops=8 * hidden * full * part,
        nbytes=10 << 20,
    )
    far = hop(far, pair)

    def grads(kernel, keep, scratch, args, copies, flops):
        outs = keep, keep, (2,) + keep
        return call(
            kernel,
            tuple(shape(s, BF16) for s in outs),
            scratch + [vmem(s, BF16) for s in outs],
            args,
            mib=20,
            spec=HBM,
            copies=copies,
            flops=flops,
            nbytes=10 << 20,
        )

    def tower_parts_of(wheres, outs, start):
        return call(
            functools.partial(tower_grads, blocks=blocks, depth=depth, layers=layers, wheres=wheres),
            tuple(shape(s, BF16) for s in outs),
            [
                vmem((full, 2 * part), BF16),
                vmem((3, hidden, part), BF16),
                vmem((2 * hidden, part), BF16),
                vmem((hidden, LANES), F32),
                vmem((3, HALF * blocks // 2, 2 * part), BF16),
                vmem((hidden, 2 * part), BF16),
            ]
            + [vmem(s, BF16) for s in outs],
            [start, x_all, x_far, acts, far, head_col],
            mib=20,
            spec=HBM,
            copies=7,
            flops=2 * hidden * full * part,
            nbytes=10 << 20,
        )

    keep = (blocks, SHARE, wide)
    (tower_out,) = tower_parts_of((2, 3), [(2,) + keep], idx)
    tower_parts = [*tower_parts_of((0, 1), [keep, keep], after(idx, tower_out)), tower_out]
    tower_arrived = hop(tower_parts[2], first)
    *input_grads, dz, dz_rest, last_far, dz_far = call(
        functools.partial(cross_backward, blocks=blocks, layers=layers, width=width, pad=pad, depth=depth),
        tuple([shape((pad, part), BF16)] * blocks)
        + (
            shape((layers, flat, part), BF16),
            shape((layers, 16, part), BF16),
            shape((1, HALF * blocks + 16, part), BF16),
            shape((layers - 1, HALF * blocks + 16, part), BF16),
        ),
        [
            vmem((layers, flat, depth), BF16),
            vmem((blocks, width, part), F32),
            vmem((blocks, 16, depth), F32),
            vmem((16, depth), F32),
            vmem((depth, part), F32),
            vmem((blocks, pad, part), F32),
            vmem((blocks, pad, part), F32),
            vmem((16, part), F32),
        ],
        [
            after(idx, tower_parts[2]),
            lines,
            *pieces,
            cross_weight,
            *cross_slices,
            tower_all,
            acts,
            z_all,
        ],
        mib=22,
        flops=2 * layers * flat * full * part,
        nbytes=20 << 20,
    )
    last_far = hop(last_far, pair)
    dz_far = hop(dz_far, pair)

    def cross_parts_of(base, count, far, start):
        return grads(
            functools.partial(cross_grads, blocks=blocks, base=base, pad=pad, depth=depth),
            (blocks, SHARE, count * low + LANES),
            [
                vmem((count, full, 2 * part), BF16),
                vmem((count, flat, part), BF16),
                vmem((count, HALF * blocks + 16, part), BF16),
                vmem((count, 16, part), BF16),
                vmem((HALF * blocks, 2 * part), BF16),
                vmem((-(-depth // MAIN), LANES, 2 * part), F32),
                vmem((blocks, HALF, LANES), F32),
                vmem((HALF * blocks, LANES), F32),
            ],
            [start, x_all, x_far, dz, dz_rest, far],
            5 * count + 3,
            2 * count * flat * full * part,
        )

    last_parts = cross_parts_of(layers - 1, 1, last_far, idx)
    cross_parts = cross_parts_of(0, layers - 1, dz_far, after(idx, last_parts[2]))

    down = lambda value: value.astype(BF16)
    up = lambda value: value.astype(F32)

    def near_sum(parts, arrived, last):
        return up(parts[0]) + up(arrived[0]) + up(last)

    def far_send(parts, arrived):
        return hop(down(up(parts[1]) + up(arrived[1])), second)

    def send_blocks(held):
        return turns([down(held[r]) for r in range(1, blocks)])

    def total_of(held, turned):
        held = held[0] + sum(up(value) for value in turned)
        for perm in others:
            held = held + hop(held, perm)
        return held

    def two_of(mine, one):
        return hop(jnp.stack([mine, one]), second)

    def far_of(mine, one, two):
        return hop(jnp.concatenate([jnp.stack([mine, one]), two]), pair)

    grad_pieces = [input_grads[0]] + turns(input_grads[1:])
    grad_pieces[1], tower_arrived, last_send = join(grad_pieces[1], tower_arrived, last_parts[2])
    tower_second = far_send(tower_parts, tower_arrived)
    last_arrived = hop(last_send, first)
    *grad_pieces, tower_second, last_arrived, cross_send = join(
        *grad_pieces, tower_second, last_arrived, cross_parts[2]
    )

    tower_held = near_sum(tower_parts, tower_arrived, tower_second)
    tower_turned = send_blocks(tower_held)
    last_second = far_send(last_parts, last_arrived)
    cross_arrived = hop(cross_send, first)
    input_out, logits_all, losses = call(
        functools.partial(finish_input, blocks=blocks),
        (shape((width, tokens), F32), shape((1, tokens), F32), shape((SHARE, LANES), F32)),
        [vmem((blocks, 8, part), F32)],
        [idx, *grad_pieces],
        mib=16,
        nbytes=2 << 20,
    )
    last_held = near_sum(last_parts, last_arrived, last_second)
    last_turned = send_blocks(last_held)
    cross_arrived, losses, last_turned[0], *tower_turned = join(
        cross_arrived, losses, last_turned[0], *tower_turned
    )

    last_turned[1:] = [after(value, last_turned[0]) for value in last_turned[1:]]
    cross_second = far_send(cross_parts, cross_arrived)
    tower_mine = down(total_of(tower_held, tower_turned) + jnp.pad(losses, ((0, 0), (full - LANES, hidden))))
    tower_one = hop(tower_mine, first)
    cross_second, tower_one, *last_turned = join(cross_second, tower_one, *last_turned)

    cross_held = near_sum(cross_parts, cross_arrived, cross_second)
    cross_turned = send_blocks(cross_held)
    tower_two = two_of(tower_mine, tower_one)
    last_mine = down(total_of(last_held, last_turned))
    last_one = hop(last_mine, first)
    tower_two, last_one, *cross_turned = join(tower_two, last_one, *cross_turned)

    cross_mine = down(total_of(cross_held, cross_turned))
    cross_one = hop(cross_mine, first)
    last_two = two_of(last_mine, last_one)
    tower_far = far_of(tower_mine, tower_one, tower_two)
    cross_one, last_two, tower_far = join(cross_one, last_two, tower_far)

    cross_two = two_of(cross_mine, cross_one)
    last_far = far_of(last_mine, last_one, last_two)
    tower_sums = [tower_mine, tower_one, tower_two, tower_far]
    last_sums = [last_mine, last_one, last_two, last_far]
    tower1_grad, tower2_grad, rows, mean = call(
        functools.partial(finish_tower, depth=depth),
        (shape((depth, size), F32), shape((size, hidden), F32), shape((3, size), F32), shape((1, 1), F32)),
        [vmem((size, full), F32), vmem((8, 1, LANES), F32)],
        [idx, *tower_sums, day_line],
        mib=16,
        nbytes=4 << 20,
    )
    def finish(sums, base, count, before):
        alias = {5: 0} if before else {}
        return call(
            functools.partial(finish_cross, blocks=blocks, base=base, more=len(before)),
            (shape((layers, width, depth), F32), shape((count + len(before) // 2, width), F32)),
            [vmem((count, width, depth), F32), vmem((MAIN, LANES), F32)],
            [idx, *sums] + [(value, spec) for value, spec in zip(before, (HBM, VMEM))],
            mib=16,
            out_spec=(HBM, VMEM),
            aliases=alias,
            copies=count,
            nbytes=4 << 20,
        )

    before = finish(last_sums, layers - 1, 1, ())
    cross_two, tower1_grad, before = join(cross_two, tower1_grad, before)
    cross_far = far_of(cross_mine, cross_one, cross_two)
    cross_grad, cross_bias_grad = finish([cross_mine, cross_one, cross_two, cross_far], 0, layers - 1, before)
    day_counts = day_line[0, :DAYS]
    return (
        mean[0, 0],
        logits_all[0],
        input_out.T,
        cross_grad,
        cross_bias_grad,
        tower1_grad,
        rows[0],
        tower2_grad,
        rows[1],
        rows[2],
        day_counts,
        field_counts,
    )


def solution(mesh):
    in_specs = (
        P("dp", "mp"),
        P("dp", None),
        P("dp"),
        P("dp"),
        P(None, "mp", None),
        P(None, "mp"),
        P(None, "mp"),
        P("mp"),
        P("mp", None),
        P("mp"),
        P("mp"),
    )
    out_specs = (
        P(),
        P("dp"),
        P("dp", "mp"),
        P(None, "mp", None),
        P(None, "mp"),
        P(None, "mp"),
        P("mp"),
        P("mp", None),
        P("mp"),
        P("mp"),
        P(),
        P(),
    )
    return jax.shard_map(
        per_device, mesh=mesh, in_specs=in_specs, out_specs=out_specs, check_vma=False
    )
```

```python
import functools

import jax
import jax.numpy as jnp
from jax import lax
from jax.experimental import pallas as pl
from jax.experimental.pallas import tpu as pltpu
from jax.sharding import PartitionSpec as P

DAYS = 24
BUCKETS = 128
BF16 = jnp.bfloat16
F32 = jnp.float32
MAIN = 256
SHARE = 32
HALF = MAIN // 2
LANES = 128
APART = 64
LOSS = 24
COUNT = 16
VMEM = pl.BlockSpec(memory_space=pltpu.VMEM)
SMEM = pl.BlockSpec(memory_space=pltpu.SMEM)
HBM = pl.BlockSpec(memory_space=pl.ANY)
FAR = pl.BlockSpec(memory_space=pltpu.HBM)
NT = (((1,), (1,)), ((), ()))
TN = (((0,), (0,)), ((), ()))
NN = (((1,), (0,)), ((), ()))


def gelu_parts(values):
    cdf_part = 0.5 * (1.0 + lax.erf(values * 0.7071067811865476))
    slope = cdf_part + values * jnp.exp(-0.5 * values * values) * 0.3989422804014327
    return (values * cdf_part, slope)


def dot(lhs, rhs, dims, precision=None):
    return lax.dot_general(lhs, rhs, dims, preferred_element_type=F32, precision=precision)


def call(kernel, outs, scratch, args, mib, spec=VMEM, copies=0, out_spec=None, aliases={}, flops=0, nbytes=0):
    arrays = [a[0] if isinstance(a, tuple) else a for a in args[1:]]
    specs = [a[1] if isinstance(a, tuple) else spec for a in args[1:]]
    if copies:
        scratch = scratch + [pltpu.SemaphoreType.DMA((copies,))]
    return pl.pallas_call(
        kernel,
        out_shape=outs,
        in_specs=[SMEM] + specs,
        out_specs=out_spec or jax.tree.map(lambda _: spec, outs),
        scratch_shapes=scratch,
        input_output_aliases=aliases,
        compiler_params=pltpu.CompilerParams(vmem_limit_bytes=mib << 20),
        cost_estimate=pl.CostEstimate(flops=flops, bytes_accessed=nbytes, transcendentals=0),
    )(args[0], *arrays)


class Copies:
    def __init__(self, sems):
        self.sems, self.count = sems, 0

    def start(self, source, target):
        copy = pltpu.make_async_copy(source, target, self.sems.at[self.count])
        self.count += 1
        copy.start()
        return copy


def wait(*copies):
    for copy in copies:
        copy.wait()


def after(value, *others):
    return lax.optimization_barrier((value,) + others)[0]


def places(idx):
    core, plane = idx[1], idx[2]
    first, second = core + 1, 2 - core
    mine = [plane, plane ^ first, plane ^ second, plane ^ 3]
    theirs = [plane, plane ^ second, plane ^ first, plane ^ 3]
    return [core * HALF + SHARE * q for q in mine] + [(1 - core) * HALF + SHARE * q for q in theirs]


def relative(idx):
    core, plane = idx[1], idx[2]
    first, second = core + 1, 2 - core
    return [plane, plane ^ second, plane ^ first, plane ^ 3]


def block_of(idx, turn, blocks):
    return lax.rem(idx[0] - turn + blocks, blocks)


def block_ahead(idx, turn, blocks):
    return lax.rem(idx[0] + turn, blocks)


def rows_at(offset, size, unit=16):
    return pl.ds(pl.multiple_of(offset, unit), size)


def split3(line):
    high = line.astype(BF16).astype(F32)
    middle = (line - high).astype(BF16).astype(F32)
    return high, middle, line - high - middle


def lane_of(shape):
    return lax.broadcasted_iota(jnp.int32, shape, 1)


def pack_rest(idx, weight, bias, inputs, vectors, weight1, weight2, ids, days, *refs, blocks):
    out, own1, tally = refs[:3]
    chunks, (lines,) = refs[3 : 3 + blocks], refs[3 + blocks :]
    layers, width, depth = weight.shape
    size = weight2.shape[0]
    left = width - MAIN
    part = chunks[0].shape[1]
    full = own1.shape[1]
    own_row = idx[1] * HALF + idx[2] * SHARE

    lines[...] = jnp.zeros_like(lines)
    for layer in range(layers):
        lines[left * layer : left * (layer + 1), 0:depth] = weight[layer, MAIN:width, :].astype(F32)
        at = left * layers + layer
        lines[at : at + 1, 0:width] = bias[layer : layer + 1, :].astype(F32)
    rest = [lines[:, at : at + part].astype(BF16) for at in range(0, lines.shape[1], part)]

    own1[:, 0:depth] = weight1[...].T
    own1[:, depth:] = jnp.zeros((size, full - depth), BF16)
    out[:, 0:full] = own1[rows_at(own_row, SHARE), :]
    out[:, full:] = weight2[rows_at(own_row, SHARE), :]

    first = 16 * len(rest)
    for turn in range(blocks):
        lanes = pl.ds(pl.multiple_of(block_ahead(idx, turn, blocks) * part, LANES), part)
        for at, value in enumerate(rest):
            chunks[turn][16 * at : 16 * (at + 1), :] = value
        chunks[turn][first : first + width, :] = inputs[:, lanes]
        chunks[turn][first + width : first + width + 3, :] = vectors[...]

    fields, tokens = ids.shape
    bucket = lax.broadcasted_iota(jnp.int32, (BUCKETS, tokens), 0)
    lane = lane_of((BUCKETS, LANES))
    tile = jnp.zeros((BUCKETS, LANES), F32)
    for field in range(fields + 1):
        line = ids[field : field + 1, :] if field < fields else days[...]
        hits = jnp.sum((bucket == line).astype(F32), axis=1, keepdims=True)
        high = jnp.floor(hits * (1.0 / 256.0))
        tile = jnp.where(lane == COUNT + field, high, tile)
        tile = jnp.where(lane == COUNT + fields + 1 + field, hits - 256.0 * high, tile)
    half = BUCKETS // 2
    tile = tile[0:half, :] + pltpu.roll(tile[half:, :], 2 * (fields + 1), 1)
    tally[0:half, :] = tile.astype(BF16)
    tally[half:, :] = jnp.zeros((tally.shape[0] - half, LANES), BF16)


def cross_eight(refs):
    near, last, near_far, last_far = refs
    return [near.at[at] for at in range(3)] + [last] + [near_far.at[at] for at in range(3)] + [last_far]


def place_cross(idx, weight, own, slices, blocks, layer, pad):
    layers, depth = weight.shape[0], weight.shape[2]
    low = depth // LANES * LANES
    weight[layer, rows_at(idx[0] * pad, MAIN), :] = own[layer, 0:MAIN, :]
    tail = layers * low + (depth - low) * layer
    for turn in range(1, blocks):
        base = block_of(idx, turn, blocks) * pad
        for offset, piece in zip(places(idx), slices):
            rows = rows_at(base + offset, SHARE)
            weight[layer, rows, 0:low] = piece[turn - 1, :, low * layer : low * (layer + 1)]
            weight[layer, rows, low:] = piece[turn - 1, :, tail : tail + depth - low]


def place_rest(idx, weight, pieces, lines, tail, layers, left, pad):
    blocks = len(pieces)
    depth = weight.shape[2]
    part = pieces[0].shape[1]
    tail[...] = jnp.zeros_like(tail)
    for turn, piece in enumerate(pieces):
        for group in range(-(-depth // part)):
            stop = min(depth, part * (group + 1))
            lines[block_of(idx, turn, blocks), :, part * group : stop] = piece[
                16 * group : 16 * (group + 1), 0 : stop - part * group
            ].astype(F32)
    for block in range(blocks):
        for layer in range(layers):
            tail[0:left, :] = lines[block, left * layer : left * (layer + 1), :]
            at = pad * block + MAIN
            weight[layer, at : at + 16, :] = tail[...].astype(BF16)


def cross_forward(idx, *refs, blocks, layers, width, pad, depth):
    pieces, refs = refs[:blocks], refs[blocks:]
    own, refs = refs[0], refs[1:]
    slices, refs = cross_eight(refs[:4]), refs[4:]
    z_out, x_out, weight, lines, tail, start, state, nat = refs
    left = width - MAIN
    place_rest(idx, weight, pieces, lines, tail, layers, left, pad)
    at = 16 * -(-depth // pieces[0].shape[1])
    bias = [lines[block, :, 0:384].T for block in range(blocks)]
    for turn, piece in enumerate(pieces):
        block = block_of(idx, turn, blocks)
        start[block, 0:width, :] = piece[at : at + width, :].astype(F32)
        start[block, width:, :] = jnp.zeros((pad - width, piece.shape[1]), F32)
    full = nat.shape[0]
    ones = lax.broadcasted_iota(jnp.int32, (full - depth, nat.shape[1]), 0) == 0
    nat[depth:full, :] = ones.astype(F32)
    for block in range(blocks):
        nat[width * block : width * (block + 1), :] = start[block, 0:width, :]
    for layer in range(layers):
        x_out[layer] = nat[...].astype(BF16)
        place_cross(idx, weight, own, slices, blocks, layer, pad)
        at = left * layers + layer
        for block in range(blocks):
            rows = slice(pad * block, pad * (block + 1))
            value = dot(weight[layer, rows, :], x_out[layer, 0:depth, :], NN) + bias[block][0:pad, at : at + 1]
            z_out[layer, rows, :] = value
            before = start[block] if layer == 0 else state[block]
            value = start[block] * value + before
            state[block] = value
            nat[width * block : width * (block + 1), :] = value[0:width, :]
    x_out[layers] = nat[...].astype(BF16)


def tower_both(idx, *refs, blocks, layers, width, depth, fields, examples):
    (labels, day_ids), refs = refs[:2], refs[2:]
    pieces, refs = refs[:blocks], refs[blocks:]
    (own1, own2), refs = refs[:2], refs[2:]
    slices, refs = refs[:8], refs[8:]
    x_all, acts, far, heads, tower, lines_out, day_out, field_out = refs[:8]
    inputs, slope1, act2, headed, vectors = refs[8:]
    hidden = tower.shape[0]
    full = x_all.shape[1]
    size = hidden // blocks
    part = x_all.shape[2]
    low = depth // LANES * LANES
    at = 16 * -(-depth // part) + width
    for turn, piece in enumerate(pieces):
        inputs[block_of(idx, turn, blocks)] = piece[at : at + 3, :].astype(F32)
    base = idx[0] * size
    tower[rows_at(base, size), 0:full] = own1[...]
    tower[rows_at(base, size), full:] = own2[...]
    for turn in range(1, blocks):
        base = block_of(idx, turn, blocks) * size
        for offset, piece in zip(places(idx), slices):
            rows = rows_at(base + offset, SHARE)
            tower[rows, :] = piece[turn - 1, :, piece.shape[2] - tower.shape[1] :]
    parts = [slice(size * block, size * (block + 1)) for block in range(blocks)]
    columns = []
    for block in range(blocks):
        vectors[0:3, :] = inputs[block]
        columns.append(vectors[...].T)
    for rows, column in zip(parts, columns):
        act, slope = gelu_parts(dot(tower[rows, 0:depth], x_all[layers, 0:depth, :], NN) + column[:, 0:1])
        acts[0, rows, :] = act.astype(BF16)
        slope1[rows, :] = slope
    logits = jnp.zeros((1, part), F32)
    for rows, column in zip(parts, columns):
        act, slope = gelu_parts(dot(tower[:, full + rows.start : full + rows.stop], acts[0], TN) + column[:, 2:3])
        act2[rows, :] = act
        headed[rows, :] = column[:, 1:2] * slope
        logits += jnp.sum(act * column[:, 1:2], axis=0, keepdims=True)

    half = BUCKETS // 2
    tally = jnp.zeros((half, LANES), F32)
    for piece in slices:
        at = piece.shape[2] - tower.shape[1] + low
        tally += piece[0 : half // SHARE, :, at : at + LANES].astype(F32).reshape(half, LANES)
    count = jnp.concatenate([tally, pltpu.roll(tally, LANES - 2 * (fields + 1), 1)], axis=0)
    high = count[:, COUNT : COUNT + fields + 1]
    count = 256.0 * high + count[:, COUNT + fields + 1 : COUNT + 2 * (fields + 1)]
    days = count[0:32, fields : fields + 1]
    padded = jnp.concatenate([count, jnp.zeros((BUCKETS, LANES - fields - 1), F32)], axis=1).T
    field_out[...] = padded[0:fields, :].astype(jnp.int32)
    day_out[...] = padded[fields : fields + 1, :].astype(jnp.int32)

    mine = pl.ds(pl.multiple_of(idx[0] * part, LANES), part)
    lab = labels[:, mine].astype(F32)
    table = (lax.broadcasted_iota(jnp.int32, (32, part), 0) == day_ids[:, mine]).astype(F32)
    share = examples / (DAYS * jnp.maximum(days, 1.0))
    weights = jnp.sum(table * share, axis=0, keepdims=True)
    decay = jnp.exp(-jnp.abs(logits))
    loss = jnp.maximum(logits, 0.0) + jnp.log1p(decay) - lab * logits
    sigmoid = jnp.where(logits >= 0.0, 1.0, decay) / (1.0 + decay)
    dl = weights * (sigmoid - lab)
    losses = dot(jnp.broadcast_to(loss, (8, part)), table, NT, lax.Precision.HIGHEST)[0:1, :]
    lines_out[0:1, :] = logits
    lines_out[1:2, :] = jnp.zeros_like(logits)
    lines_out[1:2, 0 : losses.shape[1]] = losses

    acts[1] = (dl * headed[...]).astype(BF16)
    far[0:hidden, :] = acts[1]
    for rows in parts:
        acts[2, rows, :] = (dot(tower[rows, full:], acts[1], NN) * slope1[rows, :]).astype(BF16)
    for block in range(blocks):
        rows = rows_at(block * size + (1 - idx[1]) * HALF, HALF)
        at = hidden + HALF * block
        far[at : at + HALF, :] = acts[0, rows, :]
        at = hidden + HALF * (block + blocks)
        far[at : at + HALF, :] = acts[2, rows, :]
    for rows in parts:
        heads[rows, :] = jnp.broadcast_to(jnp.sum(act2[rows, :] * dl, axis=1, keepdims=True), (size, LANES))


def cross_backward(idx, *refs, blocks, layers, width, pad, depth):
    extra_lines, refs = refs[0], refs[1:]
    pieces, refs = refs[:blocks], refs[blocks:]
    own, refs = refs[0], refs[1:]
    slices, refs = cross_eight(refs[:4]), refs[4:]
    (tower, acts, z_all), refs = refs[:3], refs[3:]
    eg_out, refs = refs[:blocks], refs[blocks:]
    dz_out, rest_out, dz_far_last, dz_far_out = refs[:4]
    weight, inputs, lines, tail, flow, padded, total, rest = refs[4:]
    left = width - MAIN
    place_rest(idx, weight, pieces, lines, tail, layers, left, pad)
    at = 16 * -(-depth // pieces[0].shape[1])
    for turn, piece in enumerate(pieces):
        inputs[block_of(idx, turn, blocks)] = piece[at : at + width, :].astype(F32)
    flow[...] = dot(tower[:, 0:depth], acts[2], TN)
    padded[...] = jnp.zeros_like(padded)
    rest[...] = jnp.zeros_like(rest)
    for layer in reversed(range(layers)):
        for block in range(blocks):
            rows = slice(pad * block, pad * (block + 1))
            dx = flow[width * block : width * (block + 1), :]
            padded[block, 0:width, :] = dx
            dx = padded[block, 0:width, :]
            dz = dx * inputs[block]
            term = dx * z_all[layer, pad * block : pad * block + width, :]
            total[block, 0:width, :] = term if layer == layers - 1 else total[block, 0:width, :] + term
            rest[left * block : left * (block + 1), :] = dz[MAIN:width, :]
            padded[block, 0:width, :] = dz
            dz_out[layer, rows, :] = padded[block].astype(BF16)
        rest_out[layer] = rest[...].astype(BF16)
        far = dz_far_last.at[0] if layer == layers - 1 else dz_far_out.at[layer]
        far[HALF * blocks :, :] = rest[...].astype(BF16)
        for block in range(blocks):
            rows = rows_at(pad * block + (1 - idx[1]) * HALF, HALF)
            far[HALF * block : HALF * (block + 1), :] = dz_out[layer, rows, :]
        place_cross(idx, weight, own, slices, blocks, layer, pad)
        flow[...] += dot(weight[layer], dz_out[layer], TN)
    extras = split3(extra_lines[0:1, :]) + split3(extra_lines[1:2, :])
    for block in range(blocks):
        total[block, 0:width, :] += flow[width * block : width * (block + 1), :]
        total[block, width:, :] = jnp.zeros((pad - width, flow.shape[1]), F32)
        for at, extra in enumerate(extras):
            total[block, width + at : width + at + 1, :] = extra
    for turn in range(blocks):
        eg_out[turn][...] = total[block_ahead(idx, turn, blocks)].astype(BF16)


def tower_grads(idx, x_all, x_far, acts, far, head, *refs, blocks, depth, layers, wheres):
    outs = refs[: 1 + (0 in wheres)]
    x_cat, acts_in, far_in, heads, lhs, d_cat = refs[len(outs) : len(outs) + 6]
    holds, sems = refs[len(outs) + 6 : -1], refs[-1]
    hidden = acts.shape[1]
    size = hidden // blocks
    part = acts.shape[2]
    low = depth // LANES * LANES
    bias = depth - low
    copies = Copies(sems)
    first = [
        copies.start(acts, acts_in),
        copies.start(far, far_in),
        copies.start(x_all.at[layers], x_cat.at[:, 0:part]),
        copies.start(x_far.at[layers], x_cat.at[:, part : 2 * part]),
        copies.start(head, heads),
    ]
    wait(*first)
    lane = lane_of((SHARE, LANES))
    pick = (lax.broadcasted_iota(jnp.int32, (LANES, 2 * part), 0) == bias + 1).astype(BF16)
    order = [(where, slot) for where in wheres for slot in range(blocks)]
    shares = relative(idx)
    d_cat[:, 0:part] = acts_in[1]
    d_cat[:, part:] = far_in[0:hidden, :]
    scale = []
    for at, (where, slot) in enumerate(order):
        block = block_ahead(idx, slot, blocks)
        rows = rows_at(block * size + idx[1] * HALF + SHARE * shares[where], SHARE)
        other = rows_at(block * size + (1 - idx[1]) * HALF + SHARE * shares[where], SHARE)
        lines = rows_at(hidden + HALF * block + SHARE * shares[where], SHARE)
        after_it = rows_at(hidden + HALF * (block + blocks) + SHARE * shares[where], SHARE)
        here = slice(SHARE * at, SHARE * (at + 1))
        lhs[0, here, 0:part] = acts_in[2, rows, :]
        lhs[0, here, part:] = far_in[after_it, :]
        lhs[1, here, 0:part] = acts_in[0, rows, :]
        lhs[1, here, part:] = far_in[lines, :]
        lhs[2, here, 0:part] = acts_in[1, rows, :]
        lhs[2, here, part:] = far_in[rows, :]
        scale.append(
            jnp.where(lane == bias + 2, heads[rows, :], 0.0) + jnp.where(lane == bias + 3, heads[other, :], 0.0)
        )
    extra = dot(lhs[2], pick, NT)
    wide = dot(lhs[0], x_cat[...], NT)
    deep = dot(lhs[1], d_cat[...], NT)
    for at, (where, slot) in enumerate(order):
        target = (holds[where] if 0 in wheres else holds[0].at[where - 2]).at[slot]
        here = slice(SHARE * at, SHARE * (at + 1))
        target[:, 0:low] = wide[here, 0:low].astype(BF16)
        target[:, low : low + LANES] = (wide[here, low:] + extra[here, :] + scale[at]).astype(BF16)
        target[:, low + LANES :] = deep[here, :].astype(BF16)
    wait(*[copies.start(hold, out) for hold, out in zip(holds, outs)])


def cross_grads(idx, x_all, x_far, dz, rest, dz_far, near_out, far_out, send_out, *refs, blocks, base, pad, depth):
    x_cat, dz_in, far_in, rest_in, lhs, few, extra, tiles, near, away, send, sems = refs
    part = dz.shape[2]
    low = depth // LANES * LANES
    groups = -(-depth // MAIN)
    count = dz_far.shape[0]
    left = rest_in.shape[1] // blocks
    copies = Copies(sems)
    first = []
    for layer in reversed(range(count)):
        first.append(
            [
                copies.start(dz.at[base + layer], dz_in.at[layer]),
                copies.start(dz_far.at[layer], far_in.at[layer]),
                copies.start(rest.at[base + layer], rest_in.at[layer]),
                copies.start(x_all.at[base + layer], x_cat.at[layer, :, 0:part]),
                copies.start(x_far.at[base + layer], x_cat.at[layer, :, part : 2 * part]),
            ]
        )
    few[...] = jnp.zeros_like(few)
    order = [(where, slot) for where in range(4) for slot in range(blocks)]
    shares = relative(idx)
    lane = lane_of((HALF, LANES))
    bias = depth - low
    span = left * groups
    for layer, started in zip(reversed(range(count)), first):
        wait(*started)
        value = jnp.zeros((HALF, LANES), F32)
        near_rest = rest_in[layer].astype(F32)
        far_rest = far_in[layer, HALF * blocks :, :].astype(F32)
        for group in range(groups):
            for block in range(blocks):
                lines = slice(span * block + left * group, span * block + left * (group + 1))
                few[group, lines, 0:part] = near_rest[left * block : left * (block + 1), :]
                few[group, lines, part:] = far_rest[left * block : left * (block + 1), :]
            if MAIN * (group + 1) <= depth:
                rows = rows_at(MAIN * group + idx[1] * HALF, HALF)
            else:
                rows = slice(MAIN * group, MAIN * group + HALF)
            value += dot(x_cat[layer, rows, :], few[group].astype(BF16), NT)
        inside = (lane > bias) & (lane <= bias + span)
        for block in range(blocks):
            extra[block] = jnp.where(inside, pltpu.roll(value, (bias + 1 - span * block) % LANES, 1), 0.0)
        for at, (where, slot) in enumerate(order):
            block = block_ahead(idx, slot, blocks)
            rows = rows_at(pad * block + idx[1] * HALF + SHARE * shares[where], SHARE)
            lines = rows_at(HALF * block + SHARE * shares[where], SHARE)
            here = slice(SHARE * at, SHARE * (at + 1))
            lhs[here, 0:part] = dz_in[layer, rows, :]
            lhs[here, part:] = far_in[layer, lines, :]
        grad = dot(lhs[...], x_cat[layer], NT)
        for at, (where, slot) in enumerate(order):
            target = (near, away, send.at[0], send.at[1])[where].at[slot]
            here = slice(SHARE * at, SHARE * (at + 1))
            target[:, low * layer : low * (layer + 1)] = grad[here, 0:low].astype(BF16)
            tile = grad[here, low:] + extra[block_ahead(idx, slot, blocks), rows_at(SHARE * shares[where], SHARE), :]
            if layer < count - 1:
                tile = tiles[here, :] + (pltpu.roll(tile, APART * layer, 1) if layer else tile)
            elif layer:
                tile = pltpu.roll(tile, APART * layer, 1)
            if layer:
                tiles[here, :] = tile
            else:
                target[:, low * count :] = tile.astype(BF16)
    wait(copies.start(send, send_out), copies.start(near, near_out), copies.start(away, far_out))


def eight(mine, one, two, far):
    return [mine, one, two.at[0], two.at[1]] + [far.at[at] for at in range(4)]


def finish_input(idx, *refs, blocks):
    pieces, (out, logits, losses, day_held) = refs[:blocks], refs[blocks:]
    width = out.shape[0]
    size = pieces[0].shape[1]
    for turn, piece in enumerate(pieces):
        block = block_of(idx, turn, blocks)
        lanes = pl.ds(pl.multiple_of(block * size, LANES), size)
        values = piece[...].astype(F32)
        line = lambda at: values[width + at : width + at + 1, :]
        out[:, lanes] = values[0:width, :]
        logits[:, lanes] = line(0) + line(1) + line(2)
        day_held[block] = jnp.broadcast_to(line(3) + line(4) + line(5), day_held.shape[1:])
    days = day_held[0]
    for block in range(1, blocks):
        days += day_held[block]
    row = lax.broadcasted_iota(jnp.int32, losses.shape, 0)
    tile = jnp.zeros(losses.shape, F32)
    for at, value in enumerate(split3(days[0:1, 0:LANES])):
        tile = jnp.where(row == at, value, tile)
    losses[...] = jnp.where(lane_of(tile.shape) < LOSS, 0.0, pltpu.roll(tile, LOSS, 1))


def finish_tower(idx, *refs, depth):
    slices, (counts, out1, out2, rows_out, mean_out, lines, day_held) = eight(*refs[:4]), refs[4:]
    low = depth // LANES * LANES
    size = out2.shape[0]
    for offset, piece in zip(places(idx), slices):
        lines[rows_at(offset, SHARE), :] = piece[:, 0 : low + LANES].astype(F32)
        out2[rows_at(offset, SHARE), :] = piece[:, low + LANES :].astype(F32)
        tile = piece[0:16, low : low + LANES].astype(F32)
        day_held[lax.div(offset, SHARE)] = tile[0:1, :] + tile[1:2, :] + tile[2:3, :]
    turned = lines[...].T
    out1[...] = turned[0:depth, :]
    head = turned[depth + 3 : depth + 4, :]
    rows_out[0:1, :] = turned[depth : depth + 1, :]
    rows_out[1:2, :] = turned[depth + 1 : depth + 2, :]
    rows_out[2:3, 0:HALF] = turned[depth + 2 : depth + 3, 0:HALF] + head[:, HALF:]
    rows_out[2:3, HALF:] = turned[depth + 2 : depth + 3, HALF:] + head[:, 0:HALF]
    days = day_held[0]
    for at in range(1, day_held.shape[0]):
        days += day_held[at]
    days = days[:, LOSS : LOSS + DAYS]
    mean = days / jnp.maximum(counts[:, 0:DAYS].astype(F32), 1.0)
    mean_out[...] = jnp.sum(mean, axis=1, keepdims=True) / DAYS


def finish_cross(idx, *refs, blocks, base, more):
    slices, refs = eight(*refs[:4]), refs[4:]
    before, (out, bias_out, held, lines, sems) = refs[:more], refs[more:]
    count, width, depth = held.shape
    left = width - MAIN
    low = depth // LANES * LANES
    copies = Copies(sems)
    last = []
    if more:
        bias_out[count:, :] = before[1][...]
    for offset, piece in zip(places(idx), slices):
        lines[rows_at(offset, SHARE), :] = piece[:, low * count :].astype(F32)
    turned = lines[...].T
    for layer in range(count):
        for offset, piece in zip(places(idx), slices):
            rows = rows_at(offset, SHARE)
            held[layer, rows, 0:low] = piece[:, low * layer : low * (layer + 1)].astype(F32)
        held[layer, 0:MAIN, low:] = lines[:, APART * layer : APART * layer + depth - low]
        bias = APART * layer + depth - low
        bias_out[layer : layer + 1, 0:MAIN] = turned[bias : bias + 1, :]
        for group in range(-(-depth // MAIN)):
            rest = turned[bias + 1 + left * group : bias + 1 + left * (group + 1), :]
            stop = min(depth, MAIN * (group + 1)) - MAIN * group
            held[layer, MAIN:width, MAIN * group : MAIN * group + stop] = rest[:, 0:stop]
        last.append(copies.start(held.at[layer], out.at[base + layer]))
        corner = jnp.broadcast_to(rest[:, stop : stop + 1], (left, LANES))
        ahead = lax.broadcasted_iota(jnp.int32, (left, LANES), 0) == lane_of((left, LANES))
        line = jnp.sum(jnp.where(ahead, corner, 0.0), axis=0, keepdims=True)
        bias_out[layer : layer + 1, MAIN:width] = line[:, 0:left]
    wait(*last)


def per_device(
    embedded,
    feature_ids,
    day_ids,
    labels,
    cross_weight,
    cross_bias,
    tower1,
    tower1_bias,
    tower2,
    tower2_bias,
    head_weight,
):
    blocks = lax.axis_size("mp")
    groups = lax.axis_size("dp")
    tokens, width = embedded.shape
    layers, _, depth = cross_weight.shape
    size, hidden = tower2.shape
    pad = -(-width // 16) * 16
    full = -(-(depth + 3) // LANES) * LANES
    part = tokens // blocks
    examples = tokens * groups
    flat = blocks * pad
    shape = jax.ShapeDtypeStruct
    vmem = pltpu.VMEM

    me = lax.axis_index("mp")
    group = lax.axis_index("dp")
    core, plane = group & 1, (group >> 1) & 3
    idx = jnp.stack([me, core, plane, group & 7]).astype(jnp.int32)
    swap = lambda bits: [(i, i ^ bits(i)) for i in range(groups)]
    first = swap(lambda i: 4 if i & 1 else 2)
    second = swap(lambda i: 2 if i & 1 else 4)
    pair = swap(lambda i: 1)
    others = [swap(lambda i, b=b: 1 << b) for b in range(3, groups.bit_length() - 1)]
    turn_by = lambda r: [(i, (i + r) % blocks) for i in range(blocks)]
    hop = lambda value, perm: lax.ppermute(value, "dp", perm)
    turns = lambda values: [
        lax.ppermute(value, "mp", turn_by(r + 1)) for r, value in enumerate(values)
    ]

    own_row = core * HALF + plane * SHARE
    cross_send = lax.dynamic_slice(cross_weight, (0, own_row, 0), (layers, SHARE, depth))
    low = depth // LANES * LANES
    fill = jnp.zeros((SHARE, LANES - layers * (depth - low)), BF16)
    cross_send = jnp.concatenate([rows[:, :low] for rows in cross_send] + [rows[:, low:] for rows in cross_send] + [fill], axis=1)
    cross_turned = turns([cross_send] * (blocks - 1))
    vectors = jnp.stack([tower1_bias, head_weight, tower2_bias])
    wide = full + hidden
    groups_of = -(-depth // part)
    tower_send, tower_own, tally, *chunks = call(
        functools.partial(pack_rest, blocks=blocks),
        tuple(
            [
                shape((SHARE, wide), BF16),
                shape((size, full), BF16),
                shape(((blocks - 1) * SHARE, LANES), BF16),
            ]
            + [shape((16 * groups_of + width + 3, part), BF16)] * blocks
        ),
        [vmem((16, groups_of * part), F32)],
        [
            after(idx, cross_send),
            cross_weight,
            cross_bias,
            embedded.T,
            vectors,
            tower1,
            tower2,
            feature_ids.T,
            day_ids[None, :],
        ],
        mib=24,
        nbytes=2 << 20,
    )
    for perm in others:
        tally = tally + hop(tally, perm)
    tally = jnp.pad(tally.reshape(blocks - 1, SHARE, LANES), ((0, 0), (0, 0), (full - LANES, hidden)))

    join = lambda *values: lax.optimization_barrier(values)
    cross_mine = jnp.stack(cross_turned)
    cross_mine, tower_send, *chunks = join(cross_mine, tower_send, *chunks)
    cross_one, cross_two = hop(cross_mine, first), hop(cross_mine, second)
    tower_turned = turns([tower_send] * (blocks - 1))
    cross_one, cross_two, *tower_turned = join(cross_one, cross_two, *tower_turned)

    turn = lambda value, r: lax.ppermute(value, "mp", turn_by(r))
    pieces = [chunks[0]] + [turn(after(chunks[r], tower_turned[0]), r) for r in range(1, blocks - 1)]
    tower_mine = jnp.stack(tower_turned) + tally
    both = jnp.concatenate([cross_one, tower_mine], axis=2)
    tower_one, both = hop(tower_mine, first), hop(both, second)
    cross_near = jnp.stack([cross_mine, cross_one, cross_two])
    cross_far = hop(cross_near, pair)
    pieces.append(turn(after(chunks[-1], cross_far), blocks - 1))
    both, tower_one, cross_far, *pieces = join(both, tower_one, cross_far, *pieces)

    tower_three = hop(tower_one, second)
    both_far, tower_far, tower_next = hop(both, pair), hop(tower_mine, pair), hop(tower_one, pair)
    both_far, tower_far, tower_next = join(both_far, tower_far, tower_next)
    cross_slices = [cross_near, both, cross_far, both_far]

    z_all, x_all = call(
        functools.partial(cross_forward, blocks=blocks, layers=layers, width=width, pad=pad, depth=depth),
        (shape((layers, flat, part), F32), shape((layers + 1, full, part), BF16)),
        [
            vmem((layers, flat, depth), BF16),
            vmem((blocks, 16, depth), F32),
            vmem((16, depth), F32),
            vmem((blocks, pad, part), F32),
            vmem((blocks, pad, part), F32),
            vmem((full, part), F32),
        ],
        [idx, *pieces, cross_weight, *cross_slices],
        mib=28,
        flops=2 * layers * flat * full * part,
        nbytes=20 << 20,
    )
    tower_last = hop(after(tower_three, z_all), pair)
    tower_slices = [tower_mine, tower_one, both, tower_three, tower_far, tower_next, both_far, tower_last]
    x_far = hop(after(x_all, tower_last), pair)
    fields = feature_ids.shape[1]
    acts, far, head_col, tower_all, lines, day_line, field_counts = call(
        functools.partial(
            tower_both, blocks=blocks, layers=layers, width=width, depth=depth, fields=fields, examples=examples
        ),
        (
            shape((3, hidden, part), BF16),
            shape((2 * hidden, part), BF16),
            shape((hidden, LANES), F32),
            shape((hidden, wide), BF16),
            shape((2, part), F32),
            shape((1, BUCKETS), jnp.int32),
            shape((fields, BUCKETS), jnp.int32),
        ),
        [
            vmem((blocks, 3, part), F32),
            vmem((hidden, part), F32),
            vmem((hidden, part), F32),
            vmem((hidden, part), F32),
            vmem((8, part), F32),
        ],
        [
            idx,
            labels[None, :],
            day_ids[None, :],
            *pieces,
            tower_own,
            tower2,
            *tower_slices,
            x_all,
        ],
        mib=28,
        flops=8 * hidden * full * part,
        nbytes=10 << 20,
    )
    far = hop(far, pair)

    def grads(kernel, keep, scratch, args, copies, flops):
        outs = keep, keep, (2,) + keep
        return call(
            kernel,
            tuple(shape(s, BF16) for s in outs),
            scratch + [vmem(s, BF16) for s in outs],
            args,
            mib=20,
            spec=HBM,
            copies=copies,
            flops=flops,
            nbytes=10 << 20,
        )

    def tower_parts_of(wheres, outs, start):
        return call(
            functools.partial(tower_grads, blocks=blocks, depth=depth, layers=layers, wheres=wheres),
            tuple(shape(s, BF16) for s in outs),
            [
                vmem((full, 2 * part), BF16),
                vmem((3, hidden, part), BF16),
                vmem((2 * hidden, part), BF16),
                vmem((hidden, LANES), F32),
                vmem((3, HALF * blocks // 2, 2 * part), BF16),
                vmem((hidden, 2 * part), BF16),
            ]
            + [vmem(s, BF16) for s in outs],
            [start, x_all, x_far, acts, far, head_col],
            mib=20,
            spec=HBM,
            copies=7,
            flops=2 * hidden * full * part,
            nbytes=10 << 20,
        )

    keep = (blocks, SHARE, wide)
    (tower_out,) = tower_parts_of((2, 3), [(2,) + keep], idx)
    tower_arrived = hop(tower_out, first)
    *input_grads, dz, dz_rest, last_far, dz_far = call(
        functools.partial(cross_backward, blocks=blocks, layers=layers, width=width, pad=pad, depth=depth),
        tuple([shape((pad, part), BF16)] * blocks)
        + (
            shape((layers, flat, part), BF16),
            shape((layers, 16, part), BF16),
            shape((1, HALF * blocks + 16, part), BF16),
            shape((layers - 1, HALF * blocks + 16, part), BF16),
        ),
        [
            vmem((layers, flat, depth), BF16),
            vmem((blocks, width, part), F32),
            vmem((blocks, 16, depth), F32),
            vmem((16, depth), F32),
            vmem((depth, part), F32),
            vmem((blocks, pad, part), F32),
            vmem((blocks, pad, part), F32),
            vmem((16, part), F32),
        ],
        [
            after(idx, tower_out),
            lines,
            *pieces,
            cross_weight,
            *cross_slices,
            tower_all,
            acts,
            z_all,
        ],
        mib=22,
        flops=2 * layers * flat * full * part,
        nbytes=20 << 20,
    )
    last_far = hop(last_far, pair)
    dz_far = hop(dz_far, pair)

    def cross_parts_of(base, count, far, start):
        return grads(
            functools.partial(cross_grads, blocks=blocks, base=base, pad=pad, depth=depth),
            (blocks, SHARE, count * low + LANES),
            [
                vmem((count, full, 2 * part), BF16),
                vmem((count, flat, part), BF16),
                vmem((count, HALF * blocks + 16, part), BF16),
                vmem((count, 16, part), BF16),
                vmem((HALF * blocks, 2 * part), BF16),
                vmem((-(-depth // MAIN), LANES, 2 * part), F32),
                vmem((blocks, HALF, LANES), F32),
                vmem((HALF * blocks, LANES), F32),
            ],
            [start, x_all, x_far, dz, dz_rest, far],
            5 * count + 3,
            2 * count * flat * full * part,
        )

    last_parts = cross_parts_of(layers - 1, 1, last_far, idx)
    tower_parts = [*tower_parts_of((0, 1), [keep, keep], after(idx, last_parts[2])), tower_out]
    grad_pieces = [input_grads[0]] + turns(input_grads[1:])
    cross_parts = cross_parts_of(0, layers - 1, dz_far, after(idx, last_parts[2], grad_pieces[1]))

    down = lambda value: value.astype(BF16)
    up = lambda value: value.astype(F32)

    def near_sum(parts, arrived, last):
        return up(parts[0]) + up(arrived[0]) + up(last)

    def far_send(parts, arrived):
        return hop(down(up(parts[1]) + up(arrived[1])), second)

    def send_blocks(held):
        return turns([down(held[r]) for r in range(1, blocks)])

    def total_of(held, turned):
        held = held[0] + sum(up(value) for value in turned)
        for perm in others:
            held = held + hop(held, perm)
        return held

    def two_of(mine, one):
        return hop(jnp.stack([mine, one]), second)

    def far_of(mine, one, two):
        return hop(jnp.concatenate([jnp.stack([mine, one]), two]), pair)

    tower_arrived, last_send = join(tower_arrived, last_parts[2])
    tower_second = far_send(tower_parts, tower_arrived)
    last_arrived = hop(last_send, first)
    *grad_pieces, tower_second, last_arrived, cross_send = join(
        *grad_pieces, tower_second, last_arrived, cross_parts[2]
    )

    tower_held = near_sum(tower_parts, tower_arrived, tower_second)
    tower_turned = send_blocks(tower_held)
    last_second = far_send(last_parts, last_arrived)
    cross_arrived = hop(cross_send, first)
    input_out, logits_all, losses = call(
        functools.partial(finish_input, blocks=blocks),
        (shape((width, tokens), F32), shape((1, tokens), F32), shape((SHARE, LANES), F32)),
        [vmem((blocks, 8, part), F32)],
        [idx, *grad_pieces],
        mib=16,
        nbytes=2 << 20,
    )
    last_held = near_sum(last_parts, last_arrived, last_second)
    last_turned = send_blocks(last_held)
    cross_arrived, losses, last_turned[0], *tower_turned = join(
        cross_arrived, losses, last_turned[0], *tower_turned
    )

    last_turned[1:] = [after(value, last_turned[0]) for value in last_turned[1:]]
    cross_second = far_send(cross_parts, cross_arrived)
    tower_mine = down(total_of(tower_held, tower_turned) + jnp.pad(losses, ((0, 0), (full - LANES, hidden))))
    tower_one = hop(tower_mine, first)
    cross_second, tower_one, *last_turned = join(cross_second, tower_one, *last_turned)

    cross_held = near_sum(cross_parts, cross_arrived, cross_second)
    cross_turned = send_blocks(cross_held)
    tower_two = two_of(tower_mine, tower_one)
    last_mine = down(total_of(last_held, last_turned))
    last_one = hop(last_mine, first)
    tower_two, last_one, *cross_turned = join(tower_two, last_one, *cross_turned)

    cross_mine = down(total_of(cross_held, cross_turned))
    cross_one = hop(cross_mine, first)
    last_two = two_of(last_mine, last_one)
    tower_far = far_of(tower_mine, tower_one, tower_two)
    cross_one, last_two, tower_far = join(cross_one, last_two, tower_far)

    cross_two = two_of(cross_mine, cross_one)
    last_far = far_of(last_mine, last_one, last_two)
    tower_sums = [tower_mine, tower_one, tower_two, tower_far]
    last_sums = [last_mine, last_one, last_two, last_far]
    tower1_grad, tower2_grad, rows, mean = call(
        functools.partial(finish_tower, depth=depth),
        (shape((depth, size), F32), shape((size, hidden), F32), shape((3, size), F32), shape((1, 1), F32)),
        [vmem((size, full), F32), vmem((8, 1, LANES), F32)],
        [idx, *tower_sums, day_line],
        mib=16,
        nbytes=4 << 20,
    )
    def finish(sums, base, count, before):
        alias = {5: 0} if before else {}
        return call(
            functools.partial(finish_cross, blocks=blocks, base=base, more=len(before)),
            (shape((layers, width, depth), F32), shape((count + len(before) // 2, width), F32)),
            [vmem((count, width, depth), F32), vmem((MAIN, LANES), F32)],
            [idx, *sums] + [(value, spec) for value, spec in zip(before, (HBM, VMEM))],
            mib=16,
            out_spec=(HBM, VMEM),
            aliases=alias,
            copies=count,
            nbytes=4 << 20,
        )

    before = finish(last_sums, layers - 1, 1, ())
    cross_two, tower1_grad, before = join(cross_two, tower1_grad, before)
    cross_far = far_of(cross_mine, cross_one, cross_two)
    cross_grad, cross_bias_grad = finish([cross_mine, cross_one, cross_two, cross_far], 0, layers - 1, before)
    day_counts = day_line[0, :DAYS]
    return (
        mean[0, 0],
        logits_all[0],
        input_out.T,
        cross_grad,
        cross_bias_grad,
        tower1_grad,
        rows[0],
        tower2_grad,
        rows[1],
        rows[2],
        day_counts,
        field_counts,
    )


def solution(mesh):
    in_specs = (
        P("dp", "mp"),
        P("dp", None),
        P("dp"),
        P("dp"),
        P(None, "mp", None),
        P(None, "mp"),
        P(None, "mp"),
        P("mp"),
        P("mp", None),
        P("mp"),
        P("mp"),
    )
    out_specs = (
        P(),
        P("dp"),
        P("dp", "mp"),
        P(None, "mp", None),
        P(None, "mp"),
        P(None, "mp"),
        P("mp"),
        P("mp", None),
        P("mp"),
        P("mp"),
        P(),
        P(),
    )
    return jax.shard_map(
        per_device, mesh=mesh, in_specs=in_specs, out_specs=out_specs, check_vma=False
    )
```
